32 devices in a mesh: dp: 8 (over y, x, core), tensor: 4 (over z).
Axes of the slice: x: 2, y: 2, z: 4, core: 2. Of those that a mesh axis runs over, the one named last changes fastest.
Arguments:
- tokens: bfloat16 [16, 1024, 2048], P('dp', 'tensor'), may hold values from -6 to 6
- segments: int32 [16, 1024], P('dp'), may hold values from 0 to 3, as said below
- attn_norm: bfloat16 [2048], P('dp'), may hold values from 0.099609375 to 1.8984375
- w_query: bfloat16 [2048, 2048], P('dp', 'tensor'), may hold values from -0.125 to 0.125
- w_key: bfloat16 [2048, 512], P('dp', 'tensor'), may hold values from -0.125 to 0.125
- w_value: bfloat16 [2048, 512], P('dp', 'tensor'), may hold values from -0.125 to 0.125
- w_out: bfloat16 [2048, 2048], P('tensor', 'dp'), may hold values from -1 to 1
- mlp_norm: bfloat16 [2048], P('dp'), may hold values from 0.099609375 to 1.8984375
- w_gate: bfloat16 [2048, 8192], P('dp', 'tensor'), may hold values from -0.125 to 0.125
- w_up: bfloat16 [2048, 8192], P('dp', 'tensor'), may hold values from -0.125 to 0.125
- w_down: bfloat16 [8192, 2048], P('tensor', 'dp'), may hold values from -0.0625 to 0.0625
- cotangent: bfloat16 [16, 1024, 2048], P('dp', 'tensor'), may hold values from -6 to 6
Outputs:
- mixed: bfloat16 [16, 1024, 2048], P('dp', 'tensor')
- grad_tokens: bfloat16 [16, 1024, 2048], P('dp', 'tensor')
- grad_attn_norm: float32 [2048], P(('dp', 'tensor'))
- grad_query: float32 [2048, 2048], P('dp', 'tensor')
- grad_key: float32 [2048, 512], P('dp', 'tensor')
- grad_value: float32 [2048, 512], P('dp', 'tensor')
- grad_out: float32 [2048, 2048], P('tensor', 'dp')
- sensitivity_perceptron_rescale: float32 [2048], P(('dp', 'tensor'))
- grad_gate: float32 [2048, 8192], P('dp', 'tensor')
- grad_up: float32 [2048, 8192], P('dp', 'tensor')
- grad_down: float32 [8192, 2048], P('tensor', 'dp')
The draws below stay inside these ranges and needn't reach their ends.
Inputs may be any that keep to these rules, and one draw needn't show every extreme that they name: `segments`: in each sequence the document numbers start at 0, never fall and end at 3; the first and the last document are never empty, and number 2 may be skipped. Document 1 begins within the first 256 positions and ends within the last 256 positions.
All inputs are finite; a program needn't handle non-finite values.
Results may differ from the reference program's by a relative error of at most 0.02.
Values may be sent and summed in bfloat16 or wider, within the bound.
No kernel may reach another device: no remote copies, remote signals or barrier semaphores. Data moves between devices by JAX's collectives and lax.ppermute only.
A program may use at most 320 MiB of HBM per device.

```python
import jax
import jax.numpy as jnp
from jax import lax

D = 2048
HQ = 32
KV = 8
HD = 64
FF = 8192
L = 1024
SEQS = 16
SHARD_LEN = 256


def draw_segments(key, part):
    key = jax.random.fold_in(key, 7)
    first_key, last_key, cut_key = jax.random.split(key, 3)
    first_end = jax.random.randint(first_key, (SEQS, 1), 1, SHARD_LEN)
    long_end = L - jax.random.randint(last_key, (SEQS, 1), 1, SHARD_LEN)
    fraction = jax.random.randint(cut_key, (SEQS, 1), 0, 1048576)
    cut_point = long_end + fraction * (L - long_end) // 1048576
    positions = jnp.arange(L, dtype=jnp.int32)[None, :]
    numbers = (positions >= first_end).astype(jnp.int32) + (positions >= long_end).astype(jnp.int32) + (positions >= cut_point).astype(jnp.int32)
    return numbers.astype(jnp.int32)


def steps_of(key, shape, shards, low, largest):
    level, own = 1.0, jax.random.fold_in(key, 6)
    for axis_at, shards_of in shards:
        steps = jnp.exp(jax.random.uniform(jax.random.fold_in(own, axis_at), (shards_of,), jnp.float32, low / len(shards), largest / len(shards)))
        level = level * jnp.repeat(steps, shape[axis_at] // shards_of).reshape([-1 if axis == axis_at else 1 for axis in range(len(shape))])
    return level


def scatter_about(stream_key, extent, scale, reach, pieces=(), held_as=jnp.bfloat16):
    array = jax.random.normal(stream_key, extent, jnp.float32) * scale
    if len(pieces) > 0:
        array = steps_of(stream_key, extent, pieces, -0.22, 0.18) * array
    return jnp.clip(array, min=-reach, max=reach).astype(held_as)


def setup_inputs(seed: int = 0) -> dict:
    keys = jax.random.split(jax.random.key(seed), 13)
    tokens = scatter_about(keys[0], (SEQS, L, D), 1.0, 6.0, ((0, 8), (1, 4)))
    segments = draw_segments(jax.random.fold_in(keys[12], 71), 0)
    attn_norm = jnp.clip(1.0 + 0.18 * jax.random.normal(keys[2], (D,), jnp.float32), 0.099609375, 1.8984375).astype(jnp.bfloat16)
    w_query = scatter_about(keys[3], (D, HQ * HD), D ** -0.5, 0.125, ((0, 8), (1, 4)))
    w_key = scatter_about(keys[4], (D, KV * HD), D ** -0.5, 0.125, ((0, 8), (1, 4)))
    w_value = scatter_about(keys[5], (D, KV * HD), D ** -0.5, 0.125, ((0, 8), (1, 4)))
    w_out = scatter_about(keys[6], (HQ * HD, D), (HQ * HD // 64) ** -0.5, 1.0, ((0, 4), (1, 8)))
    mlp_norm = jnp.clip(1.0 + 0.18 * jax.random.normal(keys[7], (D,), jnp.float32), 0.099609375, 1.8984375).astype(jnp.bfloat16)
    w_gate = scatter_about(keys[8], (D, FF), D ** -0.5, 0.125, ((0, 8), (1, 4)))
    w_up = scatter_about(keys[9], (D, FF), D ** -0.5, 0.125, ((0, 8), (1, 4)))
    w_down = scatter_about(keys[10], (FF, D), FF ** -0.5, 0.0625, ((0, 4), (1, 8)))
    cotangent = scatter_about(keys[11], (SEQS, L, D), 1.0, 6.0, ((0, 8), (1, 4)))
    return dict(tokens=tokens, segments=segments, attn_norm=attn_norm, w_query=w_query, w_key=w_key, w_value=w_value, w_out=w_out, mlp_norm=mlp_norm, w_gate=w_gate, w_up=w_up, w_down=w_down, cotangent=cotangent)


EPS = 1e-05
THETA = 500000.0

@jax.custom_vjp
def low(v):
    return lax.optimization_barrier(v.astype(jnp.bfloat16)).astype(jnp.float32)

@jax.custom_vjp
def low_back(v):
    return v

def low_keep(v):
    return (low(v), None)

def low_pass(kept, grad):
    return (grad,)

def back_keep(v):
    return (v, None)

def back_low(kept, grad):
    return (low(grad),)
low.defvjp(low_keep, low_pass)
low_back.defvjp(back_keep, back_low)

def careful_multiply(left, right):
    return jnp.dot(left, right, precision=lax.Precision.HIGHEST, preferred_element_type=jnp.float32)

def rotary_tables(positions, head_size):
    half_size = head_size // 2
    frequency = THETA ** (-2.0 * jnp.arange(half_size, dtype=jnp.float32) / head_size)
    angles = positions.astype(jnp.float32)[:, None] * frequency[None, :]
    cos_table = jnp.cos(angles)
    sine_table = jnp.sin(angles)
    return (jnp.concatenate([cos_table, cos_table], -1), jnp.concatenate([sine_table, sine_table], -1))

def rotate(values, cos_table, sine_table):
    half_size = values.shape[-1] // 2
    turned = jnp.concatenate([-values[..., half_size:], values[..., :half_size]], -1)
    return values * cos_table[:, None, :] + turned * sine_table[:, None, :]

def attend(queries, key_rows, values, seg_ids):
    group_size = HQ // KV
    block_rows = min(512, L)
    block_count = L // block_rows
    key_all = jnp.repeat(key_rows, group_size, axis=1)
    value_all = jnp.repeat(values, group_size, axis=1)
    key_pos = jnp.arange(L, dtype=jnp.int32)

    def block_fn(inputs):
        query_block, query_pos, query_seg = inputs
        scores = low_back(jnp.einsum('qhd,khd->hqk', query_block, key_all, precision=lax.Precision.HIGHEST))
        allowed = (key_pos[None, :] <= query_pos[:, None]) & (seg_ids[None, :] == query_seg[:, None])
        logits = jnp.where(allowed[None], scores * HD ** (-0.5), -1e+30)
        row_max = lax.optimization_barrier(jnp.max(logits, -1, keepdims=True))
        exponent = jnp.exp(logits - row_max)
        weights = low(exponent / lax.optimization_barrier(jnp.sum(exponent, -1, keepdims=True)))
        return jnp.einsum('hqk,khd->qhd', weights, value_all, precision=lax.Precision.HIGHEST)
    result = lax.map(jax.checkpoint(block_fn), (queries.reshape(block_count, block_rows, HQ, HD), key_pos.reshape(block_count, block_rows), seg_ids.reshape(block_count, block_rows)))
    return result.reshape(L, HQ * HD)

def layer_forward(token_vals, seg_ids, attn_norm, w_query, w_key, w_value, w_out, mlp_norm, w_gate, w_up, w_down):
    positions = jnp.arange(L, dtype=jnp.int32)
    cos_table, sine_table = rotary_tables(positions, HD)
    norm_one = lax.rsqrt(lax.optimization_barrier(jnp.mean(token_vals * token_vals, -1, keepdims=True)) + EPS)
    scaled_one = low(token_vals * norm_one)
    first_normalized = low(scaled_one * attn_norm)
    asker_unturned = low_back(careful_multiply(first_normalized, w_query)).reshape(L, HQ, HD)
    key_pre = low_back(careful_multiply(first_normalized, w_key)).reshape(L, KV, HD)
    values = low(low_back(careful_multiply(first_normalized, w_value))).reshape(L, KV, HD)
    queries = low(rotate(asker_unturned, cos_table, sine_table))
    key_rows = low(rotate(key_pre, cos_table, sine_table))
    head_outputs = low(low_back(attend(queries, key_rows, values, seg_ids)))
    residual = token_vals + low_back(careful_multiply(head_outputs, w_out))
    norm_two = lax.rsqrt(lax.optimization_barrier(jnp.mean(residual * residual, -1, keepdims=True)) + EPS)
    scaled_two = low(residual * norm_two)
    latter_rescaled_rows = low(scaled_two * mlp_norm)
    gate = low_back(careful_multiply(latter_rescaled_rows, w_gate))
    upward_projection = low_back(careful_multiply(latter_rescaled_rows, w_up))
    inner_activation = low(jax.nn.silu(gate) * upward_projection)
    return residual + low_back(careful_multiply(inner_activation, w_down))

def reference(tokens, segments, attn_norm, w_query, w_key, w_value, w_out, mlp_norm, w_gate, w_up, w_down, cotangent):
    params = tuple((weight.astype(jnp.float32) for weight in (attn_norm, w_query, w_key, w_value, w_out, mlp_norm, w_gate, w_up, w_down)))

    def seq_step(totals, inputs):
        token_seq, seg_seq, cot_seq = inputs

        def forward_fn(token_vals, *weight_vals):
            return layer_forward(token_vals, seg_seq, *weight_vals)
        output_seq, pullback = jax.vjp(forward_fn, token_seq.astype(jnp.float32), *params)
        gradients = pullback(cot_seq.astype(jnp.float32))
        totals = tuple((total + grad_val for total, grad_val in zip(totals, gradients[1:])))
        return (totals, (output_seq.astype(jnp.bfloat16), gradients[0].astype(jnp.bfloat16)))
    initial = tuple((jnp.zeros(weight.shape, jnp.float32) for weight in params))
    totals, outputs = lax.scan(seq_step, initial, (tokens, segments, cotangent))
    return (outputs[0], outputs[1], totals[0], totals[1], totals[2], totals[3], totals[4], totals[5], totals[6], totals[7], totals[8])
```

```python
import functools

import jax
import jax.numpy as jnp
from jax import lax
from jax.experimental import pallas as pl
from jax.experimental.pallas import tpu as pltpu
from jax.sharding import PartitionSpec as P

HD = 64
EPS = 1e-05
THETA = 500000.0
LOG2E = 1.4426950408889634
LANES = 128
PLANE = 4
f32 = jnp.float32
bf16 = jnp.bfloat16


def call(body, flops, moved, vmem=50, **kw):
    return pl.pallas_call(
        body,
        compiler_params=pltpu.CompilerParams(vmem_limit_bytes=vmem * 2**20),
        cost_estimate=pl.CostEstimate(flops=flops, bytes_accessed=moved, transcendentals=0),
        **kw,
    )


def nn(a, b):
    return jnp.dot(a, b, preferred_element_type=f32)


def nt(a, b):
    return lax.dot_general(a, b, (((1,), (1,)), ((), ())), preferred_element_type=f32)


def tn(a, b):
    return lax.dot_general(a, b, (((0,), (0,)), ((), ())), preferred_element_type=f32)


def swap_halves(x):
    lane = lax.broadcasted_iota(jnp.int32, x.shape, 1)
    return jnp.where(lane % HD < HD // 2, pltpu.roll(x, LANES - HD // 2, 1), pltpu.roll(x, HD // 2, 1))


def gather_keys(k_refs, v_refs, blocks):
    k = jnp.concatenate([k_refs[j][0] for j in range(blocks)], 0)
    v = jnp.concatenate([v_refs[j][0] for j in range(blocks)], 0)
    return k, v


def padded_rows(part, e):
    zero = jnp.zeros_like(part)
    return jnp.concatenate([part, zero] if e == 0 else [zero, part], 0)


def attend_blocks(blocks, group, q_ref, k_refs, v_refs, bias_ref, o_ref, lse_ref, qt_ref, ot_ref):
    span = q_ref.shape[0]
    n = blocks * span
    k, v = gather_keys(k_refs, v_refs, blocks)
    vt = v.T
    qt_ref[...] = q_ref[...].T
    factor = HD**-0.5 * LOG2E

    def step(i, carry):
        for e in range(2):
            head = e * group + i
            rows = pl.ds(pl.multiple_of(head * HD, HD), HD)
            scores = nn(k, padded_rows(qt_ref[rows, :], e))
            logits = scores * factor + bias_ref[0, :n, :]
            top = jnp.max(logits, 0, keepdims=True)
            weights = jnp.exp2(logits - top)
            total = jnp.sum(weights, 0, keepdims=True)
            out = nn(vt[e * HD : (e + 1) * HD], weights.astype(bf16))
            ot_ref[rows, :] = out * (1.0 / total)
            lse_ref[0, 0, pl.ds(head, 1), :] = top + jnp.log2(total)
        return carry

    lax.fori_loop(0, group, step, 0)
    o_ref[...] = ot_ref[...].T.astype(bf16)


def attend_kernel(count, group, place, *refs):
    q_ref, k_refs, v_refs = refs[0], refs[1 : 1 + count], refs[1 + count : 1 + 2 * count]
    rest = refs[1 + 2 * count :]
    for blocks in range(1, count + 1):

        @pl.when(place[0] == blocks - 1)
        def _(blocks=blocks):
            attend_blocks(blocks, group, q_ref, k_refs, v_refs, *rest)


def attend(place, queries, pairs, bias, span, group):
    rows, width = queries.shape
    count = len(pairs)
    seqs = rows // span
    kv_width = pairs[0].shape[2]
    tiles = kv_width // LANES
    wide = width // tiles
    in_specs = [pl.BlockSpec((span, wide), lambda b, p, s: (b, p))]
    for part in range(2):
        in_specs += [pl.BlockSpec((1, span, LANES), lambda b, p, s, part=part: (part, b, p))] * count
    in_specs.append(pl.BlockSpec((1, count * span, span), lambda b, p, s: (b, 0, 0)))
    heads = wide // HD
    spec = pltpu.PrefetchScalarGridSpec(
        num_scalar_prefetch=1,
        grid=(seqs, tiles),
        in_specs=in_specs,
        out_specs=[
            pl.BlockSpec((span, wide), lambda b, p, s: (b, p)),
            pl.BlockSpec((1, 1, heads, span), lambda b, p, s: (b, p, 0, 0)),
        ],
        scratch_shapes=[pltpu.VMEM((wide, span), bf16), pltpu.VMEM((wide, span), f32)],
    )
    return call(
        functools.partial(attend_kernel, count, group),
        flops=rows * width * span * count * 8,
        moved=rows * width * 4,
        grid_spec=spec,
        out_shape=[
            jax.ShapeDtypeStruct((rows, width), bf16),
            jax.ShapeDtypeStruct((seqs, tiles, heads, span), f32),
        ],
    )(place, queries, *pairs, *pairs, bias)


def unattend_blocks(
    blocks, count, group, q_ref, g_ref, k_refs, v_refs, bias_ref, lse_ref, cos_ref, sin_ref,
    dq_ref, dkv_ref, qt_ref, gt_ref, dqt_ref, dk_ref, dv_ref,
):
    span = q_ref.shape[0]
    n = blocks * span
    k, v = gather_keys(k_refs, v_refs, blocks)
    kt = k.T
    qt_ref[...] = q_ref[...].T
    gt_ref[...] = g_ref[...].T
    dk_ref[...] = jnp.zeros_like(dk_ref)
    dv_ref[...] = jnp.zeros_like(dv_ref)
    factor = HD**-0.5 * LOG2E
    lane = lax.broadcasted_iota(jnp.int32, (span, LANES), 1)

    def moved(tile, b, e):
        if b != e:
            tile = pltpu.roll(tile, HD, 1)
        return jnp.where((lane < HD) if e == 0 else (lane >= HD), tile, 0.0).astype(bf16)

    def step(i, carry):
        for e in range(2):
            tile_at = pl.ds(pl.multiple_of((e * (group // 2) + i) * LANES, LANES), LANES)
            q_tile = q_ref[:, tile_at].astype(f32)
            g_tile = g_ref[:, tile_at].astype(f32)
            all_ds, all_p = [], []
            for b in range(2):
                head = e * group + 2 * i + b
                rows = pl.ds(pl.multiple_of(head * HD, HD), HD)
                scores = nn(k, padded_rows(qt_ref[rows, :], e))
                lse = lse_ref[0, 0, pl.ds(head, 1), :]
                probs = jnp.exp2(scores * factor + bias_ref[0, :n, :] - lse)
                dp = nn(v, padded_rows(gt_ref[rows, :], e))
                delta = jnp.sum(probs * dp, 0, keepdims=True)
                ds = (probs * (dp - delta)).astype(bf16)
                dqt_ref[rows, :] = nn(kt[e * HD : (e + 1) * HD], ds)
                all_ds.append(ds)
                all_p.append(probs.astype(bf16))
            q_rows = jnp.concatenate([moved(q_tile, b, e) for b in range(2)], 0)
            g_rows = jnp.concatenate([moved(g_tile, b, e) for b in range(2)], 0)
            dk_ref[:n, :] += nn(jnp.concatenate(all_ds, 1), q_rows)
            dv_ref[:n, :] += nn(jnp.concatenate(all_p, 1), g_rows)
        return carry

    lax.fori_loop(0, group // 2, step, 0)
    scale = HD**-0.5
    dq = dqt_ref[...].T * scale
    for t in range(dq.shape[1] // LANES):
        part = dq[:, t * LANES : (t + 1) * LANES]
        dq_ref[:, t * LANES : (t + 1) * LANES] = (
            part * cos_ref[...] - swap_halves(part) * sin_ref[...]
        ).astype(bf16)
    for j in range(count):
        dkv_ref[j, 0] = (dk_ref[j * span : (j + 1) * span, :] * scale).astype(bf16)
        dkv_ref[j, 1] = dv_ref[j * span : (j + 1) * span, :].astype(bf16)


def unattend_kernel(count, group, place, *refs):
    q_ref, g_ref, k_refs, v_refs = refs[0], refs[1], refs[2 : 2 + count], refs[2 + count : 2 + 2 * count]
    rest = refs[2 + 2 * count :]
    for blocks in range(1, count + 1):

        @pl.when(place[0] == blocks - 1)
        def _(blocks=blocks):
            unattend_blocks(blocks, count, group, q_ref, g_ref, k_refs, v_refs, *rest)


def unattend(place, queries, grads, pairs, bias, lse, cos, sin, span, group):
    rows, width = queries.shape
    count = len(pairs)
    seqs = rows // span
    kv_width = pairs[0].shape[2]
    tiles = kv_width // LANES
    wide = width // tiles
    heads = wide // HD
    tall = pl.BlockSpec((span, wide), lambda b, p, s: (b, p))
    table = pl.BlockSpec((span, LANES), lambda b, p, s: (0, 0))
    in_specs = [tall, tall]
    for part in range(2):
        in_specs += [pl.BlockSpec((1, span, LANES), lambda b, p, s, part=part: (part, b, p))] * count
    in_specs += [
        pl.BlockSpec((1, count * span, span), lambda b, p, s: (b, 0, 0)),
        pl.BlockSpec((1, 1, heads, span), lambda b, p, s: (b, p, 0, 0)),
        table,
        table,
    ]
    spec = pltpu.PrefetchScalarGridSpec(
        num_scalar_prefetch=1,
        grid=(seqs, tiles),
        in_specs=in_specs,
        out_specs=[tall, pl.BlockSpec((count, 2, span, LANES), lambda b, p, s: (0, 0, b, p))],
        scratch_shapes=[
            pltpu.VMEM((wide, span), bf16),
            pltpu.VMEM((wide, span), bf16),
            pltpu.VMEM((wide, span), f32),
            pltpu.VMEM((count * span, LANES), f32),
            pltpu.VMEM((count * span, LANES), f32),
        ],
    )
    return call(
        functools.partial(unattend_kernel, count, group),
        flops=rows * width * span * count * 20,
        moved=rows * width * 8,
        grid_spec=spec,
        out_shape=[
            jax.ShapeDtypeStruct((rows, width), bf16),
            jax.ShapeDtypeStruct((count, 2, rows, kv_width), bf16),
        ],
    )(place, queries, grads, *pairs, *pairs, bias, lse, cos, sin)


def turn(y, cos, sin, out_ref, start=0):
    for t in range(y.shape[1] // LANES):
        part = y[:, t * LANES : (t + 1) * LANES]
        out_ref[:, t * LANES : (t + 1) * LANES] = (part * cos + swap_halves(part) * sin).astype(bf16)


def project_pairs(normed, weights, cos, sin, depth):
    rows, width = normed.shape
    parts, shards, _, cols = weights.shape
    half = cols // 2

    def body(x_ref, w_ref, cos_ref, sin_ref, o_ref):
        w = w_ref[:, 0, :depth, :].reshape(parts * depth, cols)
        y = nn(x_ref[...], w)
        k = y[:, :half]
        o_ref[0] = (k * cos_ref[...] + swap_halves(k) * sin_ref[...]).astype(bf16)
        o_ref[1] = y[:, half:].astype(bf16)

    whole = lambda s: (0, 0)
    return call(
        body,
        flops=2 * rows * width * shards * cols,
        moved=weights.size * 2 + normed.size * 2,
        grid=(shards,),
        in_specs=[
            pl.BlockSpec((rows, width), whole),
            pl.BlockSpec((parts, 1, weights.shape[2], cols), lambda s: (0, s, 0, 0)),
            pl.BlockSpec((rows, LANES), whole),
            pl.BlockSpec((rows, LANES), whole),
        ],
        out_specs=pl.BlockSpec((2, rows, half), lambda s: (0, 0, s)),
        out_shape=jax.ShapeDtypeStruct((2, rows, half * shards), bf16),
    )(normed, weights, cos, sin)


def project_queries(normed, weights, cos, sin):
    rows, width = normed.shape
    parts, shards, depth, cols = weights.shape

    def body(x_ref, w_ref, cos_ref, sin_ref, o_ref):
        y = nn(x_ref[...], w_ref[:, 0].reshape(parts * depth, cols))
        turn(y, cos_ref[...], sin_ref[...], o_ref)

    whole = lambda s: (0, 0)
    return call(
        body,
        flops=2 * rows * width * shards * cols,
        moved=weights.size * 2 + normed.size * 2,
        grid=(shards,),
        in_specs=[
            pl.BlockSpec((rows, width), whole),
            pl.BlockSpec((parts, 1, depth, cols), lambda s: (0, s, 0, 0)),
            pl.BlockSpec((rows, LANES), whole),
            pl.BlockSpec((rows, LANES), whole),
        ],
        out_specs=pl.BlockSpec((rows, cols), lambda s: (0, s)),
        out_shape=jax.ShapeDtypeStruct((rows, cols * shards), bf16),
    )(normed, weights, cos, sin)


def project_out(heads_out, weights, tokens):
    rows, width = heads_out.shape
    parts, shards, depth, cols = weights.shape

    def body(x_ref, w_ref, t_ref, o_ref):
        y = nn(x_ref[...], w_ref[0].reshape(shards * depth, cols))
        o_ref[...] = t_ref[...].astype(f32) + y

    tile = pl.BlockSpec((rows, cols), lambda s: (0, s))
    return call(
        body,
        flops=2 * rows * width * parts * cols,
        moved=weights.size * 2 + rows * width * 8,
        grid=(parts,),
        in_specs=[
            pl.BlockSpec((rows, width), lambda s: (0, 0)),
            pl.BlockSpec((1, shards, depth, cols), lambda s: (s, 0, 0, 0)),
            tile,
        ],
        out_specs=tile,
        out_shape=jax.ShapeDtypeStruct((rows, cols * parts), f32),
    )(heads_out, weights, tokens)


def unproject_out(grads, weights):
    rows, width = grads.shape
    parts, shards, depth, cols = weights.shape

    def body(x_ref, w_ref, o_ref):
        w = jnp.concatenate([w_ref[i, 0] for i in range(parts)], 1)
        o_ref[...] = nt(x_ref[...], w).astype(bf16)

    return call(
        body,
        flops=2 * rows * width * shards * depth,
        moved=weights.size * 2 + rows * width * 4,
        grid=(shards,),
        in_specs=[
            pl.BlockSpec((rows, width), lambda s: (0, 0)),
            pl.BlockSpec((parts, 1, depth, cols), lambda s: (0, s, 0, 0)),
        ],
        out_specs=pl.BlockSpec((rows, depth), lambda s: (0, s)),
        out_shape=jax.ShapeDtypeStruct((rows, depth * shards), bf16),
    )(grads, weights)


def unproject_in(dq, dkv, w_q, w_kv):
    rows, width = dq.shape
    parts, shards, depth, cols = w_q.shape
    thin = w_kv.shape[3] // 2

    def body(q_ref, kv_ref, wq_ref, wkv_ref, o_ref):
        total = jnp.zeros((rows, depth), f32)
        for s in range(shards):
            left = jnp.concatenate(
                [
                    q_ref[:, s * cols : (s + 1) * cols],
                    kv_ref[0, :, s * thin : (s + 1) * thin],
                    kv_ref[1, :, s * thin : (s + 1) * thin],
                ],
                1,
            )
            total += nt(left, jnp.concatenate([wq_ref[0, s], wkv_ref[0, s, :depth, :]], 1))
        o_ref[...] = total

    return call(
        body,
        flops=2 * rows * parts * depth * shards * (cols + 2 * thin),
        moved=(w_q.size + w_kv.size) * 2 + rows * width * 6,
        grid=(parts,),
        in_specs=[
            pl.BlockSpec((rows, width), lambda s: (0, 0)),
            pl.BlockSpec(dkv.shape, lambda s: (0, 0, 0)),
            pl.BlockSpec((1, shards, depth, cols), lambda s: (s, 0, 0, 0)),
            pl.BlockSpec((1, shards, w_kv.shape[2], 2 * thin), lambda s: (s, 0, 0, 0)),
        ],
        out_specs=pl.BlockSpec((rows, depth), lambda s: (0, s)),
        out_shape=jax.ShapeDtypeStruct((rows, parts * depth), f32),
    )(dq, dkv, w_q, w_kv)


def query_weight_grad(normed, dq, parts, shards):
    rows, width = normed.shape
    depth, cols = width // parts, dq.shape[1] // shards

    def body(x_ref, y_ref, o_ref):
        total = tn(x_ref[...], y_ref[...])
        for s in range(shards):
            o_ref[0, s] = total[:, s * cols : (s + 1) * cols].astype(bf16)

    return call(
        body,
        flops=2 * rows * width * dq.shape[1],
        moved=rows * width * 4 + width * dq.shape[1] * 2,
        grid=(parts,),
        in_specs=[
            pl.BlockSpec((rows, depth), lambda s: (0, s)),
            pl.BlockSpec(dq.shape, lambda s: (0, 0)),
        ],
        out_specs=pl.BlockSpec((1, shards, depth, cols), lambda s: (s, 0, 0, 0)),
        out_shape=jax.ShapeDtypeStruct((parts, shards, depth, cols), bf16),
    )(normed, dq)


def pair_weight_grad(normed, dkv, gains, parts, shards):
    rows, width = normed.shape
    depth, thin = width // parts, dkv.shape[2] // shards
    extra = gains.shape[1]

    def body(x_ref, y_ref, g_ref, o_ref):
        dk, dv = tn(x_ref[...], y_ref[0]), tn(x_ref[...], y_ref[1])
        for s in range(shards):
            o_ref[0, s, :depth, :thin] = dk[:, s * thin : (s + 1) * thin].astype(bf16)
            o_ref[0, s, :depth, thin:] = dv[:, s * thin : (s + 1) * thin].astype(bf16)
            o_ref[0, s, depth:, :] = g_ref[0].astype(bf16)

    return call(
        body,
        flops=4 * rows * width * dkv.shape[2],
        moved=rows * width * 4 + width * dkv.shape[2] * 4,
        grid=(parts,),
        in_specs=[
            pl.BlockSpec((rows, depth), lambda s: (0, s)),
            pl.BlockSpec(dkv.shape, lambda s: (0, 0, 0)),
            pl.BlockSpec((1, extra, depth), lambda s: (s, 0, 0)),
        ],
        out_specs=pl.BlockSpec((1, shards, depth + extra, 2 * thin), lambda s: (s, 0, 0, 0)),
        out_shape=jax.ShapeDtypeStruct((parts, shards, depth + extra, 2 * thin), bf16),
    )(normed, dkv, gains)


def out_weight_grad(heads_out, grads, parts, shards):
    rows, width = grads.shape
    cols, depth = width // parts, heads_out.shape[1] // shards

    def body(x_ref, y_ref, o_ref):
        total = tn(x_ref[...], y_ref[...])
        for i in range(parts):
            o_ref[i, 0] = total[:, i * cols : (i + 1) * cols].astype(bf16)

    return call(
        body,
        flops=2 * rows * width * heads_out.shape[1],
        moved=rows * width * 4 + width * heads_out.shape[1] * 2,
        grid=(shards,),
        in_specs=[
            pl.BlockSpec((rows, depth), lambda s: (0, s)),
            pl.BlockSpec((rows, width), lambda s: (0, 0)),
        ],
        out_specs=pl.BlockSpec((parts, 1, depth, cols), lambda s: (0, s, 0, 0)),
        out_shape=jax.ShapeDtypeStruct((parts, shards, depth, cols), bf16),
    )(heads_out, grads)


def finish_pairs(own, come, cos, sin):
    _, rows, width = own.shape

    def body(a_ref, b_ref, cos_ref, sin_ref, o_ref):
        total = a_ref[...].astype(f32) + b_ref[...].astype(f32)
        k = total[0]
        o_ref[0] = (k * cos_ref[...] - swap_halves(k) * sin_ref[...]).astype(bf16)
        o_ref[1] = total[1].astype(bf16)

    tile = pl.BlockSpec((2, rows, LANES), lambda s: (0, 0, s))
    table = pl.BlockSpec((rows, LANES), lambda s: (0, 0))
    return call(
        body,
        flops=own.size * 6,
        moved=own.size * 6,
        grid=(width // LANES,),
        in_specs=[tile, tile, table, table],
        out_specs=tile,
        out_shape=jax.ShapeDtypeStruct(own.shape, bf16),
    )(own, come, cos, sin)


def gate_up(x, w_gate, w_up):
    rows, width = x.shape
    shards, _, cols = w_gate.shape
    tall = min(512, rows)

    def body(x_ref, g_ref, u_ref, go_ref, uo_ref, i_ref):
        left = x_ref[...]
        gate, up = nn(left, g_ref[0]), nn(left, u_ref[0])
        go_ref[...] = gate.astype(bf16)
        uo_ref[...] = up.astype(bf16)
        i_ref[...] = (gate / (1.0 + jnp.exp(-gate)) * up).astype(bf16)

    weight = pl.BlockSpec((1, width, cols), lambda s, m: (s, 0, 0))
    tile = pl.BlockSpec((tall, cols), lambda s, m: (m, s))
    shape = jax.ShapeDtypeStruct((rows, shards * cols), bf16)
    return call(
        body,
        flops=4 * rows * width * shards * cols,
        moved=w_gate.size * 4 + rows * width * 10,
        grid=(shards, rows // tall),
        in_specs=[pl.BlockSpec((tall, width), lambda s, m: (m, 0)), weight, weight],
        out_specs=[tile] * 3,
        out_shape=[shape] * 3,
    )(x, w_gate, w_up)


def inner_grads(g, w_down, gate, up):
    rows, width = g.shape
    shards, cols, _ = w_down.shape
    tall = min(512, rows)

    def body(x_ref, w_ref, g_ref, u_ref, dg_ref, du_ref):
        grad = nt(x_ref[...], w_ref[0])
        gate, up = g_ref[...].astype(f32), u_ref[...].astype(f32)
        s = 1.0 / (1.0 + jnp.exp(-gate))
        dg_ref[...] = (grad * up * s * (1.0 + gate * (1.0 - s))).astype(bf16)
        du_ref[...] = (grad * gate * s).astype(bf16)

    tile = pl.BlockSpec((tall, cols), lambda s, m: (m, s))
    shape = jax.ShapeDtypeStruct((rows, shards * cols), bf16)
    return call(
        body,
        flops=2 * rows * width * shards * cols,
        moved=w_down.size * 2 + rows * width * 10,
        grid=(shards, rows // tall),
        in_specs=[
            pl.BlockSpec((tall, width), lambda s, m: (m, 0)),
            pl.BlockSpec((1, cols, width), lambda s, m: (s, 0, 0)),
            tile,
            tile,
        ],
        out_specs=[tile] * 2,
        out_shape=[shape] * 2,
    )(g, w_down, gate, up)


def down(inner, w_down):
    rows, width = inner.shape
    cols = w_down.shape[2]
    wide = 512
    tall = min(512, rows)

    def body(x_ref, w_ref, o_ref):
        o_ref[...] = nn(x_ref[...], w_ref[...]).astype(bf16)

    return call(
        body,
        flops=2 * rows * width * cols,
        moved=w_down.size * 2 + rows * width * 4,
        grid=(cols // wide, rows // tall),
        in_specs=[
            pl.BlockSpec((tall, width), lambda n, m: (m, 0)),
            pl.BlockSpec((width, wide), lambda n, m: (0, n)),
        ],
        out_specs=pl.BlockSpec((tall, wide), lambda n, m: (m, n)),
        out_shape=jax.ShapeDtypeStruct((rows, cols), bf16),
    )(inner, w_down.reshape(width, cols))


def normed_grads(d_gate, d_up, w_gate, w_up):
    rows, width = d_gate.shape
    shards, depth, cols = w_gate.shape
    wide = 512
    tall = min(512, rows)

    def body(g_ref, u_ref, wg_ref, wu_ref, o_ref):
        total = jnp.zeros((tall, wide), f32)
        for d_ref, w_ref in ((g_ref, wg_ref), (u_ref, wu_ref)):
            total += nt(d_ref[...], jnp.concatenate([w_ref[s] for s in range(shards)], 1))
        o_ref[...] = total.astype(bf16)

    weight = pl.BlockSpec((shards, wide, cols), lambda n, m: (0, n, 0))
    left = pl.BlockSpec((tall, width), lambda n, m: (m, 0))
    return call(
        body,
        flops=4 * rows * width * depth,
        moved=w_gate.size * 4 + rows * width * 6,
        grid=(depth // wide, rows // tall),
        in_specs=[left, left, weight, weight],
        out_specs=pl.BlockSpec((tall, wide), lambda n, m: (m, n)),
        out_shape=jax.ShapeDtypeStruct((rows, depth), bf16),
    )(d_gate, d_up, w_gate, w_up)


def column_weight_grad(xs, ys, shards):
    rows, width = xs[0].shape
    cols = ys[0].shape[1] // shards
    depth = width // PLANE // 2
    count = len(xs)

    def body(*refs):
        x_refs, y_refs, o_ref, xt_ref = refs[:count], refs[count : 2 * count], refs[2 * count], refs[-1]

        @pl.when(pl.program_id(1) == 0)
        def _():
            for j in range(count):
                xt_ref[:, j * rows : (j + 1) * rows] = x_refs[j][...].T

        y = jnp.concatenate([r[...] for r in y_refs], 0)
        for core in range(2):
            o_ref[core, 0, 0] = nn(xt_ref[core * depth : (core + 1) * depth, :], y).astype(bf16)

    return call(
        body,
        flops=2 * count * rows * width * shards * cols,
        moved=count * rows * width * 6 + width * shards * cols * 2,
        grid=(PLANE, shards),
        in_specs=[pl.BlockSpec((rows, 2 * depth), lambda q, s: (0, q))] * count
        + [pl.BlockSpec((rows, cols), lambda q, s: (0, s))] * count,
        out_specs=pl.BlockSpec((2, 1, 1, depth, cols), lambda q, s: (0, s, q, 0, 0)),
        out_shape=jax.ShapeDtypeStruct((2, shards, PLANE, depth, cols), bf16),
        scratch_shapes=[pltpu.VMEM((2 * depth, count * rows), bf16)],
    )(*xs, *ys)


def row_weight_grad(xs, ys, shards):
    rows, width = ys[0].shape
    tall = xs[0].shape[1] // shards
    depth = width // PLANE // 2
    count = len(xs)

    def body(*refs):
        x_refs, y_refs, o_ref, xt_ref = refs[:count], refs[count : 2 * count], refs[2 * count], refs[-1]

        @pl.when(pl.program_id(1) == 0)
        def _():
            for j in range(count):
                xt_ref[:, j * rows : (j + 1) * rows] = x_refs[j][...].T

        total = nn(xt_ref[...], jnp.concatenate([r[...] for r in y_refs], 0)).astype(bf16)
        for core in range(2):
            o_ref[core, 0] = total[:, core * depth : (core + 1) * depth]

    return call(
        body,
        flops=2 * count * rows * width * shards * tall,
        moved=count * rows * width * 6 + width * shards * tall * 2,
        grid=(shards, PLANE),
        in_specs=[pl.BlockSpec((rows, tall), lambda s, q: (0, s))] * count
        + [pl.BlockSpec((rows, 2 * depth), lambda s, q: (0, q))] * count,
        out_specs=pl.BlockSpec((2, 1, tall, depth), lambda s, q: (0, s, 0, q)),
        out_shape=jax.ShapeDtypeStruct((2, shards, tall, PLANE * depth), bf16),
        scratch_shapes=[pltpu.VMEM((tall, count * rows), bf16)],
    )(*xs, *ys)


def hop(a, bits):
    n = lax.axis_size("dp")
    return lax.ppermute(a, "dp", [(i, i ^ bits) for i in range(n)])


def climb(a, step):
    n = lax.axis_size("tensor")
    return lax.ppermute(a, "tensor", [(i, i + step) for i in range(n) if 0 <= i + step < n])


def plane_gather(a):
    half = a.shape[0] // 2
    by_x, by_y = hop(a, 2), hop(a, 4)
    far = jnp.concatenate([hop(by_x[:half], 4), hop(by_y[half:], 2)], 0)
    return a, by_x, by_y, far


def added(a, b):
    return (a.astype(f32) + b.astype(f32)).astype(a.dtype)


def plane_scatter(own, to_x, to_y, far):
    half = own.shape[0] // 2
    first, second = hop(far[:half], 2), hop(far[half:], 4)
    to_y = jnp.concatenate([added(to_y[:half], first), to_y[half:]], 0)
    to_x = jnp.concatenate([to_x[:half], added(to_x[half:], second)], 0)
    return own.astype(f32) + hop(to_x, 2).astype(f32) + hop(to_y, 4).astype(f32)


def by_chip(parts, chip):
    a, b, c, d = parts
    odd = (chip & 1) == 1
    a, b, c, d = (
        jnp.where(odd, b, a),
        jnp.where(odd, a, b),
        jnp.where(odd, d, c),
        jnp.where(odd, c, d),
    )
    high = (chip & 2) == 2
    return (
        jnp.where(high, c, a),
        jnp.where(high, d, b),
        jnp.where(high, a, c),
        jnp.where(high, b, d),
    )


def trade(pieces, axis, chip):
    come = []
    for r in range(PLANE):
        piece = lax.dynamic_index_in_dim(pieces, chip ^ r, axis, keepdims=False)
        come.append(piece if r == 0 else hop(piece, 2 * r))
    return by_chip(come, chip)


def sum_all(blocks, chip, core):
    parts, shards = blocks.shape[:2]
    pairs = blocks.reshape((parts // 2, 2) + blocks.shape[1:])
    come = hop(lax.dynamic_index_in_dim(pairs, 1 - core, 1, keepdims=False), 1)
    mine = added(lax.dynamic_index_in_dim(pairs, core, 1, keepdims=False), come)
    own = [lax.dynamic_index_in_dim(mine, chip ^ r, 0, keepdims=False) for r in range(PLANE)]
    total = plane_scatter(*own).astype(bf16)
    return lax.psum_scatter(total, "tensor", scatter_dimension=0, tiled=False)


def rotary_tables(positions):
    half_size = HD // 2
    frequency = THETA ** (-2.0 * jnp.arange(half_size, dtype=f32) / HD)
    angles = positions.astype(f32)[:, None] * frequency[None, :]
    cos, sin = jnp.cos(angles), jnp.sin(angles)
    return (
        jnp.concatenate([cos, cos] * (LANES // HD), -1),
        jnp.concatenate([-sin, sin] * (LANES // HD), -1),
    )


def norm_backward(grad_scaled, unrounded, norm_scale):
    return norm_scale * (grad_scaled - unrounded * jnp.mean(unrounded * grad_scaled, -1, keepdims=True))


def shards(
    tokens, segments, attn_norm, w_query, w_key, w_value, w_out, mlp_norm, w_gate, w_up, w_down, cotangent
):
    dp_count, tp_count = lax.axis_size("dp"), lax.axis_size("tensor")
    groups = dp_count // 8
    place = lax.axis_index("tensor")
    index = lax.axis_index("dp")
    core, chip = index & 1, (index >> 1) & 3
    seqs, span, width = tokens.shape
    rows = seqs * span
    block = width // 8

    group_sets = [[g * 8 + l for g in range(groups)] for l in range(8)]

    def widen(a, axis):
        if groups == 1:
            return a
        return lax.all_gather(a, "dp", axis=axis, tiled=True, axis_index_groups=group_sets)

    def narrow(a, axis):
        if groups == 1:
            return a
        return lax.psum_scatter(
            a.astype(bf16), "dp", scatter_dimension=axis, tiled=True, axis_index_groups=group_sets
        )

    def inward(a):
        if groups == 1:
            return a
        lead = a.shape[:-1]
        return jnp.swapaxes(a.reshape(lead + (groups, 8, -1)), -3, -2).reshape(lead + (-1,))

    def outward(a):
        if groups == 1:
            return a
        lead = a.shape[:-1]
        return jnp.swapaxes(a.reshape(lead + (8, groups, -1)), -3, -2).reshape(lead + (-1,))

    eight = [[g * 8 + l for l in range(8)] for g in range(groups)]

    def everywhere(a):
        near = lax.all_gather(a, "tensor", axis=0, tiled=False)
        if groups == 1:
            return lax.all_gather(near, "dp", axis=0, tiled=False)
        return lax.all_gather(near, "dp", axis=0, tiled=False, axis_index_groups=eight)

    tokens = inward(tokens).reshape(rows, width)
    cotangent = inward(cotangent).reshape(rows, width)
    attn_norm, mlp_norm = widen(attn_norm, 0), widen(mlp_norm, 0)
    w_query, w_key, w_value = widen(w_query, 0), widen(w_key, 0), widen(w_value, 0)
    w_gate, w_up = widen(w_gate, 0), widen(w_up, 0)
    w_out, w_down = widen(w_out, 1), widen(w_down, 1)

    kv_cols = 2 * w_key.shape[1]
    kv_group = w_query.shape[1] // w_key.shape[1]
    gains = jnp.concatenate(
        [
            jnp.pad(attn_norm, (0, kv_cols - block))[None],
            jnp.pad(mlp_norm, (0, kv_cols - block))[None],
            jnp.zeros((14, kv_cols), bf16),
        ],
        0,
    )
    all_kv = everywhere(jnp.concatenate([jnp.concatenate([w_key, w_value], 1), gains], 0))
    all_q = everywhere(w_query)
    all_out = everywhere(w_out)
    gain_one = all_kv[:, 0, block, :block].reshape(width).astype(f32)
    gain_two = all_kv[:, 0, block + 1, :block].reshape(width).astype(f32)

    def columns(w):
        pieces = w.reshape(block, PLANE, -1)
        near = jnp.stack(trade(pieces, 1, chip), 0)
        mine = lax.all_gather(near, "tensor", axis=0, tiled=False)
        other = hop(mine, 1)
        pair = [jnp.where(core == 0, mine, other), jnp.where(core == 0, other, mine)]
        return jnp.stack(pair, 2).reshape(tp_count, width, -1)

    def lines(w):
        pieces = w.reshape(PLANE, -1, block)
        near = jnp.concatenate(trade(pieces, 0, chip), 1)
        mine = lax.all_gather(near, "tensor", axis=0, tiled=False)
        other = hop(mine, 1)
        tall = mine.shape[1]
        mine, other = (a.reshape(tp_count, tall, PLANE, block) for a in (mine, other))
        pair = [jnp.where(core == 0, mine, other), jnp.where(core == 0, other, mine)]
        return jnp.stack(pair, 3).reshape(tp_count, tall, width)

    all_gate, all_up, all_down = columns(w_gate), columns(w_up), lines(w_down)
    chunks = [slice(b * span, (b + 1) * span) for b in range(seqs)]
    cot_full = [jnp.concatenate(plane_gather(cotangent[c]), 0) for c in chunks]

    cos, sin = rotary_tables(place * span + jnp.arange(span, dtype=jnp.int32))
    cos_rows, sin_rows = jnp.tile(cos, (seqs, 1)), jnp.tile(sin, (seqs, 1))
    x = tokens.astype(f32)
    norm_one = lax.rsqrt(jnp.mean(x * x, -1, keepdims=True) + EPS)
    scaled_one = (x * norm_one).astype(bf16)
    normed_one = (scaled_one.astype(f32) * gain_one).astype(bf16)
    pair = project_pairs(normed_one, all_kv, cos_rows, sin_rows, block)
    pairs = [pair]
    for _ in range(tp_count - 1):
        pairs.append(climb(pairs[-1], 1))
    queries = project_queries(normed_one, all_q, cos_rows, sin_rows)

    seg_blocks = segments.reshape(seqs, tp_count, span)
    own_seg = lax.dynamic_index_in_dim(seg_blocks, place, 1, keepdims=False)
    here = jnp.arange(span, dtype=jnp.int32)
    bias = []
    for j in range(tp_count):
        key_seg = lax.dynamic_index_in_dim(seg_blocks, jnp.maximum(place - j, 0), 1, keepdims=False)
        allowed = key_seg[:, :, None] == own_seg[:, None, :]
        if j == 0:
            allowed &= here[None, :, None] <= here[None, None, :]
        bias.append(jnp.where(allowed, 0.0, -1e30).astype(f32))
    bias = jnp.concatenate(bias, 1)
    spot = place.reshape(1).astype(jnp.int32)
    heads_out, lse = attend(spot, queries, pairs, bias, span, kv_group)
    residual = project_out(heads_out, all_out, tokens)

    norm_two = lax.rsqrt(jnp.mean(residual * residual, -1, keepdims=True) + EPS)
    scaled_two = (residual * norm_two).astype(bf16)
    normed_two = (scaled_two.astype(f32) * gain_two).astype(bf16)
    full_two = [jnp.concatenate(plane_gather(normed_two[c]), 0) for c in chunks]
    forward = [gate_up(f, all_gate, all_up) for f in full_two]
    inner = [f[2] for f in forward]

    def quarters(a):
        return [a[r * span : (r + 1) * span] for r in range(PLANE)]

    backward = [inner_grads(g, all_down, f[0], f[1]) for g, f in zip(cot_full, forward)]
    d_gate, d_up = [d[0] for d in backward], [d[1] for d in backward]
    grad_normed_two = jnp.concatenate(
        [plane_scatter(*quarters(normed_grads(a, b, all_gate, all_up))) for a, b in zip(d_gate, d_up)], 0
    )

    def core_sum(a):
        come = hop(lax.dynamic_index_in_dim(a, 1 - core, 0, keepdims=False), 1)
        mine = added(lax.dynamic_index_in_dim(a, core, 0, keepdims=False), come)
        return lax.psum_scatter(mine, "tensor", scatter_dimension=0, tiled=False)

    def columns_back(a):
        return jnp.concatenate(trade(core_sum(a), 0, chip), 1)

    def lines_back(a):
        mine = core_sum(a)
        return jnp.concatenate(trade(mine.reshape(mine.shape[0], PLANE, block), 1, chip), 0)

    grad_down = lines_back(row_weight_grad(inner, cot_full, tp_count))
    grad_gate = columns_back(column_weight_grad(full_two, d_gate, tp_count))
    grad_up = columns_back(column_weight_grad(full_two, d_up, tp_count))

    mixed = [plane_scatter(*quarters(down(i, all_down))) for i in inner]
    mixed = (residual + jnp.concatenate(mixed, 0)).astype(bf16)

    gain_two_terms = jnp.sum(scaled_two.astype(f32) * grad_normed_two, 0)
    unrounded_two = residual * norm_two
    grad_residual = cotangent.astype(f32) + norm_backward(
        grad_normed_two * gain_two, unrounded_two, norm_two
    )

    grad_low = grad_residual.astype(bf16)
    grad_heads = unproject_out(grad_low, all_out)
    grad_out = sum_all(out_weight_grad(heads_out, grad_low, 8, tp_count), chip, core)
    dq, dkv = unattend(spot, queries, grad_heads, pairs, bias, lse, cos, sin, span, kv_group)
    come = climb(dkv[tp_count - 1], -1)
    for j in range(tp_count - 2, 0, -1):
        come = climb(added(dkv[j], come), -1)
    dkv = finish_pairs(dkv[0], come, cos_rows, sin_rows)
    grad_query = sum_all(query_weight_grad(normed_one, dq, 8, tp_count), chip, core)
    grad_normed_one = unproject_in(dq, dkv, all_q, all_kv)
    gain_one_terms = jnp.sum(scaled_one.astype(f32) * grad_normed_one, 0)
    gain_terms = jnp.stack([gain_one_terms.reshape(8, block), gain_two_terms.reshape(8, block)], 1)
    gain_terms = jnp.pad(gain_terms, ((0, 0), (0, 14), (0, kv_cols - block)))
    kv_sum = sum_all(pair_weight_grad(normed_one, dkv, gain_terms, 8, tp_count), chip, core)
    grad_tokens = grad_residual + norm_backward(grad_normed_one * gain_one, x * norm_one, norm_one)
    grad_tokens = grad_tokens.astype(bf16)

    def gain_share(line):
        line = narrow(line, 0)
        share = line.shape[0] // tp_count
        return lax.dynamic_slice_in_dim(line, place * share, share, 0).astype(f32)

    half = kv_cols // 2
    return (
        outward(mixed).reshape(seqs, span, width),
        outward(grad_tokens).reshape(seqs, span, width),
        gain_share(kv_sum[block, :block]),
        narrow(grad_query, 0).astype(f32),
        narrow(kv_sum[:block, :half], 0).astype(f32),
        narrow(kv_sum[:block, half:], 0).astype(f32),
        narrow(grad_out, 1).astype(f32),
        gain_share(kv_sum[block + 1, :block]),
        narrow(grad_gate, 0).astype(f32),
        narrow(grad_up, 0).astype(f32),
        narrow(grad_down, 1).astype(f32),
    )


def solution(mesh):
    placed = (
        P("dp", "tensor", None),
        P("dp", None),
        P("dp"),
        P("dp", "tensor"),
        P("dp", "tensor"),
        P("dp", "tensor"),
        P("tensor", "dp"),
        P("dp"),
        P("dp", "tensor"),
        P("dp", "tensor"),
        P("tensor", "dp"),
        P("dp", "tensor", None),
    )
    return jax.shard_map(
        shards,
        mesh=mesh,
        in_specs=placed,
        out_specs=(
            P("dp", "tensor", None),
            P("dp", "tensor", None),
            P(("dp", "tensor")),
            P("dp", "tensor"),
            P("dp", "tensor"),
            P("dp", "tensor"),
            P("tensor", "dp"),
            P(("dp", "tensor")),
            P("dp", "tensor"),
            P("dp", "tensor"),
            P("tensor", "dp"),
        ),
        check_vma=False,
    )
```

```python
import functools

import jax
import jax.numpy as jnp
from jax import lax
from jax.experimental import pallas as pl
from jax.experimental.pallas import tpu as pltpu
from jax.sharding import PartitionSpec as P

HD = 64
EPS = 1e-05
THETA = 500000.0
LOG2E = 1.4426950408889634
LANES = 128
PLANE = 4
f32 = jnp.float32
bf16 = jnp.bfloat16


def call(body, flops, moved, vmem=50, **kw):
    return pl.pallas_call(
        body,
        compiler_params=pltpu.CompilerParams(vmem_limit_bytes=vmem * 2**20),
        cost_estimate=pl.CostEstimate(flops=flops, bytes_accessed=moved, transcendentals=0),
        **kw,
    )


def nn(a, b):
    return jnp.dot(a, b, preferred_element_type=f32)


def nt(a, b):
    return lax.dot_general(a, b, (((1,), (1,)), ((), ())), preferred_element_type=f32)


def tn(a, b):
    return lax.dot_general(a, b, (((0,), (0,)), ((), ())), preferred_element_type=f32)


def swap_halves(x):
    lane = lax.broadcasted_iota(jnp.int32, x.shape, 1)
    return jnp.where(lane % HD < HD // 2, pltpu.roll(x, LANES - HD // 2, 1), pltpu.roll(x, HD // 2, 1))


def gather_keys(k_refs, v_refs, blocks):
    k = jnp.concatenate([k_refs[j][0, 0] for j in range(blocks)], 0)
    v = jnp.concatenate([v_refs[j][0, 0] for j in range(blocks)], 0)
    return k, v


def padded_rows(part, e):
    zero = jnp.zeros_like(part)
    return jnp.concatenate([part, zero] if e == 0 else [zero, part], 0)


def attend_blocks(blocks, group, q_ref, k_refs, v_refs, bias_ref, o_ref, lse_ref, qt_ref, ot_ref):
    span = q_ref.shape[0]
    n = blocks * span
    k, v = gather_keys(k_refs, v_refs, blocks)
    vt = v.T
    qt_ref[...] = q_ref[...].T
    factor = HD**-0.5 * LOG2E

    def step(i, carry):
        for e in range(2):
            head = e * group + i
            rows = pl.ds(pl.multiple_of(head * HD, HD), HD)
            scores = nn(k, padded_rows(qt_ref[rows, :], e))
            logits = scores * factor + bias_ref[0, :n, :]
            top = jnp.max(logits, 0, keepdims=True)
            weights = jnp.exp2(logits - top)
            total = jnp.sum(weights, 0, keepdims=True)
            out = nn(vt[e * HD : (e + 1) * HD], weights.astype(bf16))
            ot_ref[rows, :] = out * (1.0 / total)
            lse_ref[0, 0, pl.ds(head, 1), :] = top + jnp.log2(total)
        return carry

    lax.fori_loop(0, group, step, 0)
    o_ref[...] = ot_ref[...].T.astype(bf16)


def attend_kernel(count, group, place, *refs):
    q_ref, k_refs, v_refs = refs[0], refs[1 : 1 + count], refs[1 + count : 1 + 2 * count]
    rest = refs[1 + 2 * count :]
    for blocks in range(1, count + 1):

        @pl.when(place[0] == blocks - 1)
        def _(blocks=blocks):
            attend_blocks(blocks, group, q_ref, k_refs, v_refs, *rest)


def key_specs(count, span):
    return [
        pl.BlockSpec(
            (1, 1, span, LANES), lambda b, p, s, part=part, j=j: (jnp.maximum(s[0] - j, 0), part, b, p)
        )
        for part in range(2)
        for j in range(count)
    ]


def attend(place, queries, pairs, bias, span, group):
    rows, width = queries.shape
    count = pairs.shape[0]
    seqs = rows // span
    kv_width = pairs.shape[3]
    tiles = kv_width // LANES
    wide = width // tiles
    in_specs = [pl.BlockSpec((span, wide), lambda b, p, s: (b, p))] + key_specs(count, span)
    in_specs.append(pl.BlockSpec((1, count * span, span), lambda b, p, s: (b, 0, 0)))
    heads = wide // HD
    spec = pltpu.PrefetchScalarGridSpec(
        num_scalar_prefetch=1,
        grid=(seqs, tiles),
        in_specs=in_specs,
        out_specs=[
            pl.BlockSpec((span, wide), lambda b, p, s: (b, p)),
            pl.BlockSpec((1, 1, heads, span), lambda b, p, s: (b, p, 0, 0)),
        ],
        scratch_shapes=[pltpu.VMEM((wide, span), bf16), pltpu.VMEM((wide, span), f32)],
    )
    return call(
        functools.partial(attend_kernel, count, group),
        flops=rows * width * span * count * 8,
        moved=rows * width * 4,
        grid_spec=spec,
        out_shape=[
            jax.ShapeDtypeStruct((rows, width), bf16),
            jax.ShapeDtypeStruct((seqs, tiles, heads, span), f32),
        ],
    )(place, queries, *([pairs] * (2 * count)), bias)


def unattend_blocks(
    blocks, count, group, q_ref, g_ref, k_refs, v_refs, bias_ref, lse_ref, cos_ref, sin_ref,
    dq_ref, dkv_ref, qt_ref, gt_ref, dqt_ref, dk_ref, dv_ref,
):
    span = q_ref.shape[0]
    n = blocks * span
    k, v = gather_keys(k_refs, v_refs, blocks)
    kt = k.T
    qt_ref[...] = q_ref[...].T
    gt_ref[...] = g_ref[...].T
    dk_ref[...] = jnp.zeros_like(dk_ref)
    dv_ref[...] = jnp.zeros_like(dv_ref)
    factor = HD**-0.5 * LOG2E
    lane = lax.broadcasted_iota(jnp.int32, (span, LANES), 1)

    def moved(tile, b, e):
        if b != e:
            tile = pltpu.roll(tile, HD, 1)
        return jnp.where((lane < HD) if e == 0 else (lane >= HD), tile, 0.0).astype(bf16)

    def step(i, carry):
        for e in range(2):
            tile_at = pl.ds(pl.multiple_of((e * (group // 2) + i) * LANES, LANES), LANES)
            q_tile = q_ref[:, tile_at].astype(f32)
            g_tile = g_ref[:, tile_at].astype(f32)
            all_ds, all_p = [], []
            for b in range(2):
                head = e * group + 2 * i + b
                rows = pl.ds(pl.multiple_of(head * HD, HD), HD)
                scores = nn(k, padded_rows(qt_ref[rows, :], e))
                lse = lse_ref[0, 0, pl.ds(head, 1), :]
                probs = jnp.exp2(scores * factor + bias_ref[0, :n, :] - lse)
                dp = nn(v, padded_rows(gt_ref[rows, :], e))
                delta = jnp.sum(probs * dp, 0, keepdims=True)
                ds = (probs * (dp - delta)).astype(bf16)
                dqt_ref[rows, :] = nn(kt[e * HD : (e + 1) * HD], ds)
                all_ds.append(ds)
                all_p.append(probs.astype(bf16))
            q_rows = jnp.concatenate([moved(q_tile, b, e) for b in range(2)], 0)
            g_rows = jnp.concatenate([moved(g_tile, b, e) for b in range(2)], 0)
            dk_ref[:n, :] += nn(jnp.concatenate(all_ds, 1), q_rows)
            dv_ref[:n, :] += nn(jnp.concatenate(all_p, 1), g_rows)
        return carry

    lax.fori_loop(0, group // 2, step, 0)
    scale = HD**-0.5
    dq = dqt_ref[...].T * scale
    for t in range(dq.shape[1] // LANES):
        part = dq[:, t * LANES : (t + 1) * LANES]
        dq_ref[:, t * LANES : (t + 1) * LANES] = (
            part * cos_ref[...] - swap_halves(part) * sin_ref[...]
        ).astype(bf16)
    for n in range(count):
        j = blocks - 1 - n if n < blocks else n
        dkv_ref[n, 0] = (dk_ref[j * span : (j + 1) * span, :] * scale).astype(bf16)
        dkv_ref[n, 1] = dv_ref[j * span : (j + 1) * span, :].astype(bf16)


def unattend_kernel(count, group, skip, place, *refs):
    refs = refs[skip:]
    q_ref, g_ref, k_refs, v_refs = refs[0], refs[1], refs[2 : 2 + count], refs[2 + count : 2 + 2 * count]
    rest = refs[2 + 2 * count :]
    for blocks in range(1, count + 1):

        @pl.when(place[0] == blocks - 1)
        def _(blocks=blocks):
            unattend_blocks(blocks, count, group, q_ref, g_ref, k_refs, v_refs, *rest)


def unattend(place, queries, grads, pairs, bias, lse, cos, sin, span, group, deps=()):
    rows, width = queries.shape
    count = pairs.shape[0]
    seqs = rows // span
    kv_width = pairs.shape[3]
    tiles = kv_width // LANES
    wide = width // tiles
    heads = wide // HD
    tall = pl.BlockSpec((span, wide), lambda b, p, s: (b, p))
    table = pl.BlockSpec((span, LANES), lambda b, p, s: (0, 0))
    deps = jax.tree.leaves(deps)
    in_specs = [pl.BlockSpec(memory_space=pl.ANY)] * len(deps) + [tall, tall] + key_specs(count, span)
    in_specs += [
        pl.BlockSpec((1, count * span, span), lambda b, p, s: (b, 0, 0)),
        pl.BlockSpec((1, 1, heads, span), lambda b, p, s: (b, p, 0, 0)),
        table,
        table,
    ]
    spec = pltpu.PrefetchScalarGridSpec(
        num_scalar_prefetch=1,
        grid=(seqs, tiles),
        in_specs=in_specs,
        out_specs=[tall, pl.BlockSpec((count, 2, span, LANES), lambda b, p, s: (0, 0, b, p))],
        scratch_shapes=[
            pltpu.VMEM((wide, span), bf16),
            pltpu.VMEM((wide, span), bf16),
            pltpu.VMEM((wide, span), f32),
            pltpu.VMEM((count * span, LANES), f32),
            pltpu.VMEM((count * span, LANES), f32),
        ],
    )
    return call(
        functools.partial(unattend_kernel, count, group, len(deps)),
        flops=rows * width * span * count * 20,
        moved=rows * width * 8,
        grid_spec=spec,
        out_shape=[
            jax.ShapeDtypeStruct((rows, width), bf16),
            jax.ShapeDtypeStruct((count, 2, rows, kv_width), bf16),
        ],
    )(place, *deps, queries, grads, *([pairs] * (2 * count)), bias, lse, cos, sin)


def turn(y, cos, sin, out_ref, start=0):
    for t in range(y.shape[1] // LANES):
        part = y[:, t * LANES : (t + 1) * LANES]
        out_ref[:, t * LANES : (t + 1) * LANES] = (part * cos + swap_halves(part) * sin).astype(bf16)


def block_home(spot, half, r):
    core = spot[1] if half == 0 else 1 - spot[1]
    return 2 * (spot[2] ^ r) + core


def lanes_at(ref, at, size):
    return ref[:, pl.ds(pl.multiple_of(at * size, size), size)]


def by_block(ref, spot, size):
    return jnp.concatenate(
        [lanes_at(ref, block_home(spot, half, r), size) for half in range(2) for r in range(PLANE)], 1
    )


def by_slot(ref, spot, shards, size):
    return jnp.concatenate([lanes_at(ref, slot_home(spot, s, shards), size) for s in range(shards)], 1)


def slot_home(spot, s, shards):
    return lax.rem(spot[0] + shards - s, shards)


def grid_call(body, grid, in_specs, out_specs, out_shape, flops, moved, scratch=(), deps=()):
    deps = jax.tree.leaves(deps)

    def late(spot, *refs):
        body(spot, *refs[len(deps) :])

    run = call(
        late,
        flops=flops,
        moved=moved,
        grid_spec=pltpu.PrefetchScalarGridSpec(
            num_scalar_prefetch=1,
            grid=grid,
            in_specs=[pl.BlockSpec(memory_space=pl.ANY)] * len(deps) + list(in_specs),
            out_specs=out_specs,
            scratch_shapes=list(scratch),
        ),
        out_shape=out_shape,
    )
    return lambda spot, *arrays: run(spot, *deps, *arrays)


def project_pairs(spot, normed, weights, cos, sin, depth, deps=()):
    rows, width = normed.shape
    parts, shards, _, cols = weights.shape
    half = cols // 2

    def body(spot, x_ref, w_ref, cos_ref, sin_ref, o_ref):
        w = w_ref[:, 0, :depth, :].reshape(parts * depth, cols)
        y = nn(x_ref[...], w)
        k = y[:, :half]
        o_ref[0] = (k * cos_ref[...] + swap_halves(k) * sin_ref[...]).astype(bf16)
        o_ref[1] = y[:, half:].astype(bf16)

    whole = lambda s, _: (0, 0)
    return grid_call(
        body,
        (shards,),
        [
            pl.BlockSpec((rows, width), whole),
            pl.BlockSpec((parts, 1, weights.shape[2], cols), lambda s, _: (0, s, 0, 0)),
            pl.BlockSpec((rows, LANES), whole),
            pl.BlockSpec((rows, LANES), whole),
        ],
        pl.BlockSpec((2, rows, half), lambda s, spot: (0, 0, slot_home(spot, s, shards))),
        jax.ShapeDtypeStruct((2, rows, half * shards), bf16),
        2 * rows * width * shards * cols,
        weights.size * 2 + normed.size * 2,
        deps=deps,
    )(spot, normed, weights, cos, sin)


def project_queries(spot, normed, weights, cos, sin):
    rows, width = normed.shape
    shards, depth, cols = weights[0].shape
    count = len(weights)

    def body(spot, *refs):
        x_ref, w_refs, cos_ref, sin_ref, o_ref, xs_ref = refs[0], refs[1 : 1 + count], *refs[1 + count :]

        @pl.when(pl.program_id(0) == 0)
        def _():
            xs_ref[...] = by_block(x_ref, spot, depth)

        y = nn(xs_ref[...], jnp.concatenate([w[0] for w in w_refs], 0))
        turn(y, cos_ref[...], sin_ref[...], o_ref)

    whole = lambda s, _: (0, 0)
    return grid_call(
        body,
        (shards,),
        [pl.BlockSpec((rows, width), whole)]
        + [pl.BlockSpec((1, depth, cols), lambda s, _: (s, 0, 0))] * count
        + [pl.BlockSpec((rows, LANES), whole)] * 2,
        pl.BlockSpec((rows, cols), lambda s, spot: (0, slot_home(spot, s, shards))),
        jax.ShapeDtypeStruct((rows, cols * shards), bf16),
        2 * rows * width * shards * cols,
        width * shards * cols * 2 + normed.size * 4,
        [pltpu.VMEM((rows, width), bf16)],
    )(spot, normed, *weights, cos, sin)


def folded(w):
    half = w.shape[0] // 2
    return jnp.concatenate([w[:half], w[half:]], 1)


def unfolded(w):
    half = w.shape[1] // 2
    return jnp.concatenate([w[:, :half], w[:, half:]], 0)


def project_out(spot, heads_out, weights, tokens, deps=()):
    rows, width = heads_out.shape
    shards, depth, cols = weights[0].shape
    depth, cols = 2 * depth, cols // 2
    count = len(weights)
    tall = min(256, rows)

    def body(spot, *refs):
        x_ref, w_refs, t_ref, o_ref = refs[0], refs[1 : 1 + count], *refs[1 + count :]
        x = by_slot(x_ref, spot, shards, depth)
        for n, w_ref in enumerate(w_refs):
            at = block_home(spot, n // PLANE, n % PLANE)
            y = nn(x, jnp.concatenate([unfolded(w_ref[s]) for s in range(shards)], 0))
            o_ref[:, pl.ds(pl.multiple_of(at * cols, cols), cols)] = lanes_at(t_ref, at, cols).astype(f32) + y

    tile = pl.BlockSpec((tall, width), lambda m, _: (m, 0))
    return grid_call(
        body,
        (rows // tall,),
        [tile] + [pl.BlockSpec(w.shape, lambda m, _: (0, 0, 0)) for w in weights] + [tile],
        tile,
        jax.ShapeDtypeStruct((rows, cols * count), f32),
        2 * rows * width * count * cols,
        width * cols * count * 2 + rows * width * 8,
        deps=deps,
    )(spot, heads_out, *weights, tokens)


def unproject_out(spot, grads, weights, deps=()):
    rows, width = grads.shape
    shards, depth, cols = weights[0].shape
    depth, cols = 2 * depth, cols // 2
    count = len(weights)

    def body(spot, *refs):
        x_ref, w_refs, o_ref, xs_ref = refs[0], refs[1 : 1 + count], *refs[1 + count :]

        @pl.when(pl.program_id(0) == 0)
        def _():
            xs_ref[...] = by_block(x_ref, spot, cols)

        w = jnp.concatenate([unfolded(w_ref[0]) for w_ref in w_refs], 1)
        o_ref[...] = nt(xs_ref[...], w).astype(bf16)

    return grid_call(
        body,
        (shards,),
        [pl.BlockSpec((rows, width), lambda s, _: (0, 0))]
        + [pl.BlockSpec((1, depth // 2, 2 * cols), lambda s, _: (s, 0, 0))] * count,
        pl.BlockSpec((rows, depth), lambda s, spot: (0, slot_home(spot, s, shards))),
        jax.ShapeDtypeStruct((rows, depth * shards), bf16),
        2 * rows * width * shards * depth,
        width * shards * depth * 2 + rows * width * 6,
        [pltpu.VMEM((rows, width), bf16)],
        deps=deps,
    )(spot, grads, *weights)


def unproject_in(spot, dq, dkv, w_q, w_kv):
    rows, width = dq.shape
    shards, depth, cols = w_q[0].shape
    thin = w_kv.shape[3] // 2
    count = len(w_q)
    tall = min(256, rows)

    def body(spot, *refs):
        q_ref, kv_ref, wq_refs, wkv_ref, o_ref = *refs[:2], refs[2 : 2 + count], *refs[2 + count :]
        left = by_slot(q_ref, spot, shards, cols)
        thin_left = jnp.concatenate(
            [
                kv_ref[n, :, pl.ds(pl.multiple_of(slot_home(spot, s, shards) * thin, thin), thin)]
                for s in range(shards)
                for n in range(2)
            ],
            1,
        )
        for n, w_ref in enumerate(wq_refs):
            at = block_home(spot, n // PLANE, n % PLANE)
            y = nt(left, jnp.concatenate([w_ref[s] for s in range(shards)], 1))
            y += nt(thin_left, jnp.concatenate([wkv_ref[at, s, :depth, :] for s in range(shards)], 1))
            o_ref[:, pl.ds(pl.multiple_of(at * depth, depth), depth)] = y

    tile = pl.BlockSpec((tall, width), lambda m, _: (m, 0))
    return grid_call(
        body,
        (rows // tall,),
        [tile, pl.BlockSpec((2, tall, dkv.shape[2]), lambda m, _: (0, m, 0))]
        + [pl.BlockSpec(w.shape, lambda m, _: (0, 0, 0)) for w in w_q]
        + [pl.BlockSpec(w_kv.shape, lambda m, _: (0, 0, 0, 0))],
        pl.BlockSpec((tall, count * depth), lambda m, _: (m, 0)),
        jax.ShapeDtypeStruct((rows, count * depth), f32),
        2 * rows * count * depth * shards * (cols + 2 * thin),
        count * depth * shards * cols * 2 + w_kv.size * 2 + rows * width * 6,
    )(spot, dq, dkv, *w_q, w_kv)


def of_core(ref, core, depth):
    return ref[:, pl.ds(pl.multiple_of(core * depth, depth), depth)]


def in_blocks_grad(spot, normed, dq, dkv, gains, shards):
    rows, width = normed.shape
    depth = width // PLANE // 2
    y = dq if dkv is None else dkv
    cols = (dq.shape[1] if dkv is None else 2 * dkv.shape[2]) // shards
    extra = 0 if gains is None else gains.shape[1]

    def body(spot, x_ref, y_ref, *refs):
        for n, core in ((0, spot[1]), (1, 1 - spot[1])):
            x, o_ref = of_core(x_ref, core, depth), refs[-2 + n]
            totals = [tn(x, y_ref[...])] if dkv is None else [tn(x, y_ref[0]), tn(x, y_ref[1])]
            thin = cols // len(totals)
            for s in range(shards):
                for m, total in enumerate(totals):
                    o_ref[0, s, :depth, m * thin : (m + 1) * thin] = total[:, s * thin : (s + 1) * thin].astype(bf16)
                if extra:
                    o_ref[0, s, depth:, :] = refs[0][core].astype(bf16)

    whole = pl.BlockSpec(y.shape, (lambda q, _: (0, 0)) if dkv is None else (lambda q, _: (0, 0, 0)))
    more = [] if gains is None else [pl.BlockSpec((2, extra, gains.shape[2]), lambda q, _: (q, 0, 0))]
    shape = jax.ShapeDtypeStruct((PLANE, shards, depth + extra, cols), bf16)
    return grid_call(
        body,
        (PLANE,),
        [pl.BlockSpec((rows, 2 * depth), lambda q, _: (0, q)), whole] + more,
        [pl.BlockSpec((1, shards, depth + extra, cols), lambda q, _: (q, 0, 0, 0))] * 2,
        [shape] * 2,
        2 * rows * width * shards * cols,
        rows * width * 4 + width * shards * cols * 2,
    )(spot, normed, y, *([] if gains is None else [gains]))


def out_blocks_grad(spot, heads_out, grads, shards):
    rows, width = grads.shape
    cols, depth = width // PLANE // 2, heads_out.shape[1] // shards

    def body(spot, x_ref, y_ref, *o_refs):
        for n, core in ((0, spot[1]), (1, 1 - spot[1])):
            total = tn(x_ref[...], of_core(y_ref, core, cols)).astype(bf16)
            for s in range(shards):
                o_refs[n][0, s] = folded(total[s * depth : (s + 1) * depth])

    shape = jax.ShapeDtypeStruct((PLANE, shards, depth // 2, 2 * cols), bf16)
    return grid_call(
        body,
        (PLANE,),
        [
            pl.BlockSpec((rows, heads_out.shape[1]), lambda q, _: (0, 0)),
            pl.BlockSpec((rows, 2 * cols), lambda q, _: (0, q)),
        ],
        [pl.BlockSpec((1, shards, depth // 2, 2 * cols), lambda q, _: (q, 0, 0, 0))] * 2,
        [shape] * 2,
        2 * rows * width * heads_out.shape[1],
        rows * width * 4 + width * heads_out.shape[1] * 2,
    )(spot, heads_out, grads)


def finish_pairs(spot, own, cos, sin, deps=()):
    _, rows, width = own.shape

    def body(spot, a_ref, cos_ref, sin_ref, o_ref):
        k = a_ref[0].astype(f32)
        o_ref[0] = (k * cos_ref[...] - swap_halves(k) * sin_ref[...]).astype(bf16)
        o_ref[1] = a_ref[1]

    tile = pl.BlockSpec((2, rows, LANES), lambda s, _: (0, 0, s))
    table = pl.BlockSpec((rows, LANES), lambda s, _: (0, 0))
    return grid_call(
        body,
        (width // LANES,),
        [tile, table, table],
        tile,
        jax.ShapeDtypeStruct(own.shape, bf16),
        own.size * 6,
        own.size * 4,
        deps=deps,
    )(spot, own, cos, sin)


def lanes_of(x_refs, core, depth):
    return jnp.concatenate(
        [
            jnp.concatenate([lanes_at(x, 2 * q + core, depth) for q in range(PLANE)], 1)
            for x in x_refs
        ],
        0,
    )


def gate_up(spot, xs, own, other):
    span, width = xs[0].shape
    rows = span * len(xs)
    shards, half, cols = own[0].shape
    depth = half // PLANE
    count = len(xs)

    def body(spot, *refs):
        x_refs, (og_ref, ou_ref, tg_ref, tu_ref, go_ref, uo_ref, i_ref) = refs[:count], refs[count:]
        core = spot[1]
        left, right = lanes_of(x_refs, core, depth), lanes_of(x_refs, 1 - core, depth)
        gate = nn(left, og_ref[0]) + nn(right, tg_ref[0])
        up = nn(left, ou_ref[0]) + nn(right, tu_ref[0])
        go_ref[...] = gate.astype(bf16)
        uo_ref[...] = up.astype(bf16)
        i_ref[...] = (gate / (1.0 + jnp.exp(-gate)) * up).astype(bf16)

    weight = pl.BlockSpec((1, half, cols), lambda s, _: (s, 0, 0))
    tile = pl.BlockSpec((rows, cols), lambda s, _: (0, s))
    shape = jax.ShapeDtypeStruct((rows, shards * cols), bf16)
    return grid_call(
        body,
        (shards,),
        [pl.BlockSpec((span, width), lambda s, _: (0, 0))] * count + [weight] * 4,
        [tile] * 3,
        [shape] * 3,
        4 * rows * width * shards * cols,
        own[0].size * 8 + rows * width * 10,
    )(spot, *xs, *own, *other)


def inner_grads(spot, gs, own, other, gate, up, deps=()):
    span, width = gs[0].shape
    rows = span * len(gs)
    shards, _, deep, cols = own.shape
    depth, cols = cols // 2, 2 * deep
    count = len(gs)

    def body(spot, *refs):
        x_refs, (own_ref, other_ref, g_ref, u_ref, dg_ref, du_ref) = refs[:count], refs[count:]
        core = spot[1]
        grad = jnp.zeros((rows, cols), f32)
        for w_ref, at in ((own_ref, core), (other_ref, 1 - core)):
            w = jnp.concatenate([unfolded(w_ref[0, q]) for q in range(PLANE)], 1)
            grad += nt(lanes_of(x_refs, at, depth), w)
        gate, up = g_ref[...].astype(f32), u_ref[...].astype(f32)
        s = 1.0 / (1.0 + jnp.exp(-gate))
        dg_ref[...] = (grad * up * s * (1.0 + gate * (1.0 - s))).astype(bf16)
        du_ref[...] = (grad * gate * s).astype(bf16)

    tile = pl.BlockSpec((rows, cols), lambda s, _: (0, s))
    weight = pl.BlockSpec((1, PLANE, deep, 2 * depth), lambda s, _: (s, 0, 0, 0))
    shape = jax.ShapeDtypeStruct((rows, shards * cols), bf16)
    return grid_call(
        body,
        (shards,),
        [pl.BlockSpec((span, width), lambda s, _: (0, 0))] * count + [weight, weight, tile, tile],
        [tile] * 2,
        [shape] * 2,
        2 * rows * width * shards * cols,
        own.size * 4 + rows * width * 10,
        deps=deps,
    )(spot, *gs, own, other, gate, up)


def split_rows(total, o_refs, at, depth):
    span = total.shape[0] // len(o_refs)
    for r, o_ref in enumerate(o_refs):
        o_ref[:, pl.ds(pl.multiple_of(at * depth, depth), depth)] = total[r * span : (r + 1) * span].astype(bf16)


def down(spot, inner, own, other, deps=()):
    rows, width = inner.shape
    shards, _, deep, cols = own.shape
    depth = cols // 2
    span = rows // PLANE

    def body(spot, x_ref, own_ref, other_ref, *o_refs):
        core = spot[1]
        for w_ref, at in ((own_ref, core), (other_ref, 1 - core)):
            w = jnp.concatenate([unfolded(w_ref[s, 0]) for s in range(shards)], 0)
            split_rows(nn(x_ref[...], w), o_refs, at, depth)

    weight = pl.BlockSpec((shards, 1, deep, cols), lambda q, _: (0, q, 0, 0))
    return grid_call(
        body,
        (PLANE,),
        [pl.BlockSpec((rows, width), lambda q, _: (0, 0)), weight, weight],
        [pl.BlockSpec((span, 2 * depth), lambda q, _: (0, q))] * PLANE,
        [jax.ShapeDtypeStruct((span, 2 * PLANE * depth), bf16)] * PLANE,
        4 * rows * width * PLANE * depth,
        own.size * 4 + rows * width * 4,
        deps=deps,
    )(spot, inner, own, other)


def normed_grads(spot, d_gate, d_up, own, other):
    rows, width = d_gate.shape
    shards, half, cols = own[0].shape
    depth = half // PLANE
    span = rows // PLANE

    def body(spot, g_ref, u_ref, og_ref, ou_ref, tg_ref, tu_ref, *o_refs):
        core = spot[1]
        for gate_ref, up_ref, at in ((og_ref, ou_ref, core), (tg_ref, tu_ref, 1 - core)):
            total = nt(g_ref[...], jnp.concatenate([gate_ref[s] for s in range(shards)], 1))
            total += nt(u_ref[...], jnp.concatenate([up_ref[s] for s in range(shards)], 1))
            split_rows(total, o_refs, at, depth)

    weight = pl.BlockSpec((shards, depth, cols), lambda q, _: (0, q, 0))
    left = pl.BlockSpec((rows, width), lambda q, _: (0, 0))
    return grid_call(
        body,
        (PLANE,),
        [left, left] + [weight] * 4,
        [pl.BlockSpec((span, 2 * depth), lambda q, _: (0, q))] * PLANE,
        [jax.ShapeDtypeStruct((span, 2 * half), bf16)] * PLANE,
        8 * rows * width * half,
        own[0].size * 8 + rows * width * 6,
    )(spot, d_gate, d_up, *own, *other)


def turned(x_refs, xt_ref):
    at = 0
    for x_ref in x_refs:
        xt_ref[:, at : at + x_ref.shape[0]] = x_ref[...].T
        at += x_ref.shape[0]


def summed(xt_ref, ys):
    total, at = None, 0
    for y in ys:
        part = nn(xt_ref[:, at : at + y.shape[0]], y)
        total, at = (part if total is None else total + part), at + y.shape[0]
    return total


def column_weight_grad(spot, xs, ys, shards, deps=()):
    span, width = xs[0].shape
    rows = span * len(xs)
    cols = ys[0].shape[1] // shards
    depth = width // PLANE // 2
    count = len(xs)
    pair = 2

    def body(spot, *refs):
        x_refs, y_refs, o_refs, xt_ref = refs[:count], refs[count:-3], refs[-3:-1], refs[-1]

        @pl.when(pl.program_id(1) == 0)
        def _():
            turned(x_refs, xt_ref)

        total = summed(xt_ref, [r[...] for r in y_refs]).astype(bf16)
        first = spot[1] == 0
        for q in range(pair):
            a = total[2 * q * depth : (2 * q + 1) * depth]
            b = total[(2 * q + 1) * depth : (2 * q + 2) * depth]
            o_refs[0][0, q] = jnp.where(first, a, b)
            o_refs[1][0, q] = jnp.where(first, b, a)

    shape = jax.ShapeDtypeStruct((shards, PLANE, depth, cols), bf16)
    return grid_call(
        body,
        (PLANE // pair, shards),
        [pl.BlockSpec((span, 2 * pair * depth), lambda q, s, _: (0, q))] * count
        + [pl.BlockSpec((y.shape[0], cols), lambda q, s, _: (0, s)) for y in ys],
        [pl.BlockSpec((1, pair, depth, cols), lambda q, s, _: (s, q, 0, 0))] * 2,
        [shape] * 2,
        2 * rows * width * shards * cols,
        rows * width * 6 + width * shards * cols * 2,
        [pltpu.VMEM((2 * pair * depth, rows), bf16)],
        deps=deps,
    )(spot, *xs, *ys)


def row_weight_grad(spot, xs, ys, shards):
    span, width = ys[0].shape
    rows = span * len(ys)
    tall = xs[0].shape[1] // shards
    depth = width // PLANE // 2
    count = len(xs)
    pair = 2 if shards % 2 == 0 else 1

    def body(spot, *refs):
        x_refs, y_refs, o_refs, xt_ref = refs[:count], refs[count:-3], refs[-3:-1], refs[-1]

        @pl.when(pl.program_id(1) == 0)
        def _():
            turned(x_refs, xt_ref)

        y = jnp.concatenate([r[...] for r in y_refs], 0)
        total = nn(xt_ref[...], y).astype(bf16)
        first = spot[1] == 0
        for s in range(pair):
            part = total[s * tall : (s + 1) * tall]
            a, b = folded(part[:, :depth]), folded(part[:, depth:])
            o_refs[0][s, 0] = jnp.where(first, a, b)
            o_refs[1][s, 0] = jnp.where(first, b, a)

    shape = jax.ShapeDtypeStruct((shards, PLANE, tall // 2, 2 * depth), bf16)
    return grid_call(
        body,
        (shards // pair, PLANE),
        [pl.BlockSpec((x.shape[0], pair * tall), lambda s, q, _: (0, s)) for x in xs]
        + [pl.BlockSpec((span, 2 * depth), lambda s, q, _: (0, q))] * len(ys),
        [pl.BlockSpec((pair, 1, tall // 2, 2 * depth), lambda s, q, _: (s, q, 0, 0))] * 2,
        [shape] * 2,
        2 * rows * width * shards * tall,
        rows * width * 6 + width * shards * tall * 2,
        [pltpu.VMEM((pair * tall, rows), bf16)],
    )(spot, *xs, *ys)


def hop(a, bits):
    n = lax.axis_size("dp")
    return lax.ppermute(a, "dp", [(i, i ^ bits) for i in range(n)])


def added(a, b):
    return (a.astype(f32) + b.astype(f32)).astype(a.dtype)


def plane_gather(a):
    return [a] + [hop(a, 2 * r) for r in range(1, PLANE)]


def plane_scatter(blocks):
    total = blocks[0].astype(f32)
    for r in range(1, PLANE):
        total += hop(blocks[r], 2 * r).astype(f32)
    return total


def shift(a, step):
    n = lax.axis_size("tensor")
    return lax.ppermute(a, "tensor", [(i, (i + step) % n) for i in range(n)])


def line_gather(a):
    return [a] + [shift(a, s) for s in range(1, lax.axis_size("tensor"))]


def line_scatter(blocks):
    n, place = lax.axis_size("tensor"), lax.axis_index("tensor")
    total = lax.dynamic_index_in_dim(blocks, place, 0, keepdims=False).astype(f32)
    for step in range(1, n):
        mine = lax.dynamic_index_in_dim(blocks, lax.rem(place + step, n), 0, keepdims=False)
        total += shift(mine, step).astype(f32)
    return total


def after(a, *others):
    others = jax.tree.leaves(others)
    place = pl.BlockSpec(memory_space=pl.ANY)
    return pl.pallas_call(
        lambda *refs: None,
        in_specs=[place] * (1 + len(others)),
        out_specs=place,
        out_shape=jax.ShapeDtypeStruct(a.shape, a.dtype),
        input_output_aliases={0: 0},
        cost_estimate=pl.CostEstimate(flops=1, bytes_accessed=1, transcendentals=0),
    )(a, *others)


def by_chip(parts, chip):
    a, b, c, d = parts
    odd = (chip & 1) == 1
    a, b, c, d = (
        jnp.where(odd, b, a),
        jnp.where(odd, a, b),
        jnp.where(odd, d, c),
        jnp.where(odd, c, d),
    )
    high = (chip & 2) == 2
    return (
        jnp.where(high, c, a),
        jnp.where(high, d, b),
        jnp.where(high, a, c),
        jnp.where(high, b, d),
    )


def trade(pieces, axis, chip):
    come = []
    for r in range(PLANE):
        piece = lax.dynamic_index_in_dim(pieces, chip ^ r, axis, keepdims=False)
        come.append(piece if r == 0 else hop(piece, 2 * r))
    return by_chip(come, chip)


def sum_all(pair, chip):
    mine = added(pair[0], hop(pair[1], 1))
    own = [lax.dynamic_index_in_dim(mine, chip ^ r, 0, keepdims=False) for r in range(PLANE)]
    return line_scatter(plane_scatter(own).astype(bf16))


def rotary_tables(positions):
    half_size = HD // 2
    frequency = THETA ** (-2.0 * jnp.arange(half_size, dtype=f32) / HD)
    angles = positions.astype(f32)[:, None] * frequency[None, :]
    cos, sin = jnp.cos(angles), jnp.sin(angles)
    return (
        jnp.concatenate([cos, cos] * (LANES // HD), -1),
        jnp.concatenate([-sin, sin] * (LANES // HD), -1),
    )


def norm_backward(grad_scaled, unrounded, norm_scale):
    return norm_scale * (grad_scaled - unrounded * jnp.mean(unrounded * grad_scaled, -1, keepdims=True))


def shards(
    tokens, segments, attn_norm, w_query, w_key, w_value, w_out, mlp_norm, w_gate, w_up, w_down, cotangent
):
    dp_count, tp_count = lax.axis_size("dp"), lax.axis_size("tensor")
    groups = dp_count // 8
    place = lax.axis_index("tensor")
    index = lax.axis_index("dp")
    core, chip = index & 1, (index >> 1) & 3
    seqs, span, width = tokens.shape
    rows = seqs * span
    block = width // 8

    group_sets = [[g * 8 + l for g in range(groups)] for l in range(8)]

    def widen(a, axis):
        if groups == 1:
            return a
        return lax.all_gather(a, "dp", axis=axis, tiled=True, axis_index_groups=group_sets)

    def narrow(a, axis):
        if groups == 1:
            return a
        return lax.psum_scatter(
            a.astype(bf16), "dp", scatter_dimension=axis, tiled=True, axis_index_groups=group_sets
        )

    def inward(a):
        if groups == 1:
            return a
        lead = a.shape[:-1]
        return jnp.swapaxes(a.reshape(lead + (groups, 8, -1)), -3, -2).reshape(lead + (-1,))

    def outward(a):
        if groups == 1:
            return a
        lead = a.shape[:-1]
        return jnp.swapaxes(a.reshape(lead + (8, groups, -1)), -3, -2).reshape(lead + (-1,))

    eight = [[g * 8 + l for l in range(8)] for g in range(groups)]

    def along(a):
        return lax.all_gather(a, "tensor", axis=0, tiled=False)

    def in_plane(a):
        if groups == 1:
            return lax.all_gather(a, "dp", axis=0, tiled=False)
        return lax.all_gather(a, "dp", axis=0, tiled=False, axis_index_groups=eight)

    tokens = inward(tokens).reshape(rows, width)
    cotangent = inward(cotangent).reshape(rows, width)
    attn_norm, mlp_norm = widen(attn_norm, 0), widen(mlp_norm, 0)
    w_query, w_key, w_value = widen(w_query, 0), widen(w_key, 0), widen(w_value, 0)
    w_gate, w_up = widen(w_gate, 0), widen(w_up, 0)
    w_out, w_down = widen(w_out, 1), widen(w_down, 1)

    kv_cols = 2 * w_key.shape[1]
    kv_group = w_query.shape[1] // w_key.shape[1]
    gains = jnp.concatenate(
        [
            jnp.pad(attn_norm, (0, kv_cols - block))[None],
            jnp.pad(mlp_norm, (0, kv_cols - block))[None],
            jnp.zeros((14, kv_cols), bf16),
        ],
        0,
    )
    near_kv = line_gather(jnp.concatenate([jnp.concatenate([w_key, w_value], 1), gains], 0))
    lines = w_down.reshape(PLANE, 2, -1, block)
    pieces = jnp.stack(
        [
            jnp.swapaxes(w_gate.reshape(block, PLANE, -1), 0, 1),
            jnp.swapaxes(w_up.reshape(block, PLANE, -1), 0, 1),
            jnp.concatenate([lines[:, 0], lines[:, 1]], 2),
        ],
        1,
    )
    all_kv = in_plane(jnp.stack(near_kv, 0))
    near = jnp.stack(trade(after(pieces, all_kv), 0, chip), 1)
    gain_one = all_kv[:, 0, block, :block].reshape(width).astype(f32)
    gain_two = all_kv[:, 0, block + 1, :block].reshape(width).astype(f32)
    lined = line_gather(after(jnp.stack([w_query, folded(w_out)], 0), near_kv[1:]))
    lined_q, lined_out = (jnp.stack([a[n] for a in lined], 0) for n in range(2))
    chunks = [slice(b * span, (b + 1) * span) for b in range(seqs)]

    spot = jnp.stack([place, core, chip]).astype(jnp.int32)
    cos, sin = rotary_tables(place * span + jnp.arange(span, dtype=jnp.int32))
    cos_rows, sin_rows = jnp.tile(cos, (seqs, 1)), jnp.tile(sin, (seqs, 1))
    x = tokens.astype(f32)
    norm_one = lax.rsqrt(jnp.mean(x * x, -1, keepdims=True) + EPS)
    scaled_one = (x * norm_one).astype(bf16)
    normed_one = (scaled_one.astype(f32) * gain_one).astype(bf16)
    pair = project_pairs(spot, normed_one, all_kv, cos_rows, sin_rows, block, deps=lined[1:])
    pairs = along(pair)
    tall = near.shape[1] * near.shape[2]
    own_gate, own_up = along(after(near[0].reshape(tall, -1), pair)), along(after(near[1].reshape(tall, -1), pair))

    def both_cores(blocks):
        return blocks + [hop(b, 1) for b in blocks]

    all_q = plane_gather(after(lined_q, pair))
    all_out = plane_gather(after(lined_out, all_q[1:]))
    late = after(cotangent, all_q[1:])
    cot_full = [plane_gather(late[c]) for c in chunks]
    all_q, all_out = both_cores(all_q), both_cores(all_out)
    queries = project_queries(spot, normed_one, all_q, cos_rows, sin_rows)

    seg_blocks = segments.reshape(seqs, tp_count, span)
    own_seg = lax.dynamic_index_in_dim(seg_blocks, place, 1, keepdims=False)
    here = jnp.arange(span, dtype=jnp.int32)
    bias = []
    for j in range(tp_count):
        key_seg = lax.dynamic_index_in_dim(seg_blocks, jnp.maximum(place - j, 0), 1, keepdims=False)
        allowed = key_seg[:, :, None] == own_seg[:, None, :]
        if j == 0:
            allowed &= here[None, :, None] <= here[None, None, :]
        bias.append(jnp.where(allowed, 0.0, -1e30).astype(f32))
    bias = jnp.concatenate(bias, 1)
    heads_out, lse = attend(spot, queries, pairs, bias, span, kv_group)
    residual = project_out(spot, heads_out, all_out, tokens, deps=cot_full)

    norm_two = lax.rsqrt(jnp.mean(residual * residual, -1, keepdims=True) + EPS)
    scaled_two = (residual * norm_two).astype(bf16)
    normed_two = (scaled_two.astype(f32) * gain_two).astype(bf16)
    full_two = []
    for c in chunks:
        full_two.append(plane_gather(after(normed_two[c], full_two[-1][1:] if full_two else ())))
    own_gate, own_up = after(own_gate, normed_two), after(own_up, normed_two)
    own_in = (own_gate, own_up)
    other_in = (hop(own_gate, 1), hop(own_up, 1))
    own_down = along(after(near[2], residual))
    other_down = hop(own_down, 1)
    forward = [gate_up(spot, f, own_in, other_in) for f in full_two]
    inner = [f[2] for f in forward]

    def core_sum(pair):
        return added(pair[0], hop(pair[1], 1))

    def line_sum(a):
        return lax.psum_scatter(a, "tensor", scatter_dimension=0, tiled=False)

    down_parts = row_weight_grad(spot, inner, sum(cot_full, []), tp_count)
    down_pair = core_sum(down_parts)
    down_sum = line_sum(down_pair)
    d_gate, d_up, to_plane = [], [], []
    for b, (g, f) in enumerate(zip(cot_full, forward)):
        deps = down_parts if b == 0 else [down_pair, to_plane[-1]]
        dg, du = inner_grads(spot, g, own_down, other_down, f[0], f[1], deps=deps)
        d_gate.append(dg)
        d_up.append(du)
        to_plane.append(normed_grads(spot, dg, du, own_in, other_in))
    grad_normed_two = jnp.concatenate([plane_scatter(p) for p in to_plane], 0)
    tokens_two = sum(full_two, [])
    gate_parts = column_weight_grad(spot, tokens_two, d_gate, tp_count, deps=to_plane[-1])
    gate_pair = core_sum(gate_parts)
    up_parts = column_weight_grad(spot, tokens_two, d_up, tp_count, deps=gate_parts)
    up_pair = core_sum(up_parts)
    gate_sum = line_sum(gate_pair)

    gain_two_terms = jnp.sum(scaled_two.astype(f32) * grad_normed_two, 0)
    unrounded_two = residual * norm_two
    grad_residual = cotangent.astype(f32) + norm_backward(
        grad_normed_two * gain_two, unrounded_two, norm_two
    )

    grad_low = grad_residual.astype(bf16)
    grad_heads = unproject_out(spot, grad_low, all_out, deps=up_parts)
    out_parts = out_blocks_grad(spot, heads_out, grad_low, tp_count)
    deps = [out_parts, gate_pair, up_pair, down_sum]
    dq, dkv = unattend(spot, queries, grad_heads, pairs, bias, lse, cos, sin, span, kv_group, deps=deps)
    dkv = line_sum(after(dkv, gate_sum))
    grad_out = unfolded(sum_all((out_parts[0], after(out_parts[1], dq)), chip))
    query_parts = in_blocks_grad(spot, normed_one, dq, None, None, tp_count)
    grad_query = sum_all(query_parts, chip)
    to_rows = [down(spot, i, own_down, other_down, deps=query_parts) for i in inner]
    mixed = (residual + jnp.concatenate([plane_scatter(r) for r in to_rows], 0)).astype(bf16)
    up_sum = line_sum(after(up_pair, dkv))

    dkv = finish_pairs(spot, dkv, cos_rows, sin_rows, deps=[grad_out, grad_query])
    grad_normed_one = unproject_in(spot, dq, dkv, all_q, all_kv)
    gain_one_terms = jnp.sum(scaled_one.astype(f32) * grad_normed_one, 0)
    gain_terms = jnp.stack([gain_one_terms.reshape(8, block), gain_two_terms.reshape(8, block)], 1)
    gain_terms = jnp.pad(gain_terms, ((0, 0), (0, 14), (0, kv_cols - block)))
    kv_parts = in_blocks_grad(spot, normed_one, dq, dkv, gain_terms, tp_count)
    kv_sum = sum_all(kv_parts, chip)
    grad_tokens = grad_residual + norm_backward(grad_normed_one * gain_one, x * norm_one, norm_one)
    grad_tokens = grad_tokens.astype(bf16)
    sums = jnp.stack([down_sum, gate_sum, up_sum], 1)
    come = trade(sums, 0, chip)
    grad_down = jnp.concatenate([jnp.concatenate([c[0, :, :block], c[0, :, block:]], 0) for c in come], 0)
    grad_gate, grad_up = (jnp.concatenate([c[n] for c in come], 1) for n in (1, 2))

    def gain_share(line):
        line = narrow(line, 0)
        share = line.shape[0] // tp_count
        return lax.dynamic_slice_in_dim(line, place * share, share, 0).astype(f32)

    half = kv_cols // 2
    return (
        outward(mixed).reshape(seqs, span, width),
        outward(grad_tokens).reshape(seqs, span, width),
        gain_share(kv_sum[block, :block]),
        narrow(grad_query, 0).astype(f32),
        narrow(kv_sum[:block, :half], 0).astype(f32),
        narrow(kv_sum[:block, half:], 0).astype(f32),
        narrow(grad_out, 1).astype(f32),
        gain_share(kv_sum[block + 1, :block]),
        narrow(grad_gate, 0).astype(f32),
        narrow(grad_up, 0).astype(f32),
        narrow(grad_down, 1).astype(f32),
    )


def solution(mesh):
    placed = (
        P("dp", "tensor", None),
        P("dp", None),
        P("dp"),
        P("dp", "tensor"),
        P("dp", "tensor"),
        P("dp", "tensor"),
        P("tensor", "dp"),
        P("dp"),
        P("dp", "tensor"),
        P("dp", "tensor"),
        P("tensor", "dp"),
        P("dp", "tensor", None),
    )
    return jax.shard_map(
        shards,
        mesh=mesh,
        in_specs=placed,
        out_specs=(
            P("dp", "tensor", None),
            P("dp", "tensor", None),
            P(("dp", "tensor")),
            P("dp", "tensor"),
            P("dp", "tensor"),
            P("dp", "tensor"),
            P("tensor", "dp"),
            P(("dp", "tensor")),
            P("dp", "tensor"),
            P("dp", "tensor"),
            P("tensor", "dp"),
        ),
        check_vma=False,
    )
```

```python
import functools

import jax
import jax.numpy as jnp
from jax import lax
from jax.experimental import pallas as pl
from jax.experimental.pallas import tpu as pltpu
from jax.sharding import PartitionSpec as P

HD = 64
EPS = 1e-05
THETA = 500000.0
LOG2E = 1.4426950408889634
LANES = 128
PLANE = 4
f32 = jnp.float32
bf16 = jnp.bfloat16


def call(body, flops, moved, vmem=50, **kw):
    return pl.pallas_call(
        body,
        compiler_params=pltpu.CompilerParams(vmem_limit_bytes=vmem * 2**20),
        cost_estimate=pl.CostEstimate(flops=flops, bytes_accessed=moved, transcendentals=0),
        **kw,
    )


def nn(a, b):
    return jnp.dot(a, b, preferred_element_type=f32)


def nt(a, b):
    return lax.dot_general(a, b, (((1,), (1,)), ((), ())), preferred_element_type=f32)


def tn(a, b):
    return lax.dot_general(a, b, (((0,), (0,)), ((), ())), preferred_element_type=f32)


def swap_halves(x):
    lane = lax.broadcasted_iota(jnp.int32, x.shape, 1)
    return jnp.where(lane % HD < HD // 2, pltpu.roll(x, LANES - HD // 2, 1), pltpu.roll(x, HD // 2, 1))


def gather_keys(k_refs, v_refs, blocks):
    k = jnp.concatenate([k_refs[j][0, 0] for j in range(blocks)], 0)
    v = jnp.concatenate([v_refs[j][0, 0] for j in range(blocks)], 0)
    return k, v


def padded_rows(part, e):
    zero = jnp.zeros_like(part)
    return jnp.concatenate([part, zero] if e == 0 else [zero, part], 0)


def attend_blocks(blocks, group, q_ref, k_refs, v_refs, bias_ref, o_ref, lse_ref, qt_ref, ot_ref):
    span = q_ref.shape[0]
    n = blocks * span
    k, v = gather_keys(k_refs, v_refs, blocks)
    vt = v.T
    qt_ref[...] = q_ref[...].T
    factor = HD**-0.5 * LOG2E

    def step(i, carry):
        for e in range(2):
            head = e * group + i
            rows = pl.ds(pl.multiple_of(head * HD, HD), HD)
            scores = nn(k, padded_rows(qt_ref[rows, :], e))
            logits = scores * factor + bias_ref[0, :n, :]
            top = jnp.max(logits, 0, keepdims=True)
            weights = jnp.exp2(logits - top)
            total = jnp.sum(weights, 0, keepdims=True)
            out = nn(vt[e * HD : (e + 1) * HD], weights.astype(bf16))
            ot_ref[rows, :] = out * (1.0 / total)
            lse_ref[0, 0, pl.ds(head, 1), :] = top + jnp.log2(total)
        return carry

    lax.fori_loop(0, group, step, 0)
    o_ref[...] = ot_ref[...].T.astype(bf16)


def attend_kernel(count, group, place, *refs):
    q_ref, k_refs, v_refs = refs[0], refs[1 : 1 + count], refs[1 + count : 1 + 2 * count]
    rest = refs[1 + 2 * count :]
    for blocks in range(1, count + 1):

        @pl.when(place[0] == blocks - 1)
        def _(blocks=blocks):
            attend_blocks(blocks, group, q_ref, k_refs, v_refs, *rest)


def key_specs(count, span):
    return [
        pl.BlockSpec(
            (1, 1, span, LANES), lambda b, p, s, part=part, j=j: (jnp.maximum(s[0] - j, 0), part, b, p)
        )
        for part in range(2)
        for j in range(count)
    ]


def attend(place, queries, pairs, bias, span, group):
    rows, width = queries.shape
    count = pairs.shape[0]
    seqs = rows // span
    kv_width = pairs.shape[3]
    tiles = kv_width // LANES
    wide = width // tiles
    in_specs = [pl.BlockSpec((span, wide), lambda b, p, s: (b, p))] + key_specs(count, span)
    in_specs.append(pl.BlockSpec((1, count * span, span), lambda b, p, s: (b, 0, 0)))
    heads = wide // HD
    spec = pltpu.PrefetchScalarGridSpec(
        num_scalar_prefetch=1,
        grid=(seqs, tiles),
        in_specs=in_specs,
        out_specs=[
            pl.BlockSpec((span, wide), lambda b, p, s: (b, p)),
            pl.BlockSpec((1, 1, heads, span), lambda b, p, s: (b, p, 0, 0)),
        ],
        scratch_shapes=[pltpu.VMEM((wide, span), bf16), pltpu.VMEM((wide, span), f32)],
    )
    return call(
        functools.partial(attend_kernel, count, group),
        flops=rows * width * span * count * 8,
        moved=rows * width * 4,
        grid_spec=spec,
        out_shape=[
            jax.ShapeDtypeStruct((rows, width), bf16),
            jax.ShapeDtypeStruct((seqs, tiles, heads, span), f32),
        ],
    )(place, queries, *([pairs] * (2 * count)), bias)


def unattend_blocks(
    blocks, count, group, q_ref, g_ref, k_refs, v_refs, bias_ref, lse_ref, cos_ref, sin_ref,
    dq_ref, dkv_ref, qt_ref, gt_ref, dqt_ref, dk_ref, dv_ref,
):
    span = q_ref.shape[0]
    n = blocks * span
    k, v = gather_keys(k_refs, v_refs, blocks)
    kt = k.T
    qt_ref[...] = q_ref[...].T
    gt_ref[...] = g_ref[...].T
    dk_ref[...] = jnp.zeros_like(dk_ref)
    dv_ref[...] = jnp.zeros_like(dv_ref)
    factor = HD**-0.5 * LOG2E
    lane = lax.broadcasted_iota(jnp.int32, (span, LANES), 1)

    def moved(tile, b, e):
        if b != e:
            tile = pltpu.roll(tile, HD, 1)
        return jnp.where((lane < HD) if e == 0 else (lane >= HD), tile, 0.0).astype(bf16)

    def step(i, carry):
        for e in range(2):
            tile_at = pl.ds(pl.multiple_of((e * (group // 2) + i) * LANES, LANES), LANES)
            q_tile = q_ref[:, tile_at].astype(f32)
            g_tile = g_ref[:, tile_at].astype(f32)
            all_ds, all_p = [], []
            for b in range(2):
                head = e * group + 2 * i + b
                rows = pl.ds(pl.multiple_of(head * HD, HD), HD)
                scores = nn(k, padded_rows(qt_ref[rows, :], e))
                lse = lse_ref[0, 0, pl.ds(head, 1), :]
                probs = jnp.exp2(scores * factor + bias_ref[0, :n, :] - lse)
                dp = nn(v, padded_rows(gt_ref[rows, :], e))
                delta = jnp.sum(probs * dp, 0, keepdims=True)
                ds = (probs * (dp - delta)).astype(bf16)
                dqt_ref[rows, :] = nn(kt[e * HD : (e + 1) * HD], ds)
                all_ds.append(ds)
                all_p.append(probs.astype(bf16))
            q_rows = jnp.concatenate([moved(q_tile, b, e) for b in range(2)], 0)
            g_rows = jnp.concatenate([moved(g_tile, b, e) for b in range(2)], 0)
            dk_ref[:n, :] += nn(jnp.concatenate(all_ds, 1), q_rows)
            dv_ref[:n, :] += nn(jnp.concatenate(all_p, 1), g_rows)
        return carry

    lax.fori_loop(0, group // 2, step, 0)
    scale = HD**-0.5
    dq = dqt_ref[...].T * scale
    for t in range(dq.shape[1] // LANES):
        part = dq[:, t * LANES : (t + 1) * LANES]
        dq_ref[:, t * LANES : (t + 1) * LANES] = (
            part * cos_ref[...] - swap_halves(part) * sin_ref[...]
        ).astype(bf16)
    for n in range(count):
        j = blocks - 1 - n if n < blocks else n
        dkv_ref[n, 0] = (dk_ref[j * span : (j + 1) * span, :] * scale).astype(bf16)
        dkv_ref[n, 1] = dv_ref[j * span : (j + 1) * span, :].astype(bf16)


def unattend_kernel(count, group, skip, place, *refs):
    refs = refs[skip:]
    q_ref, g_ref, k_refs, v_refs = refs[0], refs[1], refs[2 : 2 + count], refs[2 + count : 2 + 2 * count]
    rest = refs[2 + 2 * count :]
    for blocks in range(1, count + 1):

        @pl.when(place[0] == blocks - 1)
        def _(blocks=blocks):
            unattend_blocks(blocks, count, group, q_ref, g_ref, k_refs, v_refs, *rest)


def unattend(place, queries, grads, pairs, bias, lse, cos, sin, span, group, deps=()):
    rows, width = queries.shape
    count = pairs.shape[0]
    seqs = rows // span
    kv_width = pairs.shape[3]
    tiles = kv_width // LANES
    wide = width // tiles
    heads = wide // HD
    tall = pl.BlockSpec((span, wide), lambda b, p, s: (b, p))
    table = pl.BlockSpec((span, LANES), lambda b, p, s: (0, 0))
    deps = jax.tree.leaves(deps)
    in_specs = [pl.BlockSpec(memory_space=pl.ANY)] * len(deps) + [tall, tall] + key_specs(count, span)
    in_specs += [
        pl.BlockSpec((1, count * span, span), lambda b, p, s: (b, 0, 0)),
        pl.BlockSpec((1, 1, heads, span), lambda b, p, s: (b, p, 0, 0)),
        table,
        table,
    ]
    spec = pltpu.PrefetchScalarGridSpec(
        num_scalar_prefetch=1,
        grid=(seqs, tiles),
        in_specs=in_specs,
        out_specs=[tall, pl.BlockSpec((count, 2, span, LANES), lambda b, p, s: (0, 0, b, p))],
        scratch_shapes=[
            pltpu.VMEM((wide, span), bf16),
            pltpu.VMEM((wide, span), bf16),
            pltpu.VMEM((wide, span), f32),
            pltpu.VMEM((count * span, LANES), f32),
            pltpu.VMEM((count * span, LANES), f32),
        ],
    )
    return call(
        functools.partial(unattend_kernel, count, group, len(deps)),
        flops=rows * width * span * count * 20,
        moved=rows * width * 8,
        grid_spec=spec,
        out_shape=[
            jax.ShapeDtypeStruct((rows, width), bf16),
            jax.ShapeDtypeStruct((count, 2, rows, kv_width), bf16),
        ],
    )(place, *deps, queries, grads, *([pairs] * (2 * count)), bias, lse, cos, sin)


def turn(y, cos, sin, out_ref, start=0):
    for t in range(y.shape[1] // LANES):
        part = y[:, t * LANES : (t + 1) * LANES]
        out_ref[:, t * LANES : (t + 1) * LANES] = (part * cos + swap_halves(part) * sin).astype(bf16)


def block_home(spot, half, r):
    core = spot[1] if half == 0 else 1 - spot[1]
    return 2 * (spot[2] ^ r) + core


def lanes_at(ref, at, size):
    return ref[:, pl.ds(pl.multiple_of(at * size, size), size)]


def by_block(ref, spot, size):
    return jnp.concatenate(
        [lanes_at(ref, block_home(spot, half, r), size) for half in range(2) for r in range(PLANE)], 1
    )


def by_slot(ref, spot, shards, size):
    return jnp.concatenate([lanes_at(ref, slot_home(spot, s, shards), size) for s in range(shards)], 1)


def slot_home(spot, s, shards):
    return lax.rem(spot[0] + shards - s, shards)


def grid_call(body, grid, in_specs, out_specs, out_shape, flops, moved, scratch=(), deps=()):
    deps = jax.tree.leaves(deps)

    def late(spot, *refs):
        body(spot, *refs[len(deps) :])

    run = call(
        late,
        flops=flops,
        moved=moved,
        grid_spec=pltpu.PrefetchScalarGridSpec(
            num_scalar_prefetch=1,
            grid=grid,
            in_specs=[pl.BlockSpec(memory_space=pl.ANY)] * len(deps) + list(in_specs),
            out_specs=out_specs,
            scratch_shapes=list(scratch),
        ),
        out_shape=out_shape,
    )
    return lambda spot, *arrays: run(spot, *deps, *arrays)


def project_pairs(spot, normed, weights, cos, sin, depth, deps=()):
    rows, width = normed.shape
    parts, shards, _, cols = weights.shape
    half = cols // 2

    def body(spot, x_ref, w_ref, cos_ref, sin_ref, o_ref):
        w = w_ref[:, 0, :depth, :].reshape(parts * depth, cols)
        y = nn(x_ref[...], w)
        k = y[:, :half]
        o_ref[0] = (k * cos_ref[...] + swap_halves(k) * sin_ref[...]).astype(bf16)
        o_ref[1] = y[:, half:].astype(bf16)

    whole = lambda s, _: (0, 0)
    return grid_call(
        body,
        (shards,),
        [
            pl.BlockSpec((rows, width), whole),
            pl.BlockSpec((parts, 1, weights.shape[2], cols), lambda s, _: (0, s, 0, 0)),
            pl.BlockSpec((rows, LANES), whole),
            pl.BlockSpec((rows, LANES), whole),
        ],
        pl.BlockSpec((2, rows, half), lambda s, spot: (0, 0, slot_home(spot, s, shards))),
        jax.ShapeDtypeStruct((2, rows, half * shards), bf16),
        2 * rows * width * shards * cols,
        weights.size * 2 + normed.size * 2,
        deps=deps,
    )(spot, normed, weights, cos, sin)


def project_queries(spot, normed, weights, cos, sin):
    rows, width = normed.shape
    shards, depth, cols = weights[0].shape
    count = len(weights)

    def body(spot, *refs):
        x_ref, w_refs, cos_ref, sin_ref, o_ref, xs_ref = refs[0], refs[1 : 1 + count], *refs[1 + count :]

        @pl.when(pl.program_id(0) == 0)
        def _():
            xs_ref[...] = by_block(x_ref, spot, depth)

        y = nn(xs_ref[...], jnp.concatenate([w[0] for w in w_refs], 0))
        turn(y, cos_ref[...], sin_ref[...], o_ref)

    whole = lambda s, _: (0, 0)
    return grid_call(
        body,
        (shards,),
        [pl.BlockSpec((rows, width), whole)]
        + [pl.BlockSpec((1, depth, cols), lambda s, _: (s, 0, 0))] * count
        + [pl.BlockSpec((rows, LANES), whole)] * 2,
        pl.BlockSpec((rows, cols), lambda s, spot: (0, slot_home(spot, s, shards))),
        jax.ShapeDtypeStruct((rows, cols * shards), bf16),
        2 * rows * width * shards * cols,
        width * shards * cols * 2 + normed.size * 4,
        [pltpu.VMEM((rows, width), bf16)],
    )(spot, normed, *weights, cos, sin)


def folded(w):
    half = w.shape[0] // 2
    return jnp.concatenate([w[:half], w[half:]], 1)


def unfolded(w):
    half = w.shape[1] // 2
    return jnp.concatenate([w[:, :half], w[:, half:]], 0)


def project_out(spot, heads_out, weights, tokens, deps=()):
    rows, width = heads_out.shape
    shards, depth, cols = weights[0].shape
    depth, cols = 2 * depth, cols // 2
    count = len(weights)
    tall = min(256, rows)

    def body(spot, *refs):
        x_ref, w_refs, t_ref, o_ref = refs[0], refs[1 : 1 + count], *refs[1 + count :]
        x = by_slot(x_ref, spot, shards, depth)
        for n, w_ref in enumerate(w_refs):
            at = block_home(spot, n // PLANE, n % PLANE)
            y = nn(x, jnp.concatenate([unfolded(w_ref[s]) for s in range(shards)], 0))
            o_ref[:, pl.ds(pl.multiple_of(at * cols, cols), cols)] = lanes_at(t_ref, at, cols).astype(f32) + y

    tile = pl.BlockSpec((tall, width), lambda m, _: (m, 0))
    return grid_call(
        body,
        (rows // tall,),
        [tile] + [pl.BlockSpec(w.shape, lambda m, _: (0, 0, 0)) for w in weights] + [tile],
        tile,
        jax.ShapeDtypeStruct((rows, cols * count), f32),
        2 * rows * width * count * cols,
        width * cols * count * 2 + rows * width * 8,
        deps=deps,
    )(spot, heads_out, *weights, tokens)


def unproject_out(spot, grads, weights, deps=()):
    rows, width = grads.shape
    shards, depth, cols = weights[0].shape
    depth, cols = 2 * depth, cols // 2
    count = len(weights)

    def body(spot, *refs):
        x_ref, w_refs, o_ref, xs_ref = refs[0], refs[1 : 1 + count], *refs[1 + count :]

        @pl.when(pl.program_id(0) == 0)
        def _():
            xs_ref[...] = by_block(x_ref, spot, cols)

        w = jnp.concatenate([unfolded(w_ref[0]) for w_ref in w_refs], 1)
        o_ref[...] = nt(xs_ref[...], w).astype(bf16)

    return grid_call(
        body,
        (shards,),
        [pl.BlockSpec((rows, width), lambda s, _: (0, 0))]
        + [pl.BlockSpec((1, depth // 2, 2 * cols), lambda s, _: (s, 0, 0))] * count,
        pl.BlockSpec((rows, depth), lambda s, spot: (0, slot_home(spot, s, shards))),
        jax.ShapeDtypeStruct((rows, depth * shards), bf16),
        2 * rows * width * shards * depth,
        width * shards * depth * 2 + rows * width * 6,
        [pltpu.VMEM((rows, width), bf16)],
        deps=deps,
    )(spot, grads, *weights)


def unproject_in(spot, dq, dkv, w_q, w_kv):
    rows, width = dq.shape
    shards, depth, cols = w_q[0].shape
    thin = w_kv.shape[3] // 2
    count = len(w_q)
    tall = min(256, rows)

    def body(spot, *refs):
        q_ref, kv_ref, wq_refs, wkv_ref, o_ref = *refs[:2], refs[2 : 2 + count], *refs[2 + count :]
        left = by_slot(q_ref, spot, shards, cols)
        thin_left = jnp.concatenate(
            [
                kv_ref[n, :, pl.ds(pl.multiple_of(slot_home(spot, s, shards) * thin, thin), thin)]
                for s in range(shards)
                for n in range(2)
            ],
            1,
        )
        for n, w_ref in enumerate(wq_refs):
            at = block_home(spot, n // PLANE, n % PLANE)
            y = nt(left, jnp.concatenate([w_ref[s] for s in range(shards)], 1))
            y += nt(thin_left, jnp.concatenate([wkv_ref[at, s, :depth, :] for s in range(shards)], 1))
            o_ref[:, pl.ds(pl.multiple_of(at * depth, depth), depth)] = y

    tile = pl.BlockSpec((tall, width), lambda m, _: (m, 0))
    return grid_call(
        body,
        (rows // tall,),
        [tile, pl.BlockSpec((2, tall, dkv.shape[2]), lambda m, _: (0, m, 0))]
        + [pl.BlockSpec(w.shape, lambda m, _: (0, 0, 0)) for w in w_q]
        + [pl.BlockSpec(w_kv.shape, lambda m, _: (0, 0, 0, 0))],
        pl.BlockSpec((tall, count * depth), lambda m, _: (m, 0)),
        jax.ShapeDtypeStruct((rows, count * depth), f32),
        2 * rows * count * depth * shards * (cols + 2 * thin),
        count * depth * shards * cols * 2 + w_kv.size * 2 + rows * width * 6,
    )(spot, dq, dkv, *w_q, w_kv)


def of_core(ref, core, depth):
    return ref[:, pl.ds(pl.multiple_of(core * depth, depth), depth)]


def in_blocks_grad(spot, normed, dq, dkv, gains, shards, deps=()):
    rows, width = normed.shape
    depth = width // PLANE // 2
    y = dq if dkv is None else dkv
    cols = (dq.shape[1] if dkv is None else 2 * dkv.shape[2]) // shards
    extra = 0 if gains is None else gains.shape[1]

    def body(spot, x_ref, y_ref, *refs):
        for n, core in ((0, spot[1]), (1, 1 - spot[1])):
            x, o_ref = of_core(x_ref, core, depth), refs[-2 + n]
            totals = [tn(x, y_ref[...])] if dkv is None else [tn(x, y_ref[0]), tn(x, y_ref[1])]
            thin = cols // len(totals)
            for s in range(shards):
                for m, total in enumerate(totals):
                    o_ref[0, s, :depth, m * thin : (m + 1) * thin] = total[:, s * thin : (s + 1) * thin].astype(bf16)
                if extra:
                    o_ref[0, s, depth:, :] = refs[0][core].astype(bf16)

    whole = pl.BlockSpec(y.shape, (lambda q, _: (0, 0)) if dkv is None else (lambda q, _: (0, 0, 0)))
    more = [] if gains is None else [pl.BlockSpec((2, extra, gains.shape[2]), lambda q, _: (q, 0, 0))]
    shape = jax.ShapeDtypeStruct((PLANE, shards, depth + extra, cols), bf16)
    return grid_call(
        body,
        (PLANE,),
        [pl.BlockSpec((rows, 2 * depth), lambda q, _: (0, q)), whole] + more,
        [pl.BlockSpec((1, shards, depth + extra, cols), lambda q, _: (q, 0, 0, 0))] * 2,
        [shape] * 2,
        2 * rows * width * shards * cols,
        rows * width * 4 + width * shards * cols * 2,
    deps=deps,
        )(spot, normed, y, *([] if gains is None else [gains]))


def out_blocks_grad(spot, heads_out, grads, shards):
    rows, width = grads.shape
    cols, depth = width // PLANE // 2, heads_out.shape[1] // shards

    def body(spot, x_ref, y_ref, *o_refs):
        for n, core in ((0, spot[1]), (1, 1 - spot[1])):
            total = tn(x_ref[...], of_core(y_ref, core, cols)).astype(bf16)
            for s in range(shards):
                o_refs[n][0, s] = folded(total[s * depth : (s + 1) * depth])

    shape = jax.ShapeDtypeStruct((PLANE, shards, depth // 2, 2 * cols), bf16)
    return grid_call(
        body,
        (PLANE,),
        [
            pl.BlockSpec((rows, heads_out.shape[1]), lambda q, _: (0, 0)),
            pl.BlockSpec((rows, 2 * cols), lambda q, _: (0, q)),
        ],
        [pl.BlockSpec((1, shards, depth // 2, 2 * cols), lambda q, _: (q, 0, 0, 0))] * 2,
        [shape] * 2,
        2 * rows * width * heads_out.shape[1],
        rows * width * 4 + width * heads_out.shape[1] * 2,
    )(spot, heads_out, grads)


def finish_pairs(spot, own, cos, sin, deps=()):
    _, rows, width = own.shape

    def body(spot, a_ref, cos_ref, sin_ref, o_ref):
        k = a_ref[0].astype(f32)
        o_ref[0] = (k * cos_ref[...] - swap_halves(k) * sin_ref[...]).astype(bf16)
        o_ref[1] = a_ref[1]

    tile = pl.BlockSpec((2, rows, LANES), lambda s, _: (0, 0, s))
    table = pl.BlockSpec((rows, LANES), lambda s, _: (0, 0))
    return grid_call(
        body,
        (width // LANES,),
        [tile, table, table],
        tile,
        jax.ShapeDtypeStruct(own.shape, bf16),
        own.size * 6,
        own.size * 4,
        deps=deps,
    )(spot, own, cos, sin)


def lanes_of(x_refs, core, depth):
    return jnp.concatenate(
        [
            jnp.concatenate([lanes_at(x, 2 * q + core, depth) for q in range(PLANE)], 1)
            for x in x_refs
        ],
        0,
    )


def still(shape, index):
    return pl.BlockSpec(shape, index, pipeline_mode=pl.Buffered(1))


def gate_up(spot, xs, own, other, deps=()):
    span, width = xs[0].shape
    rows = span * len(xs)
    shards, half, cols = own[0].shape
    depth = half // PLANE
    count = len(xs)

    def body(spot, *refs):
        x_refs, (og_ref, ou_ref, tg_ref, tu_ref, go_ref, uo_ref, i_ref) = refs[:count], refs[count:]
        core = spot[1]
        for at in range(0, count, PLANE):
            part = x_refs[at : at + PLANE]
            left, right = lanes_of(part, core, depth), lanes_of(part, 1 - core, depth)
            gate = nn(left, og_ref[0]) + nn(right, tg_ref[0])
            up = nn(left, ou_ref[0]) + nn(right, tu_ref[0])
            here = slice(at * span, (at + PLANE) * span)
            go_ref[here, :] = gate.astype(bf16)
            uo_ref[here, :] = up.astype(bf16)
            i_ref[here, :] = (gate / (1.0 + jnp.exp(-gate)) * up).astype(bf16)

    weight = pl.BlockSpec((1, half, cols), lambda s, _: (s, 0, 0))
    tile = pl.BlockSpec((rows, cols), lambda s, _: (0, s))
    shape = jax.ShapeDtypeStruct((rows, shards * cols), bf16)
    return grid_call(
        body,
        (shards,),
        [still((span, width), lambda s, _: (0, 0))] * count + [weight] * 4,
        [tile] * 3,
        [shape] * 3,
        4 * rows * width * shards * cols,
        own[0].size * 8 + rows * width * 10,
        deps=deps,
    )(spot, *xs, *own, *other)


def split_rows(total, o_refs, at, depth):
    span = total.shape[0] // len(o_refs)
    for r, o_ref in enumerate(o_refs):
        o_ref[:, pl.ds(pl.multiple_of(at * depth, depth), depth)] = total[r * span : (r + 1) * span].astype(bf16)


def down(spot, inner, own, other, seqs, deps=()):
    rows, width = inner.shape
    shards, _, deep, cols = own.shape
    depth = cols // 2
    tall = rows // seqs
    span = tall // PLANE

    def body(spot, x_ref, own_ref, other_ref, *o_refs):
        core = spot[1]
        for w_ref, at in ((own_ref, core), (other_ref, 1 - core)):
            w = jnp.concatenate([unfolded(w_ref[s, 0]) for s in range(shards)], 0)
            lanes = pl.ds(pl.multiple_of(at * depth, depth), depth)
            for b in range(seqs):
                total = nn(x_ref[b * tall : (b + 1) * tall, :], w).astype(bf16)
                for r, o_ref in enumerate(o_refs):
                    o_ref[b * span : (b + 1) * span, lanes] = total[r * span : (r + 1) * span]

    weight = pl.BlockSpec((shards, 1, deep, cols), lambda q, _: (0, q, 0, 0))
    return grid_call(
        body,
        (PLANE,),
        [still((rows, width), lambda q, _: (0, 0)), weight, weight],
        [pl.BlockSpec((seqs * span, 2 * depth), lambda q, _: (0, q))] * PLANE,
        [jax.ShapeDtypeStruct((seqs * span, 2 * PLANE * depth), bf16)] * PLANE,
        4 * rows * width * PLANE * depth,
        own.size * 4 + rows * width * 4,
        deps=deps,
    )(spot, inner, own, other)


def backward_chunk(spot, chunk, span, gs, own_down, other_down, gate, up, own, other, deps=()):
    width = gs[0].shape[1]
    rows = span * len(gs)
    shards, _, deep, cols = own_down.shape
    depth, cols = cols // 2, 2 * deep
    count = len(gs)
    half = own[0].shape[1]

    def body(spot, *refs):
        x_refs, refs = refs[:count], refs[count:]
        own_ref, other_ref, g_ref, u_ref, og_ref, ou_ref, tg_ref, tu_ref, dg_ref, du_ref = refs[:10]
        o_refs, (gs_ref, us_ref) = refs[10:-2], refs[-2:]
        core, step = spot[1], pl.program_id(0)

        @pl.when(step < shards)
        def _():
            grad = None
            for w_ref, at in ((own_ref, core), (other_ref, 1 - core)):
                w = jnp.concatenate([unfolded(w_ref[0, q]) for q in range(PLANE)], 1)
                part = nt(lanes_of(x_refs, at, depth), w)
                grad = part if grad is None else grad + part
            gate, up = g_ref[...].astype(f32), u_ref[...].astype(f32)
            s = 1.0 / (1.0 + jnp.exp(-gate))
            dg = (grad * up * s * (1.0 + gate * (1.0 - s))).astype(bf16)
            du = (grad * gate * s).astype(bf16)
            dg_ref[...] = dg
            du_ref[...] = du
            gs_ref[step] = dg
            us_ref[step] = du

        @pl.when(step >= shards)
        def _():
            for gate_ref, up_ref, at in ((og_ref, ou_ref, core), (tg_ref, tu_ref, 1 - core)):
                total = None
                for d_ref, w_ref in ((gs_ref, gate_ref), (us_ref, up_ref)):
                    left = jnp.concatenate([d_ref[s] for s in range(shards)], 1)
                    part = nt(left, jnp.concatenate([w_ref[s] for s in range(shards)], 1))
                    total = part if total is None else total + part
                split_rows(total, o_refs, at, depth)

    def early(t):
        return jnp.minimum(t, shards - 1)

    def late(t):
        return jnp.maximum(t - shards, 0)

    tile = pl.BlockSpec((rows, cols), lambda t, _: (0, early(t)))
    given = pl.BlockSpec((rows, cols), lambda t, _: (chunk, early(t)))
    first = pl.BlockSpec((1, PLANE, deep, 2 * depth), lambda t, _: (early(t), 0, 0, 0))
    second = pl.BlockSpec((shards, depth, cols), lambda t, _: (0, late(t), 0))
    shape = jax.ShapeDtypeStruct((rows, shards * cols), bf16)
    outs = grid_call(
        body,
        (shards + PLANE,),
        [still((span, width), lambda t, _: (chunk, 0))] * count + [first] * 2 + [given] * 2 + [second] * 4,
        [tile] * 2 + [pl.BlockSpec((span, 2 * depth), lambda t, _: (0, late(t)))] * PLANE,
        [shape] * 2 + [jax.ShapeDtypeStruct((span, 2 * half), bf16)] * PLANE,
        6 * rows * width * shards * cols,
        own_down.size * 12 + rows * width * 16,
        [pltpu.VMEM((shards, rows, cols), bf16)] * 2,
        deps=deps,
    )(spot, *gs, own_down, other_down, gate, up, *own, *other)
    return outs[0], outs[1], outs[2:]


def norm_backward(grad_scaled, unrounded, norm_scale):
    return norm_scale * (grad_scaled - unrounded * jnp.mean(unrounded * grad_scaled, -1, keepdims=True))


def residual_grads(spot, parts, residual, cotangent, gain, deps=()):
    rows, width = residual.shape
    tall = 128
    count, each = len(parts), len(parts[0])
    per = rows // tall // count

    def body(spot, *refs):
        p_refs = refs[: count * each]
        r_ref, c_ref, g_ref, o_ref, low_ref, sum_ref = refs[count * each :]
        m = pl.program_id(0)

        @pl.when(m == 0)
        def _():
            sum_ref[...] = jnp.zeros_like(sum_ref)

        residual = r_ref[...]
        scale = lax.rsqrt(jnp.mean(residual * residual, -1, keepdims=True) + EPS)
        unrounded = residual * scale
        for b in range(count):

            @pl.when(m // per == b)
            def _(b=b):
                grad = total_of([ref[...] for ref in p_refs[b * each : (b + 1) * each]])
                terms = unrounded.astype(bf16).astype(f32) * grad
                sum_ref[0:1, :] += jnp.sum(terms, 0, keepdims=True)
                out = c_ref[...].astype(f32) + norm_backward(grad * g_ref[...], unrounded, scale)
                o_ref[...] = out
                low_ref[...] = out.astype(bf16)

    def place_of(b):
        return lambda m, _: (jnp.clip(m - b * per, 0, per - 1), 0)

    tile = pl.BlockSpec((tall, width), lambda m, _: (m, 0))
    fixed = lambda m, _: (0, 0)
    return grid_call(
        body,
        (rows // tall,),
        [pl.BlockSpec((tall, width), place_of(b)) for b in range(count) for _ in range(each)]
        + [tile, tile, pl.BlockSpec((1, width), fixed)],
        [tile, tile, pl.BlockSpec((8, width), fixed)],
        [
            jax.ShapeDtypeStruct((rows, width), f32),
            jax.ShapeDtypeStruct((rows, width), bf16),
            jax.ShapeDtypeStruct((8, width), f32),
        ],
        rows * width * 20,
        rows * width * 20,
        deps=deps,
    )(spot, *sum(parts, []), residual, cotangent, gain)


def turned(x_refs, xt_ref):
    at = 0
    for x_ref in x_refs:
        xt_ref[:, at : at + x_ref.shape[0]] = x_ref[...].T
        at += x_ref.shape[0]


def summed(xt_ref, ys):
    total, at = None, 0
    for y in ys:
        part = nn(xt_ref[:, at : at + y.shape[0]], y)
        total, at = (part if total is None else total + part), at + y.shape[0]
    return total


def column_weight_grads(spot, xs, ys, shards, deps=()):
    span, width = xs[0].shape
    rows = span * len(xs)
    cols = ys[0][0].shape[1] // shards
    depth = width // PLANE // 2
    count, lists, pieces = len(xs), len(ys), len(ys[0])
    pair = 2

    def body(spot, *refs):
        x_refs, y_refs, o_refs, xt_ref = refs[:count], refs[count : -1 - 2 * lists], refs[-1 - 2 * lists : -1], refs[-1]
        m, s = pl.program_id(1), pl.program_id(2)

        @pl.when((m == 0) & (s == 0))
        def _():
            turned(x_refs, xt_ref)

        for n in range(lists):

            @pl.when(m == n)
            def _(n=n):
                mine = y_refs[n * pieces : (n + 1) * pieces]
                total = summed(xt_ref, [r[...] for r in mine]).astype(bf16)
                first = spot[1] == 0
                for q in range(pair):
                    a = total[2 * q * depth : (2 * q + 1) * depth]
                    b = total[(2 * q + 1) * depth : (2 * q + 2) * depth]
                    o_refs[2 * n][0, q] = jnp.where(first, a, b)
                    o_refs[2 * n + 1][0, q] = jnp.where(first, b, a)

    def column(n, m, s):
        return jnp.where(m == n, s, jnp.where(m < n, 0, shards - 1))

    shape = jax.ShapeDtypeStruct((shards, PLANE, depth, cols), bf16)
    y_specs, o_specs = [], []
    for n in range(lists):
        y_specs += [
            pl.BlockSpec((y.shape[0], cols), lambda q, m, s, _, n=n: (0, column(n, m, s))) for y in ys[n]
        ]
        o_specs += [
            pl.BlockSpec((1, pair, depth, cols), lambda q, m, s, _, n=n: (column(n, m, s), q, 0, 0))
        ] * 2
    outs = grid_call(
        body,
        (PLANE // pair, lists, shards),
        [pl.BlockSpec((span, 2 * pair * depth), lambda q, m, s, _: (0, q))] * count + y_specs,
        o_specs,
        [shape] * (2 * lists),
        2 * lists * rows * width * shards * cols,
        lists * rows * width * 6 + lists * width * shards * cols * 2,
        [pltpu.VMEM((2 * pair * depth, rows), bf16)],
        deps=deps,
    )(spot, *xs, *sum(ys, []))
    return [outs[2 * n : 2 * n + 2] for n in range(lists)]


def row_weight_grad(spot, xs, ys, span, shards, deps=()):
    width = ys[0].shape[1]
    rows = sum(y.shape[0] for y in ys)
    seqs = ys[0].shape[0] // span
    tall = xs[0].shape[1] // shards
    depth = width // PLANE // 2
    count = len(xs)
    pair = 2 if shards % 2 == 0 else 1

    def body(spot, *refs):
        x_refs, y_refs, o_refs, xt_ref = refs[:count], refs[count:-3], refs[-3:-1], refs[-1]

        @pl.when(pl.program_id(1) == 0)
        def _():
            turned(x_refs, xt_ref)

        y = jnp.concatenate([r[...] for r in y_refs], 0)
        total = nn(xt_ref[...], y).astype(bf16)
        first = spot[1] == 0
        for s in range(pair):
            part = total[s * tall : (s + 1) * tall]
            a, b = folded(part[:, :depth]), folded(part[:, depth:])
            o_refs[0][s, 0] = jnp.where(first, a, b)
            o_refs[1][s, 0] = jnp.where(first, b, a)

    shape = jax.ShapeDtypeStruct((shards, PLANE, tall // 2, 2 * depth), bf16)
    return grid_call(
        body,
        (shards // pair, PLANE),
        [pl.BlockSpec((x.shape[0], pair * tall), lambda s, q, _: (0, s)) for x in xs]
        + [pl.BlockSpec((span, 2 * depth), lambda s, q, _, b=b: (b, q)) for b in range(seqs) for _ in ys],
        [pl.BlockSpec((pair, 1, tall // 2, 2 * depth), lambda s, q, _: (s, q, 0, 0))] * 2,
        [shape] * 2,
        2 * rows * width * shards * tall,
        rows * width * 6 + width * shards * tall * 2,
        [pltpu.VMEM((pair * tall, rows), bf16)],
    deps=deps,
        )(spot, *xs, *(list(ys) * seqs))


def finish_mixed(spot, residual, blocks, deps=()):
    rows, width = residual.shape
    tall = min(128, rows)

    def body(spot, r_ref, *refs):
        total = r_ref[...]
        for ref in refs[:-1]:
            total += ref[...].astype(f32)
        refs[-1][...] = total.astype(bf16)

    tile = pl.BlockSpec((tall, width), lambda m, _: (m, 0))
    return grid_call(
        body,
        (rows // tall,),
        [tile] * (1 + len(blocks)),
        tile,
        jax.ShapeDtypeStruct((rows, width), bf16),
        rows * width * 5,
        rows * width * 14,
        deps=deps,
    )(spot, residual, *blocks)


def hop(a, bits):
    n = lax.axis_size("dp")
    return lax.ppermute(a, "dp", [(i, i ^ bits) for i in range(n)])


def added(a, b):
    return (a.astype(f32) + b.astype(f32)).astype(a.dtype)


def plane_gather(a):
    return [a] + [hop(a, 2 * r) for r in range(1, PLANE)]


def plane_trade(blocks):
    return [blocks[0]] + [hop(blocks[r], 2 * r) for r in range(1, PLANE)]


def total_of(blocks):
    total = blocks[0].astype(f32)
    for b in blocks[1:]:
        total += b.astype(f32)
    return total


def plane_scatter(blocks):
    return total_of(plane_trade(blocks))


def shift(a, step):
    n = lax.axis_size("tensor")
    return lax.ppermute(a, "tensor", [(i, (i + step) % n) for i in range(n)])


def line_gather(a):
    return [a] + [shift(a, s) for s in range(1, lax.axis_size("tensor"))]


def line_scatter(blocks):
    n, place = lax.axis_size("tensor"), lax.axis_index("tensor")
    total = lax.dynamic_index_in_dim(blocks, place, 0, keepdims=False).astype(f32)
    for step in range(1, n):
        mine = lax.dynamic_index_in_dim(blocks, lax.rem(place + step, n), 0, keepdims=False)
        total += shift(mine, step).astype(f32)
    return total


def after(a, *others):
    others = jax.tree.leaves(others)
    place = pl.BlockSpec(memory_space=pl.ANY)
    return pl.pallas_call(
        lambda *refs: None,
        in_specs=[place] * (1 + len(others)),
        out_specs=place,
        out_shape=jax.ShapeDtypeStruct(a.shape, a.dtype),
        input_output_aliases={0: 0},
        cost_estimate=pl.CostEstimate(flops=1, bytes_accessed=1, transcendentals=0),
    )(a, *others)


def token(*arrays, steps=2):
    arrays = jax.tree.leaves(arrays)
    place = pl.BlockSpec(memory_space=pl.ANY)

    def body(*refs):
        refs[-1][...] = jnp.zeros_like(refs[-1])

    for _ in range(steps):
        arrays = [
            pl.pallas_call(
                body,
                in_specs=[place] * len(arrays),
                out_specs=pl.BlockSpec(memory_space=pltpu.VMEM),
                out_shape=jax.ShapeDtypeStruct((8, LANES), f32),
            )(*arrays)
        ]
    return arrays[0]


def by_chip(parts, chip):
    a, b, c, d = parts
    odd = (chip & 1) == 1
    a, b, c, d = (
        jnp.where(odd, b, a),
        jnp.where(odd, a, b),
        jnp.where(odd, d, c),
        jnp.where(odd, c, d),
    )
    high = (chip & 2) == 2
    return (
        jnp.where(high, c, a),
        jnp.where(high, d, b),
        jnp.where(high, a, c),
        jnp.where(high, b, d),
    )


def trade(pieces, axis, chip, hold=lambda a: a):
    come = []
    for r in range(PLANE):
        piece = lax.dynamic_index_in_dim(pieces, chip ^ r, axis, keepdims=False)
        come.append(hold(piece) if r == 0 else hop(piece, 2 * r))
    return by_chip(come, chip)


def core_sum(pair, *others):
    return added(after(pair[0], others) if others else pair[0], hop(pair[1], 1))


def plane_sum(blocks, chip):
    mine = [lax.dynamic_index_in_dim(blocks, chip ^ r, 0, keepdims=False) for r in range(PLANE)]
    return plane_scatter(mine).astype(bf16)


def rotary_tables(positions):
    half_size = HD // 2
    frequency = THETA ** (-2.0 * jnp.arange(half_size, dtype=f32) / HD)
    angles = positions.astype(f32)[:, None] * frequency[None, :]
    cos, sin = jnp.cos(angles), jnp.sin(angles)
    return (
        jnp.concatenate([cos, cos] * (LANES // HD), -1),
        jnp.concatenate([-sin, sin] * (LANES // HD), -1),
    )


def shards(
    tokens, segments, attn_norm, w_query, w_key, w_value, w_out, mlp_norm, w_gate, w_up, w_down, cotangent
):
    dp_count, tp_count = lax.axis_size("dp"), lax.axis_size("tensor")
    groups = dp_count // 8
    place = lax.axis_index("tensor")
    index = lax.axis_index("dp")
    core, chip = index & 1, (index >> 1) & 3
    seqs, span, width = tokens.shape
    rows = seqs * span
    block = width // 8

    group_sets = [[g * 8 + l for g in range(groups)] for l in range(8)]

    def widen(a, axis):
        if groups == 1:
            return a
        return lax.all_gather(a, "dp", axis=axis, tiled=True, axis_index_groups=group_sets)

    def narrow(a, axis):
        if groups == 1:
            return a
        return lax.psum_scatter(
            a.astype(bf16), "dp", scatter_dimension=axis, tiled=True, axis_index_groups=group_sets
        )

    def inward(a):
        if groups == 1:
            return a
        lead = a.shape[:-1]
        return jnp.swapaxes(a.reshape(lead + (groups, 8, -1)), -3, -2).reshape(lead + (-1,))

    def outward(a):
        if groups == 1:
            return a
        lead = a.shape[:-1]
        return jnp.swapaxes(a.reshape(lead + (8, groups, -1)), -3, -2).reshape(lead + (-1,))

    eight = [[g * 8 + l for l in range(8)] for g in range(groups)]

    def along(a):
        return lax.all_gather(a, "tensor", axis=0, tiled=False)

    def in_plane(a):
        if groups == 1:
            return lax.all_gather(a, "dp", axis=0, tiled=False)
        return lax.all_gather(a, "dp", axis=0, tiled=False, axis_index_groups=eight)

    tokens = inward(tokens).reshape(rows, width)
    cotangent = inward(cotangent).reshape(rows, width)
    attn_norm, mlp_norm = widen(attn_norm, 0), widen(mlp_norm, 0)
    w_query, w_key, w_value = widen(w_query, 0), widen(w_key, 0), widen(w_value, 0)
    w_gate, w_up = widen(w_gate, 0), widen(w_up, 0)
    w_out, w_down = widen(w_out, 1), widen(w_down, 1)

    kv_cols = 2 * w_key.shape[1]
    kv_group = w_query.shape[1] // w_key.shape[1]
    gains = jnp.concatenate(
        [
            jnp.pad(attn_norm, (0, kv_cols - block))[None],
            jnp.pad(mlp_norm, (0, kv_cols - block))[None],
            jnp.zeros((14, kv_cols), bf16),
        ],
        0,
    )
    near_kv = line_gather(jnp.concatenate([jnp.concatenate([w_key, w_value], 1), gains], 0))
    lines = w_down.reshape(PLANE, 2, -1, block)
    pieces = jnp.stack(
        [
            jnp.swapaxes(w_gate.reshape(block, PLANE, -1), 0, 1),
            jnp.swapaxes(w_up.reshape(block, PLANE, -1), 0, 1),
            jnp.concatenate([lines[:, 0], lines[:, 1]], 2),
        ],
        1,
    )
    all_kv = in_plane(jnp.stack(near_kv, 0))
    gain_one = all_kv[:, 0, block, :block].reshape(width).astype(f32)
    gain_two = all_kv[:, 0, block + 1, :block].reshape(width).astype(f32)
    lined = line_gather(after(jnp.stack([w_query, folded(w_out)], 0), near_kv[1:]))
    lined_q, lined_out = (jnp.stack([a[n] for a in lined], 0) for n in range(2))
    chunks = [slice(b * span, (b + 1) * span) for b in range(seqs)]

    spot = jnp.stack([place, core, chip]).astype(jnp.int32)
    cos, sin = rotary_tables(place * span + jnp.arange(span, dtype=jnp.int32))
    cos_rows, sin_rows = jnp.tile(cos, (seqs, 1)), jnp.tile(sin, (seqs, 1))
    x = tokens.astype(f32)
    norm_one = lax.rsqrt(jnp.mean(x * x, -1, keepdims=True) + EPS)
    scaled_one = (x * norm_one).astype(bf16)
    normed_one = (scaled_one.astype(f32) * gain_one).astype(bf16)
    pair = project_pairs(spot, normed_one, all_kv, cos_rows, sin_rows, block, deps=lined[1:])
    pairs = along(pair)
    def both_cores(blocks, *others):
        if others:
            blocks = [after(b, others) for b in blocks]
        return blocks + [hop(b, 1) for b in blocks]

    all_q = plane_gather(after(lined_q, pair))
    sent = after(pieces, all_q[1:])
    all_q = both_cores(all_q)
    queries = project_queries(spot, normed_one, all_q, cos_rows, sin_rows)
    near = jnp.stack(trade(sent, 0, chip, lambda own: after(own, queries)), 1)
    tall = near.shape[1] * near.shape[2]
    own_gate, own_up = (along(after(near[n].reshape(tall, -1), pair)) for n in range(2))
    all_out = plane_gather(after(lined_out, all_q[1:], near))

    seg_blocks = segments.reshape(seqs, tp_count, span)
    own_seg = lax.dynamic_index_in_dim(seg_blocks, place, 1, keepdims=False)
    here = jnp.arange(span, dtype=jnp.int32)
    bias = []
    for j in range(tp_count):
        key_seg = lax.dynamic_index_in_dim(seg_blocks, jnp.maximum(place - j, 0), 1, keepdims=False)
        allowed = key_seg[:, :, None] == own_seg[:, None, :]
        if j == 0:
            allowed &= here[None, :, None] <= here[None, None, :]
        bias.append(jnp.where(allowed, 0.0, -1e30).astype(f32))
    bias = jnp.concatenate(bias, 1)
    heads_out, lse = attend(spot, queries, pairs, bias, span, kv_group)
    all_out = both_cores(all_out, heads_out)
    residual = project_out(spot, heads_out, all_out, tokens)

    norm_two = lax.rsqrt(jnp.mean(residual * residual, -1, keepdims=True) + EPS)
    scaled_two = (residual * norm_two).astype(bf16)
    normed_two = (scaled_two.astype(f32) * gain_two).astype(bf16)
    full_two = []
    for c in chunks:
        full_two.append(plane_gather(after(normed_two[c], full_two[-1][1:]) if full_two else normed_two[c]))
    cot_full = plane_gather(after(cotangent, full_two[-1][1:]))
    own_gate, own_up = after(own_gate, full_two[0][1:]), after(own_up, full_two[-1][1:])
    own_in = (own_gate, own_up)
    other_in = (hop(own_gate, 1), hop(own_up, 1))
    own_down = along(after(near[2], residual))
    tokens_two = sum(full_two, [])
    gate, up, inner = gate_up(spot, tokens_two, own_in, other_in)
    other_down = hop(own_down, 1)

    def line_sum(a):
        return lax.psum_scatter(a, "tensor", scatter_dimension=0, tiled=False)

    down_parts = row_weight_grad(spot, [inner], cot_full, span, tp_count)
    d_gate, d_up, from_plane, deps = [], [], [], down_parts
    for n in range(seqs):
        weights = (own_down, other_down, gate, up, own_in, other_in)
        dg, du, to_plane = backward_chunk(spot, n, span, cot_full, *weights, deps=deps)
        d_gate.append(dg)
        d_up.append(du)
        deps = to_plane
        from_plane.append(plane_trade(list(to_plane)))
    down_pair = core_sum(down_parts, d_gate[0])
    down_sum = line_sum(down_pair)
    deps = [down_pair, to_plane, [f[1:] for f in from_plane[:-1]]]
    gate_parts, up_parts = column_weight_grads(spot, tokens_two, [d_gate, d_up], tp_count, deps=deps)
    grad_residual, grad_low, gain_two_terms = residual_grads(
        spot, from_plane, residual, cotangent, gain_two[None], deps=[up_parts[0], down_sum]
    )
    gain_two_terms = gain_two_terms[0]
    gate_parts, up_parts = ((p[0], after(p[1], grad_low)) for p in (gate_parts, up_parts))
    shares = down(spot, inner, own_down, other_down, seqs, deps=grad_low)
    gate_pair, up_pair = core_sum(gate_parts, shares[0]), core_sum(up_parts, shares[0])
    gate_sum = line_sum(gate_pair)
    mixed = plane_trade(list(shares))

    out_parts = out_blocks_grad(spot, heads_out, grad_low, tp_count)
    grad_heads = unproject_out(spot, grad_low, all_out, deps=[up_parts[0], out_parts])
    deps = [out_parts, up_pair, gate_pair]
    dq, dkv = unattend(spot, queries, grad_heads, pairs, bias, lse, cos, sin, span, kv_group, deps=deps)
    gate_here = token(dq, mixed[1:], gate_sum, steps=1)
    dkv = line_sum(after(dkv, gate_here))
    up_sum = line_sum(up_pair)
    out_near = plane_sum(core_sum((out_parts[0], after(out_parts[1], gate_here))), chip)
    query_parts = in_blocks_grad(spot, normed_one, dq, None, None, tp_count, deps=gate_here)
    grad_out = unfolded(line_scatter(after(out_near, dkv)))
    query_near = plane_sum(core_sum(query_parts), chip)
    grad_query = line_scatter(after(query_near, dkv))
    mixed = finish_mixed(spot, residual, mixed, deps=query_parts)
    come = trade(after(jnp.stack([down_sum, gate_sum, up_sum], 1), out_near, query_near), 0, chip)
    grad_down = jnp.concatenate([jnp.concatenate([c[0, :, :block], c[0, :, block:]], 0) for c in come], 0)
    grad_gate, grad_up = (jnp.concatenate([c[n] for c in come], 1) for n in (1, 2))

    dkv = finish_pairs(spot, dkv, cos_rows, sin_rows, deps=[out_near, query_near])
    grad_normed_one = unproject_in(spot, dq, dkv, all_q, all_kv)
    gain_one_terms = jnp.sum(scaled_one.astype(f32) * grad_normed_one, 0)
    gain_terms = jnp.stack([gain_one_terms.reshape(8, block), gain_two_terms.reshape(8, block)], 1)
    gain_terms = jnp.pad(gain_terms, ((0, 0), (0, 14), (0, kv_cols - block)))
    kv_parts = in_blocks_grad(spot, normed_one, dq, dkv, gain_terms, tp_count)
    kv_sum = line_scatter(plane_sum(core_sum(kv_parts), chip))
    grad_tokens = grad_residual + norm_backward(grad_normed_one * gain_one, x * norm_one, norm_one)
    grad_tokens = grad_tokens.astype(bf16)
    def gain_share(line):
        line = narrow(line, 0)
        share = line.shape[0] // tp_count
        return lax.dynamic_slice_in_dim(line, place * share, share, 0).astype(f32)

    half = kv_cols // 2
    return (
        outward(mixed).reshape(seqs, span, width),
        outward(grad_tokens).reshape(seqs, span, width),
        gain_share(kv_sum[block, :block]),
        narrow(grad_query, 0).astype(f32),
        narrow(kv_sum[:block, :half], 0).astype(f32),
        narrow(kv_sum[:block, half:], 0).astype(f32),
        narrow(grad_out, 1).astype(f32),
        gain_share(kv_sum[block + 1, :block]),
        narrow(grad_gate, 0).astype(f32),
        narrow(grad_up, 0).astype(f32),
        narrow(grad_down, 1).astype(f32),
    )


def solution(mesh):
    placed = (
        P("dp", "tensor", None),
        P("dp", None),
        P("dp"),
        P("dp", "tensor"),
        P("dp", "tensor"),
        P("dp", "tensor"),
        P("tensor", "dp"),
        P("dp"),
        P("dp", "tensor"),
        P("dp", "tensor"),
        P("tensor", "dp"),
        P("dp", "tensor", None),
    )
    return jax.shard_map(
        shards,
        mesh=mesh,
        in_specs=placed,
        out_specs=(
            P("dp", "tensor", None),
            P("dp", "tensor", None),
            P(("dp", "tensor")),
            P("dp", "tensor"),
            P("dp", "tensor"),
            P("dp", "tensor"),
            P("tensor", "dp"),
            P(("dp", "tensor")),
            P("dp", "tensor"),
            P("dp", "tensor"),
            P("tensor", "dp"),
        ),
        check_vma=False,
    )
```

```python
import functools

import jax
import jax.numpy as jnp
from jax import lax
from jax.experimental import pallas as pl
from jax.experimental.pallas import tpu as pltpu
from jax.sharding import PartitionSpec as P

HD = 64
EPS = 1e-05
THETA = 500000.0
LOG2E = 1.4426950408889634
LANES = 128
PLANE = 4
f32 = jnp.float32
bf16 = jnp.bfloat16


def call(body, flops, moved, vmem=50, **kw):
    return pl.pallas_call(
        body,
        compiler_params=pltpu.CompilerParams(vmem_limit_bytes=vmem * 2**20),
        cost_estimate=pl.CostEstimate(flops=flops, bytes_accessed=moved, transcendentals=0),
        **kw,
    )


def nn(a, b):
    return jnp.dot(a, b, preferred_element_type=f32)


def nt(a, b):
    return lax.dot_general(a, b, (((1,), (1,)), ((), ())), preferred_element_type=f32)


def tn(a, b):
    return lax.dot_general(a, b, (((0,), (0,)), ((), ())), preferred_element_type=f32)


def swap_halves(x):
    lane = lax.broadcasted_iota(jnp.int32, x.shape, 1)
    return jnp.where(lane % HD < HD // 2, pltpu.roll(x, LANES - HD // 2, 1), pltpu.roll(x, HD // 2, 1))


def gather_keys(k_refs, v_refs, blocks):
    k = jnp.concatenate([k_refs[j][0, 0] for j in range(blocks)], 0)
    v = jnp.concatenate([v_refs[j][0, 0] for j in range(blocks)], 0)
    return k, v


def padded_rows(part, e):
    zero = jnp.zeros_like(part)
    return jnp.concatenate([part, zero] if e == 0 else [zero, part], 0)


def attend_blocks(blocks, group, q_ref, k_refs, v_refs, bias_ref, o_ref, lse_ref, qt_ref, ot_ref):
    span = q_ref.shape[0]
    n = blocks * span
    k, v = gather_keys(k_refs, v_refs, blocks)
    vt = v.T
    qt_ref[...] = q_ref[...].T
    factor = HD**-0.5 * LOG2E

    def step(i, carry):
        for e in range(2):
            head = e * group + i
            rows = pl.ds(pl.multiple_of(head * HD, HD), HD)
            scores = nn(k, padded_rows(qt_ref[rows, :], e))
            logits = scores * factor + bias_ref[0, :n, :]
            top = jnp.max(logits, 0, keepdims=True)
            weights = jnp.exp2(logits - top)
            total = jnp.sum(weights, 0, keepdims=True)
            out = nn(vt[e * HD : (e + 1) * HD], weights.astype(bf16))
            ot_ref[rows, :] = out * (1.0 / total)
            lse_ref[0, 0, pl.ds(head, 1), :] = top + jnp.log2(total)
        return carry

    lax.fori_loop(0, group, step, 0)
    o_ref[...] = ot_ref[...].T.astype(bf16)


def attend_kernel(count, group, place, *refs):
    q_ref, k_refs, v_refs = refs[0], refs[1 : 1 + count], refs[1 + count : 1 + 2 * count]
    rest = refs[1 + 2 * count :]
    for blocks in range(1, count + 1):

        @pl.when(place[0] == blocks - 1)
        def _(blocks=blocks):
            attend_blocks(blocks, group, q_ref, k_refs, v_refs, *rest)


def key_specs(count, span):
    return [
        pl.BlockSpec(
            (1, 1, span, LANES), lambda b, p, s, part=part, j=j: (jnp.maximum(s[0] - j, 0), part, b, p)
        )
        for part in range(2)
        for j in range(count)
    ]


def attend(place, queries, pairs, bias, span, group):
    rows, width = queries.shape
    count = pairs.shape[0]
    seqs = rows // span
    kv_width = pairs.shape[3]
    tiles = kv_width // LANES
    wide = width // tiles
    in_specs = [pl.BlockSpec((span, wide), lambda b, p, s: (b, p))] + key_specs(count, span)
    in_specs.append(pl.BlockSpec((1, count * span, span), lambda b, p, s: (b, 0, 0)))
    heads = wide // HD
    spec = pltpu.PrefetchScalarGridSpec(
        num_scalar_prefetch=1,
        grid=(seqs, tiles),
        in_specs=in_specs,
        out_specs=[
            pl.BlockSpec((span, wide), lambda b, p, s: (b, p)),
            pl.BlockSpec((1, 1, heads, span), lambda b, p, s: (b, p, 0, 0)),
        ],
        scratch_shapes=[pltpu.VMEM((wide, span), bf16), pltpu.VMEM((wide, span), f32)],
    )
    return call(
        functools.partial(attend_kernel, count, group),
        flops=rows * width * span * count * 8,
        moved=rows * width * 4,
        grid_spec=spec,
        out_shape=[
            jax.ShapeDtypeStruct((rows, width), bf16),
            jax.ShapeDtypeStruct((seqs, tiles, heads, span), f32),
        ],
    )(place, queries, *([pairs] * (2 * count)), bias)


def unattend_blocks(
    blocks, count, group, q_ref, g_ref, k_refs, v_refs, bias_ref, lse_ref, cos_ref, sin_ref,
    dq_ref, dkv_ref, qt_ref, gt_ref, dqt_ref, dk_ref, dv_ref,
):
    span = q_ref.shape[0]
    n = blocks * span
    k, v = gather_keys(k_refs, v_refs, blocks)
    kt = k.T
    qt_ref[...] = q_ref[...].T
    gt_ref[...] = g_ref[...].T
    dk_ref[...] = jnp.zeros_like(dk_ref)
    dv_ref[...] = jnp.zeros_like(dv_ref)
    factor = HD**-0.5 * LOG2E
    lane = lax.broadcasted_iota(jnp.int32, (span, LANES), 1)

    def moved(tile, b, e):
        if b != e:
            tile = pltpu.roll(tile, HD, 1)
        return jnp.where((lane < HD) if e == 0 else (lane >= HD), tile, 0.0).astype(bf16)

    def step(i, carry):
        for e in range(2):
            tile_at = pl.ds(pl.multiple_of((e * (group // 2) + i) * LANES, LANES), LANES)
            q_tile = q_ref[:, tile_at].astype(f32)
            g_tile = g_ref[:, tile_at].astype(f32)
            all_ds, all_p = [], []
            for b in range(2):
                head = e * group + 2 * i + b
                rows = pl.ds(pl.multiple_of(head * HD, HD), HD)
                scores = nn(k, padded_rows(qt_ref[rows, :], e))
                lse = lse_ref[0, 0, pl.ds(head, 1), :]
                probs = jnp.exp2(scores * factor + bias_ref[0, :n, :] - lse)
                dp = nn(v, padded_rows(gt_ref[rows, :], e))
                delta = jnp.sum(probs * dp, 0, keepdims=True)
                ds = (probs * (dp - delta)).astype(bf16)
                dqt_ref[rows, :] = nn(kt[e * HD : (e + 1) * HD], ds)
                all_ds.append(ds)
                all_p.append(probs.astype(bf16))
            q_rows = jnp.concatenate([moved(q_tile, b, e) for b in range(2)], 0)
            g_rows = jnp.concatenate([moved(g_tile, b, e) for b in range(2)], 0)
            dk_ref[:n, :] += nn(jnp.concatenate(all_ds, 1), q_rows)
            dv_ref[:n, :] += nn(jnp.concatenate(all_p, 1), g_rows)
        return carry

    lax.fori_loop(0, group // 2, step, 0)
    scale = HD**-0.5
    dq = dqt_ref[...].T * scale
    for t in range(dq.shape[1] // LANES):
        part = dq[:, t * LANES : (t + 1) * LANES]
        dq_ref[:, t * LANES : (t + 1) * LANES] = (
            part * cos_ref[...] - swap_halves(part) * sin_ref[...]
        ).astype(bf16)
    for n in range(count):
        j = blocks - 1 - n if n < blocks else n
        dkv_ref[n, 0] = (dk_ref[j * span : (j + 1) * span, :] * scale).astype(bf16)
        dkv_ref[n, 1] = dv_ref[j * span : (j + 1) * span, :].astype(bf16)


def unattend_kernel(count, group, skip, place, *refs):
    refs = refs[skip:]
    q_ref, g_ref, k_refs, v_refs = refs[0], refs[1], refs[2 : 2 + count], refs[2 + count : 2 + 2 * count]
    rest = refs[2 + 2 * count :]
    for blocks in range(1, count + 1):

        @pl.when(place[0] == blocks - 1)
        def _(blocks=blocks):
            unattend_blocks(blocks, count, group, q_ref, g_ref, k_refs, v_refs, *rest)


def unattend(place, queries, grads, pairs, bias, lse, cos, sin, span, group, deps=()):
    rows, width = queries.shape
    count = pairs.shape[0]
    seqs = rows // span
    kv_width = pairs.shape[3]
    tiles = kv_width // LANES
    wide = width // tiles
    heads = wide // HD
    tall = pl.BlockSpec((span, wide), lambda b, p, s: (b, p))
    table = pl.BlockSpec((span, LANES), lambda b, p, s: (0, 0))
    deps = jax.tree.leaves(deps)
    in_specs = [pl.BlockSpec(memory_space=pl.ANY)] * len(deps) + [tall, tall] + key_specs(count, span)
    in_specs += [
        pl.BlockSpec((1, count * span, span), lambda b, p, s: (b, 0, 0)),
        pl.BlockSpec((1, 1, heads, span), lambda b, p, s: (b, p, 0, 0)),
        table,
        table,
    ]
    spec = pltpu.PrefetchScalarGridSpec(
        num_scalar_prefetch=1,
        grid=(seqs, tiles),
        in_specs=in_specs,
        out_specs=[tall, pl.BlockSpec((count, 2, span, LANES), lambda b, p, s: (0, 0, b, p))],
        scratch_shapes=[
            pltpu.VMEM((wide, span), bf16),
            pltpu.VMEM((wide, span), bf16),
            pltpu.VMEM((wide, span), f32),
            pltpu.VMEM((count * span, LANES), f32),
            pltpu.VMEM((count * span, LANES), f32),
        ],
    )
    return call(
        functools.partial(unattend_kernel, count, group, len(deps)),
        flops=rows * width * span * count * 20,
        moved=rows * width * 8,
        grid_spec=spec,
        out_shape=[
            jax.ShapeDtypeStruct((rows, width), bf16),
            jax.ShapeDtypeStruct((count, 2, rows, kv_width), bf16),
        ],
    )(place, *deps, queries, grads, *([pairs] * (2 * count)), bias, lse, cos, sin)


def turn(y, cos, sin, out_ref, start=0):
    for t in range(y.shape[1] // LANES):
        part = y[:, t * LANES : (t + 1) * LANES]
        out_ref[:, t * LANES : (t + 1) * LANES] = (part * cos + swap_halves(part) * sin).astype(bf16)


def block_home(spot, half, r):
    core = spot[1] if half == 0 else 1 - spot[1]
    return 2 * (spot[2] ^ r) + core


def lanes_at(ref, at, size):
    return ref[:, pl.ds(pl.multiple_of(at * size, size), size)]


def by_block(ref, spot, size):
    return jnp.concatenate(
        [lanes_at(ref, block_home(spot, half, r), size) for half in range(2) for r in range(PLANE)], 1
    )


def by_slot(ref, spot, shards, size):
    return jnp.concatenate([lanes_at(ref, slot_home(spot, s, shards), size) for s in range(shards)], 1)


def slot_home(spot, s, shards):
    return lax.rem(spot[0] + shards - s, shards)


def grid_call(body, grid, in_specs, out_specs, out_shape, flops, moved, scratch=(), deps=()):
    deps = jax.tree.leaves(deps)

    def late(spot, *refs):
        body(spot, *refs[len(deps) :])

    run = call(
        late,
        flops=flops,
        moved=moved,
        grid_spec=pltpu.PrefetchScalarGridSpec(
            num_scalar_prefetch=1,
            grid=grid,
            in_specs=[pl.BlockSpec(memory_space=pl.ANY)] * len(deps) + list(in_specs),
            out_specs=out_specs,
            scratch_shapes=list(scratch),
        ),
        out_shape=out_shape,
    )
    return lambda spot, *arrays: run(spot, *deps, *arrays)


def project_pairs(spot, normed, weights, cos, sin, depth, deps=()):
    rows, width = normed.shape
    parts, shards, _, cols = weights.shape
    half = cols // 2

    def body(spot, x_ref, w_ref, cos_ref, sin_ref, o_ref):
        w = w_ref[:, 0, :depth, :].reshape(parts * depth, cols)
        y = nn(x_ref[...], w)
        k = y[:, :half]
        o_ref[0] = (k * cos_ref[...] + swap_halves(k) * sin_ref[...]).astype(bf16)
        o_ref[1] = y[:, half:].astype(bf16)

    whole = lambda s, _: (0, 0)
    return grid_call(
        body,
        (shards,),
        [
            pl.BlockSpec((rows, width), whole),
            pl.BlockSpec((parts, 1, weights.shape[2], cols), lambda s, _: (0, s, 0, 0)),
            pl.BlockSpec((rows, LANES), whole),
            pl.BlockSpec((rows, LANES), whole),
        ],
        pl.BlockSpec((2, rows, half), lambda s, spot: (0, 0, slot_home(spot, s, shards))),
        jax.ShapeDtypeStruct((2, rows, half * shards), bf16),
        2 * rows * width * shards * cols,
        weights.size * 2 + normed.size * 2,
        deps=deps,
    )(spot, normed, weights, cos, sin)


def project_queries(spot, normed, weights, cos, sin):
    rows, width = normed.shape
    shards, depth, cols = weights[0].shape
    count = len(weights)

    def body(spot, *refs):
        x_ref, w_refs, cos_ref, sin_ref, o_ref, xs_ref = refs[0], refs[1 : 1 + count], *refs[1 + count :]

        @pl.when(pl.program_id(0) == 0)
        def _():
            xs_ref[...] = by_block(x_ref, spot, depth)

        y = nn(xs_ref[...], jnp.concatenate([w[0] for w in w_refs], 0))
        turn(y, cos_ref[...], sin_ref[...], o_ref)

    whole = lambda s, _: (0, 0)
    return grid_call(
        body,
        (shards,),
        [pl.BlockSpec((rows, width), whole)]
        + [pl.BlockSpec((1, depth, cols), lambda s, _: (s, 0, 0))] * count
        + [pl.BlockSpec((rows, LANES), whole)] * 2,
        pl.BlockSpec((rows, cols), lambda s, spot: (0, slot_home(spot, s, shards))),
        jax.ShapeDtypeStruct((rows, cols * shards), bf16),
        2 * rows * width * shards * cols,
        width * shards * cols * 2 + normed.size * 4,
        [pltpu.VMEM((rows, width), bf16)],
    )(spot, normed, *weights, cos, sin)


def folded(w):
    half = w.shape[0] // 2
    return jnp.concatenate([w[:half], w[half:]], 1)


def unfolded(w):
    half = w.shape[1] // 2
    return jnp.concatenate([w[:, :half], w[:, half:]], 0)


def project_out(spot, heads_out, weights, tokens, deps=()):
    rows, width = heads_out.shape
    shards, depth, cols = weights[0].shape
    depth, cols = 2 * depth, cols // 2
    count = len(weights)
    tall = min(256, rows)

    def body(spot, *refs):
        x_ref, w_refs, t_ref, o_ref = refs[0], refs[1 : 1 + count], *refs[1 + count :]
        x = by_slot(x_ref, spot, shards, depth)
        for n, w_ref in enumerate(w_refs):
            at = block_home(spot, n // PLANE, n % PLANE)
            y = nn(x, jnp.concatenate([unfolded(w_ref[s]) for s in range(shards)], 0))
            o_ref[:, pl.ds(pl.multiple_of(at * cols, cols), cols)] = lanes_at(t_ref, at, cols).astype(f32) + y

    tile = pl.BlockSpec((tall, width), lambda m, _: (m, 0))
    return grid_call(
        body,
        (rows // tall,),
        [tile] + [pl.BlockSpec(w.shape, lambda m, _: (0, 0, 0)) for w in weights] + [tile],
        tile,
        jax.ShapeDtypeStruct((rows, cols * count), f32),
        2 * rows * width * count * cols,
        width * cols * count * 2 + rows * width * 8,
        deps=deps,
    )(spot, heads_out, *weights, tokens)


def unproject_out(spot, grads, weights, deps=()):
    rows, width = grads.shape
    shards, depth, cols = weights[0].shape
    depth, cols = 2 * depth, cols // 2
    count = len(weights)

    def body(spot, *refs):
        x_ref, w_refs, o_ref, xs_ref = refs[0], refs[1 : 1 + count], *refs[1 + count :]

        @pl.when(pl.program_id(0) == 0)
        def _():
            xs_ref[...] = by_block(x_ref, spot, cols)

        w = jnp.concatenate([unfolded(w_ref[0]) for w_ref in w_refs], 1)
        o_ref[...] = nt(xs_ref[...], w).astype(bf16)

    return grid_call(
        body,
        (shards,),
        [pl.BlockSpec((rows, width), lambda s, _: (0, 0))]
        + [pl.BlockSpec((1, depth // 2, 2 * cols), lambda s, _: (s, 0, 0))] * count,
        pl.BlockSpec((rows, depth), lambda s, spot: (0, slot_home(spot, s, shards))),
        jax.ShapeDtypeStruct((rows, depth * shards), bf16),
        2 * rows * width * shards * depth,
        width * shards * depth * 2 + rows * width * 6,
        [pltpu.VMEM((rows, width), bf16)],
        deps=deps,
    )(spot, grads, *weights)


def still(shape, index):
    return pl.BlockSpec(shape, index, pipeline_mode=pl.Buffered(1))


def unproject_queries(spot, dq, w_q, deps=()):
    rows, width = dq.shape
    shards, depth, cols = w_q[0].shape
    count = len(w_q)
    tall = min(256, rows)

    def body(spot, q_ref, *refs):
        left = by_slot(q_ref, spot, shards, cols)
        for n, w_ref in enumerate(refs[:-1]):
            at = block_home(spot, n // PLANE, n % PLANE)
            y = nt(left, jnp.concatenate([w_ref[s] for s in range(shards)], 1))
            refs[-1][:, pl.ds(pl.multiple_of(at * depth, depth), depth)] = y

    tile = pl.BlockSpec((tall, width), lambda m, _: (m, 0))
    return grid_call(
        body,
        (rows // tall,),
        [tile] + [still(w.shape, lambda m, _: (0, 0, 0)) for w in w_q],
        pl.BlockSpec((tall, count * depth), lambda m, _: (m, 0)),
        jax.ShapeDtypeStruct((rows, count * depth), f32),
        2 * rows * count * depth * shards * cols,
        count * depth * shards * cols * 2 + rows * width * 6,
        deps=deps,
    )(spot, dq, *w_q)


def unproject_pairs(spot, partial, dkv, w_kv, scaled, deps=()):
    rows, width = partial.shape
    parts, shards, _, cols = w_kv.shape
    depth, thin = width // parts, cols // 2
    tall = min(256, rows)

    def body(spot, p_ref, kv_ref, w_ref, s_ref, o_ref, sum_ref):
        @pl.when(pl.program_id(0) == 0)
        def _():
            sum_ref[...] = jnp.zeros_like(sum_ref)

        left = jnp.concatenate(
            [
                kv_ref[n, :, pl.ds(pl.multiple_of(slot_home(spot, s, shards) * thin, thin), thin)]
                for s in range(shards)
                for n in range(2)
            ],
            1,
        )
        for i in range(parts):
            here = slice(i * depth, (i + 1) * depth)
            total = nt(left, jnp.concatenate([w_ref[i, s, :depth, :] for s in range(shards)], 1))
            total += p_ref[:, here]
            o_ref[:, here] = total
            sum_ref[0:1, here] += jnp.sum(s_ref[:, here].astype(f32) * total, 0, keepdims=True)

    tile = pl.BlockSpec((tall, width), lambda m, _: (m, 0))
    return grid_call(
        body,
        (rows // tall,),
        [
            tile,
            pl.BlockSpec((2, tall, dkv.shape[2]), lambda m, _: (0, m, 0)),
            still(w_kv.shape, lambda m, _: (0, 0, 0, 0)),
            tile,
        ],
        [tile, pl.BlockSpec((8, width), lambda m, _: (0, 0))],
        [jax.ShapeDtypeStruct((rows, width), f32), jax.ShapeDtypeStruct((8, width), f32)],
        2 * rows * width * shards * cols,
        w_kv.size * 2 + rows * width * 12,
        deps=deps,
    )(spot, partial, dkv, w_kv, scaled)


def of_core(ref, core, depth):
    return ref[:, pl.ds(pl.multiple_of(core * depth, depth), depth)]


def in_blocks_grad(spot, normed, dq, dkv, gains, shards, deps=()):
    rows, width = normed.shape
    depth = width // PLANE // 2
    y = dq if dkv is None else dkv
    cols = (dq.shape[1] if dkv is None else 2 * dkv.shape[2]) // shards
    extra = 0 if gains is None else gains.shape[1]

    def body(spot, x_ref, y_ref, *refs):
        for n, core in ((0, spot[1]), (1, 1 - spot[1])):
            x, o_ref = of_core(x_ref, core, depth), refs[-2 + n]
            totals = [tn(x, y_ref[...])] if dkv is None else [tn(x, y_ref[0]), tn(x, y_ref[1])]
            thin = cols // len(totals)
            for s in range(shards):
                for m, total in enumerate(totals):
                    o_ref[0, s, :depth, m * thin : (m + 1) * thin] = total[:, s * thin : (s + 1) * thin].astype(bf16)
                if extra:
                    o_ref[0, s, depth:, :] = refs[0][core].astype(bf16)

    whole = pl.BlockSpec(y.shape, (lambda q, _: (0, 0)) if dkv is None else (lambda q, _: (0, 0, 0)))
    more = [] if gains is None else [pl.BlockSpec((2, extra, gains.shape[2]), lambda q, _: (q, 0, 0))]
    shape = jax.ShapeDtypeStruct((PLANE, shards, depth + extra, cols), bf16)
    return grid_call(
        body,
        (PLANE,),
        [pl.BlockSpec((rows, 2 * depth), lambda q, _: (0, q)), whole] + more,
        [pl.BlockSpec((1, shards, depth + extra, cols), lambda q, _: (q, 0, 0, 0))] * 2,
        [shape] * 2,
        2 * rows * width * shards * cols,
        rows * width * 4 + width * shards * cols * 2,
    deps=deps,
        )(spot, normed, y, *([] if gains is None else [gains]))


def out_blocks_grad(spot, heads_out, grads, shards):
    rows, width = grads.shape
    cols, depth = width // PLANE // 2, heads_out.shape[1] // shards

    def body(spot, x_ref, y_ref, *o_refs):
        for n, core in ((0, spot[1]), (1, 1 - spot[1])):
            total = tn(x_ref[...], of_core(y_ref, core, cols)).astype(bf16)
            for s in range(shards):
                o_refs[n][0, s] = folded(total[s * depth : (s + 1) * depth])

    shape = jax.ShapeDtypeStruct((PLANE, shards, depth // 2, 2 * cols), bf16)
    return grid_call(
        body,
        (PLANE,),
        [
            pl.BlockSpec((rows, heads_out.shape[1]), lambda q, _: (0, 0)),
            pl.BlockSpec((rows, 2 * cols), lambda q, _: (0, q)),
        ],
        [pl.BlockSpec((1, shards, depth // 2, 2 * cols), lambda q, _: (q, 0, 0, 0))] * 2,
        [shape] * 2,
        2 * rows * width * heads_out.shape[1],
        rows * width * 4 + width * heads_out.shape[1] * 2,
    )(spot, heads_out, grads)


def finish_pairs(spot, own, cos, sin, deps=()):
    _, rows, width = own.shape

    def body(spot, a_ref, cos_ref, sin_ref, o_ref):
        k = a_ref[0].astype(f32)
        o_ref[0] = (k * cos_ref[...] - swap_halves(k) * sin_ref[...]).astype(bf16)
        o_ref[1] = a_ref[1]

    tile = pl.BlockSpec((2, rows, LANES), lambda s, _: (0, 0, s))
    table = pl.BlockSpec((rows, LANES), lambda s, _: (0, 0))
    return grid_call(
        body,
        (width // LANES,),
        [tile, table, table],
        tile,
        jax.ShapeDtypeStruct(own.shape, bf16),
        own.size * 6,
        own.size * 4,
        deps=deps,
    )(spot, own, cos, sin)


def lanes_of(x_refs, core, depth):
    return jnp.concatenate(
        [
            jnp.concatenate([lanes_at(x, 2 * q + core, depth) for q in range(PLANE)], 1)
            for x in x_refs
        ],
        0,
    )


def gate_up(spot, xs, own, other, deps=()):
    span, width = xs[0].shape
    rows = span * len(xs)
    shards, half, cols = own[0].shape
    depth = half // PLANE
    count = len(xs)

    def body(spot, *refs):
        x_refs, (og_ref, ou_ref, tg_ref, tu_ref, go_ref, uo_ref, i_ref) = refs[:count], refs[count:]
        core = spot[1]
        for at in range(0, count, PLANE):
            part = x_refs[at : at + PLANE]
            left, right = lanes_of(part, core, depth), lanes_of(part, 1 - core, depth)
            gate = nn(left, og_ref[0]) + nn(right, tg_ref[0])
            up = nn(left, ou_ref[0]) + nn(right, tu_ref[0])
            here = slice(at * span, (at + PLANE) * span)
            go_ref[here, :] = gate.astype(bf16)
            uo_ref[here, :] = up.astype(bf16)
            i_ref[here, :] = (gate / (1.0 + jnp.exp(-gate)) * up).astype(bf16)

    weight = pl.BlockSpec((1, half, cols), lambda s, _: (s, 0, 0))
    tile = pl.BlockSpec((rows, cols), lambda s, _: (0, s))
    shape = jax.ShapeDtypeStruct((rows, shards * cols), bf16)
    return grid_call(
        body,
        (shards,),
        [still((span, width), lambda s, _: (0, 0))] * count + [weight] * 4,
        [tile] * 3,
        [shape] * 3,
        4 * rows * width * shards * cols,
        own[0].size * 8 + rows * width * 10,
        deps=deps,
    )(spot, *xs, *own, *other)


def split_rows(total, o_refs, at, depth):
    span = total.shape[0] // len(o_refs)
    for r, o_ref in enumerate(o_refs):
        o_ref[:, pl.ds(pl.multiple_of(at * depth, depth), depth)] = total[r * span : (r + 1) * span].astype(bf16)


def down(spot, inner, own, other, seqs, deps=()):
    rows, width = inner.shape
    shards, _, deep, cols = own.shape
    depth = cols // 2
    tall = rows // seqs
    span = tall // PLANE

    def body(spot, x_ref, own_ref, other_ref, *o_refs):
        core = spot[1]
        for w_ref, at in ((own_ref, core), (other_ref, 1 - core)):
            w = jnp.concatenate([unfolded(w_ref[s, 0]) for s in range(shards)], 0)
            lanes = pl.ds(pl.multiple_of(at * depth, depth), depth)
            for b in range(seqs):
                total = nn(x_ref[b * tall : (b + 1) * tall, :], w).astype(bf16)
                for r, o_ref in enumerate(o_refs):
                    o_ref[b * span : (b + 1) * span, lanes] = total[r * span : (r + 1) * span]

    weight = pl.BlockSpec((shards, 1, deep, cols), lambda q, _: (0, q, 0, 0))
    return grid_call(
        body,
        (PLANE,),
        [still((rows, width), lambda q, _: (0, 0)), weight, weight],
        [pl.BlockSpec((seqs * span, 2 * depth), lambda q, _: (0, q))] * PLANE,
        [jax.ShapeDtypeStruct((seqs * span, 2 * PLANE * depth), bf16)] * PLANE,
        4 * rows * width * PLANE * depth,
        own.size * 4 + rows * width * 4,
        deps=deps,
    )(spot, inner, own, other)


def backward_chunk(spot, chunk, span, gs, own_down, other_down, gate, up, own, other, deps=()):
    width = gs[0].shape[1]
    rows = span * len(gs)
    shards, _, deep, cols = own_down.shape
    depth, cols = cols // 2, 2 * deep
    count = len(gs)
    half = own[0].shape[1]

    def body(spot, *refs):
        x_refs, refs = refs[:count], refs[count:]
        own_ref, other_ref, g_ref, u_ref, og_ref, ou_ref, tg_ref, tu_ref, dg_ref, du_ref = refs[:10]
        o_refs, (gs_ref, us_ref) = refs[10:-2], refs[-2:]
        core, step = spot[1], pl.program_id(0)

        @pl.when(step < shards)
        def _():
            grad = None
            for w_ref, at in ((own_ref, core), (other_ref, 1 - core)):
                w = jnp.concatenate([unfolded(w_ref[0, q]) for q in range(PLANE)], 1)
                part = nt(lanes_of(x_refs, at, depth), w)
                grad = part if grad is None else grad + part
            gate, up = g_ref[...].astype(f32), u_ref[...].astype(f32)
            s = 1.0 / (1.0 + jnp.exp(-gate))
            dg = (grad * up * s * (1.0 + gate * (1.0 - s))).astype(bf16)
            du = (grad * gate * s).astype(bf16)
            dg_ref[...] = dg
            du_ref[...] = du
            gs_ref[step] = dg
            us_ref[step] = du

        @pl.when(step >= shards)
        def _():
            for gate_ref, up_ref, at in ((og_ref, ou_ref, core), (tg_ref, tu_ref, 1 - core)):
                total = None
                for d_ref, w_ref in ((gs_ref, gate_ref), (us_ref, up_ref)):
                    left = jnp.concatenate([d_ref[s] for s in range(shards)], 1)
                    part = nt(left, jnp.concatenate([w_ref[s] for s in range(shards)], 1))
                    total = part if total is None else total + part
                split_rows(total, o_refs, at, depth)

    def early(t):
        return jnp.minimum(t, shards - 1)

    def late(t):
        return jnp.maximum(t - shards, 0)

    tile = pl.BlockSpec((rows, cols), lambda t, _: (0, early(t)))
    given = pl.BlockSpec((rows, cols), lambda t, _: (chunk, early(t)))
    first = pl.BlockSpec((1, PLANE, deep, 2 * depth), lambda t, _: (early(t), 0, 0, 0))
    second = pl.BlockSpec((shards, depth, cols), lambda t, _: (0, late(t), 0))
    shape = jax.ShapeDtypeStruct((rows, shards * cols), bf16)
    outs = grid_call(
        body,
        (shards + PLANE,),
        [still((span, width), lambda t, _: (chunk, 0))] * count + [first] * 2 + [given] * 2 + [second] * 4,
        [tile] * 2 + [pl.BlockSpec((span, 2 * depth), lambda t, _: (0, late(t)))] * PLANE,
        [shape] * 2 + [jax.ShapeDtypeStruct((span, 2 * half), bf16)] * PLANE,
        6 * rows * width * shards * cols,
        own_down.size * 12 + rows * width * 16,
        [pltpu.VMEM((shards, rows, cols), bf16)] * 2,
        deps=deps,
    )(spot, *gs, own_down, other_down, gate, up, *own, *other)
    return outs[0], outs[1], outs[2:]


def norm_backward(grad_scaled, unrounded, norm_scale):
    return norm_scale * (grad_scaled - unrounded * jnp.mean(unrounded * grad_scaled, -1, keepdims=True))


def residual_grads(spot, parts, residual, cotangent, gain, deps=()):
    rows, width = residual.shape
    tall = 128
    count, each = len(parts), len(parts[0])
    per = rows // tall // count

    def body(spot, *refs):
        p_refs = refs[: count * each]
        r_ref, c_ref, g_ref, o_ref, low_ref, sum_ref = refs[count * each :]
        m = pl.program_id(0)

        @pl.when(m == 0)
        def _():
            sum_ref[...] = jnp.zeros_like(sum_ref)

        residual = r_ref[...]
        scale = lax.rsqrt(jnp.mean(residual * residual, -1, keepdims=True) + EPS)
        unrounded = residual * scale
        for b in range(count):

            @pl.when(m // per == b)
            def _(b=b):
                grad = total_of([ref[...] for ref in p_refs[b * each : (b + 1) * each]])
                terms = unrounded.astype(bf16).astype(f32) * grad
                sum_ref[0:1, :] += jnp.sum(terms, 0, keepdims=True)
                out = c_ref[...].astype(f32) + norm_backward(grad * g_ref[...], unrounded, scale)
                o_ref[...] = out
                low_ref[...] = out.astype(bf16)

    def place_of(b):
        return lambda m, _: (jnp.clip(m - b * per, 0, per - 1), 0)

    tile = pl.BlockSpec((tall, width), lambda m, _: (m, 0))
    fixed = lambda m, _: (0, 0)
    return grid_call(
        body,
        (rows // tall,),
        [pl.BlockSpec((tall, width), place_of(b)) for b in range(count) for _ in range(each)]
        + [tile, tile, pl.BlockSpec((1, width), fixed)],
        [tile, tile, pl.BlockSpec((8, width), fixed)],
        [
            jax.ShapeDtypeStruct((rows, width), f32),
            jax.ShapeDtypeStruct((rows, width), bf16),
            jax.ShapeDtypeStruct((8, width), f32),
        ],
        rows * width * 20,
        rows * width * 20,
        deps=deps,
    )(spot, *sum(parts, []), residual, cotangent, gain)


def turned(x_refs, xt_ref):
    at = 0
    for x_ref in x_refs:
        xt_ref[:, at : at + x_ref.shape[0]] = x_ref[...].T
        at += x_ref.shape[0]


def summed(xt_ref, ys):
    total, at = None, 0
    for y in ys:
        part = nn(xt_ref[:, at : at + y.shape[0]], y)
        total, at = (part if total is None else total + part), at + y.shape[0]
    return total


def column_weight_grads(spot, xs, ys, shards, deps=()):
    span, width = xs[0].shape
    rows = span * len(xs)
    cols = ys[0][0].shape[1] // shards
    depth = width // PLANE // 2
    count, lists, pieces = len(xs), len(ys), len(ys[0])
    pair = 2

    def body(spot, *refs):
        x_refs, y_refs, o_refs, xt_ref = refs[:count], refs[count : -1 - 2 * lists], refs[-1 - 2 * lists : -1], refs[-1]
        m, s = pl.program_id(1), pl.program_id(2)

        @pl.when((m == 0) & (s == 0))
        def _():
            turned(x_refs, xt_ref)

        for n in range(lists):

            @pl.when(m == n)
            def _(n=n):
                mine = y_refs[n * pieces : (n + 1) * pieces]
                total = summed(xt_ref, [r[...] for r in mine]).astype(bf16)
                first = spot[1] == 0
                for q in range(pair):
                    a = total[2 * q * depth : (2 * q + 1) * depth]
                    b = total[(2 * q + 1) * depth : (2 * q + 2) * depth]
                    o_refs[2 * n][0, q] = jnp.where(first, a, b)
                    o_refs[2 * n + 1][0, q] = jnp.where(first, b, a)

    def column(n, m, s):
        return jnp.where(m == n, s, jnp.where(m < n, 0, shards - 1))

    shape = jax.ShapeDtypeStruct((shards, PLANE, depth, cols), bf16)
    y_specs, o_specs = [], []
    for n in range(lists):
        y_specs += [
            pl.BlockSpec((y.shape[0], cols), lambda q, m, s, _, n=n: (0, column(n, m, s))) for y in ys[n]
        ]
        o_specs += [
            pl.BlockSpec((1, pair, depth, cols), lambda q, m, s, _, n=n: (column(n, m, s), q, 0, 0))
        ] * 2
    outs = grid_call(
        body,
        (PLANE // pair, lists, shards),
        [pl.BlockSpec((span, 2 * pair * depth), lambda q, m, s, _: (0, q))] * count + y_specs,
        o_specs,
        [shape] * (2 * lists),
        2 * lists * rows * width * shards * cols,
        lists * rows * width * 6 + lists * width * shards * cols * 2,
        [pltpu.VMEM((2 * pair * depth, rows), bf16)],
        deps=deps,
    )(spot, *xs, *sum(ys, []))
    return [outs[2 * n : 2 * n + 2] for n in range(lists)]


def row_weight_grad(spot, xs, ys, span, shards, deps=()):
    width = ys[0].shape[1]
    rows = sum(y.shape[0] for y in ys)
    seqs = ys[0].shape[0] // span
    tall = xs[0].shape[1] // shards
    depth = width // PLANE // 2
    count = len(xs)
    pair = 2 if shards % 2 == 0 else 1

    def body(spot, *refs):
        x_refs, y_refs, o_refs, xt_ref = refs[:count], refs[count:-3], refs[-3:-1], refs[-1]

        @pl.when(pl.program_id(1) == 0)
        def _():
            turned(x_refs, xt_ref)

        y = jnp.concatenate([r[...] for r in y_refs], 0)
        total = nn(xt_ref[...], y).astype(bf16)
        first = spot[1] == 0
        for s in range(pair):
            part = total[s * tall : (s + 1) * tall]
            a, b = folded(part[:, :depth]), folded(part[:, depth:])
            o_refs[0][s, 0] = jnp.where(first, a, b)
            o_refs[1][s, 0] = jnp.where(first, b, a)

    shape = jax.ShapeDtypeStruct((shards, PLANE, tall // 2, 2 * depth), bf16)
    return grid_call(
        body,
        (shards // pair, PLANE),
        [pl.BlockSpec((x.shape[0], pair * tall), lambda s, q, _: (0, s)) for x in xs]
        + [pl.BlockSpec((span, 2 * depth), lambda s, q, _, b=b: (b, q)) for b in range(seqs) for _ in ys],
        [pl.BlockSpec((pair, 1, tall // 2, 2 * depth), lambda s, q, _: (s, q, 0, 0))] * 2,
        [shape] * 2,
        2 * rows * width * shards * tall,
        rows * width * 6 + width * shards * tall * 2,
        [pltpu.VMEM((pair * tall, rows), bf16)],
    deps=deps,
        )(spot, *xs, *(list(ys) * seqs))


def finish_mixed(spot, residual, blocks, deps=()):
    rows, width = residual.shape
    tall = min(128, rows)

    def body(spot, r_ref, *refs):
        total = r_ref[...]
        for ref in refs[:-1]:
            total += ref[...].astype(f32)
        refs[-1][...] = total.astype(bf16)

    tile = pl.BlockSpec((tall, width), lambda m, _: (m, 0))
    return grid_call(
        body,
        (rows // tall,),
        [tile] * (1 + len(blocks)),
        tile,
        jax.ShapeDtypeStruct((rows, width), bf16),
        rows * width * 5,
        rows * width * 14,
        deps=deps,
    )(spot, residual, *blocks)


def hop(a, bits):
    n = lax.axis_size("dp")
    return lax.ppermute(a, "dp", [(i, i ^ bits) for i in range(n)])


def added(a, b):
    return (a.astype(f32) + b.astype(f32)).astype(a.dtype)


def plane_gather(a):
    return [a] + [hop(a, 2 * r) for r in range(1, PLANE)]


def plane_trade(blocks):
    return [blocks[0]] + [hop(blocks[r], 2 * r) for r in range(1, PLANE)]


def total_of(blocks):
    total = blocks[0].astype(f32)
    for b in blocks[1:]:
        total += b.astype(f32)
    return total


def plane_scatter(blocks):
    return total_of(plane_trade(blocks))


def shift(a, step):
    n = lax.axis_size("tensor")
    return lax.ppermute(a, "tensor", [(i, (i + step) % n) for i in range(n)])


def line_gather(a):
    return [a] + [shift(a, s) for s in range(1, lax.axis_size("tensor"))]


def line_scatter(blocks):
    n, place = lax.axis_size("tensor"), lax.axis_index("tensor")
    total = lax.dynamic_index_in_dim(blocks, place, 0, keepdims=False).astype(f32)
    for step in range(1, n):
        mine = lax.dynamic_index_in_dim(blocks, lax.rem(place + step, n), 0, keepdims=False)
        total += shift(mine, step).astype(f32)
    return total


def after(a, *others):
    others = jax.tree.leaves(others)
    place = pl.BlockSpec(memory_space=pl.ANY)
    return pl.pallas_call(
        lambda *refs: None,
        in_specs=[place] * (1 + len(others)),
        out_specs=place,
        out_shape=jax.ShapeDtypeStruct(a.shape, a.dtype),
        input_output_aliases={0: 0},
        cost_estimate=pl.CostEstimate(flops=1, bytes_accessed=1, transcendentals=0),
    )(a, *others)


def token(*arrays, steps=2):
    arrays = jax.tree.leaves(arrays)
    place = pl.BlockSpec(memory_space=pl.ANY)

    def body(*refs):
        refs[-1][...] = jnp.zeros_like(refs[-1])

    for _ in range(steps):
        arrays = [
            pl.pallas_call(
                body,
                in_specs=[place] * len(arrays),
                out_specs=pl.BlockSpec(memory_space=pltpu.VMEM),
                out_shape=jax.ShapeDtypeStruct((8, LANES), f32),
            )(*arrays)
        ]
    return arrays[0]


def by_chip(parts, chip):
    a, b, c, d = parts
    odd = (chip & 1) == 1
    a, b, c, d = (
        jnp.where(odd, b, a),
        jnp.where(odd, a, b),
        jnp.where(odd, d, c),
        jnp.where(odd, c, d),
    )
    high = (chip & 2) == 2
    return (
        jnp.where(high, c, a),
        jnp.where(high, d, b),
        jnp.where(high, a, c),
        jnp.where(high, b, d),
    )


def trade(pieces, axis, chip, hold=lambda a: a):
    come = []
    for r in range(PLANE):
        piece = lax.dynamic_index_in_dim(pieces, chip ^ r, axis, keepdims=False)
        come.append(hold(piece) if r == 0 else hop(piece, 2 * r))
    return by_chip(come, chip)


def core_sum(pair, *others):
    return added(after(pair[0], others) if others else pair[0], hop(pair[1], 1))


def plane_sum(blocks, chip):
    mine = [lax.dynamic_index_in_dim(blocks, chip ^ r, 0, keepdims=False) for r in range(PLANE)]
    return plane_scatter(mine).astype(bf16)


def rotary_tables(positions):
    half_size = HD // 2
    frequency = THETA ** (-2.0 * jnp.arange(half_size, dtype=f32) / HD)
    angles = positions.astype(f32)[:, None] * frequency[None, :]
    cos, sin = jnp.cos(angles), jnp.sin(angles)
    return (
        jnp.concatenate([cos, cos] * (LANES // HD), -1),
        jnp.concatenate([-sin, sin] * (LANES // HD), -1),
    )


def shards(
    tokens, segments, attn_norm, w_query, w_key, w_value, w_out, mlp_norm, w_gate, w_up, w_down, cotangent
):
    dp_count, tp_count = lax.axis_size("dp"), lax.axis_size("tensor")
    groups = dp_count // 8
    place = lax.axis_index("tensor")
    index = lax.axis_index("dp")
    core, chip = index & 1, (index >> 1) & 3
    seqs, span, width = tokens.shape
    rows = seqs * span
    block = width // 8

    group_sets = [[g * 8 + l for g in range(groups)] for l in range(8)]

    def widen(a, axis):
        if groups == 1:
            return a
        return lax.all_gather(a, "dp", axis=axis, tiled=True, axis_index_groups=group_sets)

    def narrow(a, axis):
        if groups == 1:
            return a
        return lax.psum_scatter(
            a.astype(bf16), "dp", scatter_dimension=axis, tiled=True, axis_index_groups=group_sets
        )

    def inward(a):
        if groups == 1:
            return a
        lead = a.shape[:-1]
        return jnp.swapaxes(a.reshape(lead + (groups, 8, -1)), -3, -2).reshape(lead + (-1,))

    def outward(a):
        if groups == 1:
            return a
        lead = a.shape[:-1]
        return jnp.swapaxes(a.reshape(lead + (8, groups, -1)), -3, -2).reshape(lead + (-1,))

    eight = [[g * 8 + l for l in range(8)] for g in range(groups)]

    def along(a):
        return lax.all_gather(a, "tensor", axis=0, tiled=False)

    def in_plane(a):
        if groups == 1:
            return lax.all_gather(a, "dp", axis=0, tiled=False)
        return lax.all_gather(a, "dp", axis=0, tiled=False, axis_index_groups=eight)

    tokens = inward(tokens).reshape(rows, width)
    cotangent = inward(cotangent).reshape(rows, width)
    attn_norm, mlp_norm = widen(attn_norm, 0), widen(mlp_norm, 0)
    w_query, w_key, w_value = widen(w_query, 0), widen(w_key, 0), widen(w_value, 0)
    w_gate, w_up = widen(w_gate, 0), widen(w_up, 0)
    w_out, w_down = widen(w_out, 1), widen(w_down, 1)

    kv_cols = 2 * w_key.shape[1]
    kv_group = w_query.shape[1] // w_key.shape[1]
    gains = jnp.concatenate(
        [
            jnp.pad(attn_norm, (0, kv_cols - block))[None],
            jnp.pad(mlp_norm, (0, kv_cols - block))[None],
            jnp.zeros((14, kv_cols), bf16),
        ],
        0,
    )
    near_kv = line_gather(jnp.concatenate([jnp.concatenate([w_key, w_value], 1), gains], 0))
    lines = w_down.reshape(PLANE, 2, -1, block)
    pieces = jnp.stack(
        [
            jnp.swapaxes(w_gate.reshape(block, PLANE, -1), 0, 1),
            jnp.swapaxes(w_up.reshape(block, PLANE, -1), 0, 1),
            jnp.concatenate([lines[:, 0], lines[:, 1]], 2),
        ],
        1,
    )
    all_kv = in_plane(jnp.stack(near_kv, 0))
    gain_one = all_kv[:, 0, block, :block].reshape(width).astype(f32)
    gain_two = all_kv[:, 0, block + 1, :block].reshape(width).astype(f32)
    lined = line_gather(after(jnp.stack([w_query, folded(w_out)], 0), near_kv[1:]))
    lined_q, lined_out = (jnp.stack([a[n] for a in lined], 0) for n in range(2))
    chunks = [slice(b * span, (b + 1) * span) for b in range(seqs)]

    spot = jnp.stack([place, core, chip]).astype(jnp.int32)
    cos, sin = rotary_tables(place * span + jnp.arange(span, dtype=jnp.int32))
    cos_rows, sin_rows = jnp.tile(cos, (seqs, 1)), jnp.tile(sin, (seqs, 1))
    x = tokens.astype(f32)
    norm_one = lax.rsqrt(jnp.mean(x * x, -1, keepdims=True) + EPS)
    scaled_one = (x * norm_one).astype(bf16)
    normed_one = (scaled_one.astype(f32) * gain_one).astype(bf16)
    pair = project_pairs(spot, normed_one, all_kv, cos_rows, sin_rows, block, deps=lined[1:])
    pairs = along(pair)
    def both_cores(blocks, *others):
        if others:
            blocks = [after(b, others) for b in blocks]
        return blocks + [hop(b, 1) for b in blocks]

    all_q = plane_gather(after(lined_q, pair))
    sent = after(pieces, all_q[1:])
    all_q = both_cores(all_q)
    queries = project_queries(spot, normed_one, all_q, cos_rows, sin_rows)
    near = jnp.stack(trade(sent, 0, chip, lambda own: after(own, queries)), 1)
    tall = near.shape[1] * near.shape[2]
    own_gate, own_up = (along(after(near[n].reshape(tall, -1), pair)) for n in range(2))
    all_out = plane_gather(after(lined_out, all_q[1:], near))

    seg_blocks = segments.reshape(seqs, tp_count, span)
    own_seg = lax.dynamic_index_in_dim(seg_blocks, place, 1, keepdims=False)
    here = jnp.arange(span, dtype=jnp.int32)
    bias = []
    for j in range(tp_count):
        key_seg = lax.dynamic_index_in_dim(seg_blocks, jnp.maximum(place - j, 0), 1, keepdims=False)
        allowed = key_seg[:, :, None] == own_seg[:, None, :]
        if j == 0:
            allowed &= here[None, :, None] <= here[None, None, :]
        bias.append(jnp.where(allowed, 0.0, -1e30).astype(f32))
    bias = jnp.concatenate(bias, 1)
    heads_out, lse = attend(spot, queries, pairs, bias, span, kv_group)
    all_out = both_cores(all_out, heads_out)
    residual = project_out(spot, heads_out, all_out, tokens)

    norm_two = lax.rsqrt(jnp.mean(residual * residual, -1, keepdims=True) + EPS)
    scaled_two = (residual * norm_two).astype(bf16)
    normed_two = (scaled_two.astype(f32) * gain_two).astype(bf16)
    full_two = []
    for c in chunks:
        full_two.append(plane_gather(after(normed_two[c], full_two[-1][1:]) if full_two else normed_two[c]))
    cot_full = plane_gather(after(cotangent, full_two[-1][1:]))
    own_gate, own_up = after(own_gate, full_two[0][1:]), after(own_up, full_two[-1][1:])
    own_in = (own_gate, own_up)
    other_in = (hop(own_gate, 1), hop(own_up, 1))
    own_down = along(after(near[2], residual))
    tokens_two = sum(full_two, [])
    gate, up, inner = gate_up(spot, tokens_two, own_in, other_in)
    other_down = hop(own_down, 1)

    def line_sum(a):
        return lax.psum_scatter(a, "tensor", scatter_dimension=0, tiled=False)

    down_parts = row_weight_grad(spot, [inner], cot_full, span, tp_count)
    d_gate, d_up, from_plane, deps = [], [], [], down_parts
    for n in range(seqs):
        weights = (own_down, other_down, gate, up, own_in, other_in)
        dg, du, to_plane = backward_chunk(spot, n, span, cot_full, *weights, deps=deps)
        d_gate.append(dg)
        d_up.append(du)
        deps = to_plane
        from_plane.append(plane_trade(list(to_plane)))
    down_pair = core_sum(down_parts, d_gate[0])
    down_sum = line_sum(down_pair)
    deps = [down_pair, to_plane, [f[1:] for f in from_plane[:-1]]]
    gate_parts, up_parts = column_weight_grads(spot, tokens_two, [d_gate, d_up], tp_count, deps=deps)
    grad_residual, grad_low, gain_two_terms = residual_grads(
        spot, from_plane, residual, cotangent, gain_two[None], deps=[up_parts[0], down_sum]
    )
    gain_two_terms = gain_two_terms[0]
    gate_parts, up_parts = ((p[0], after(p[1], grad_low)) for p in (gate_parts, up_parts))
    shares = down(spot, inner, own_down, other_down, seqs, deps=grad_low)
    gate_pair, up_pair = core_sum(gate_parts, shares[0]), core_sum(up_parts, shares[0])
    gate_sum = line_sum(gate_pair)
    mixed = plane_trade(list(shares))

    out_parts = out_blocks_grad(spot, heads_out, grad_low, tp_count)
    grad_heads = unproject_out(spot, grad_low, all_out, deps=[up_parts[0], out_parts])
    deps = [out_parts, up_pair, gate_pair]
    dq, dkv = unattend(spot, queries, grad_heads, pairs, bias, lse, cos, sin, span, kv_group, deps=deps)
    gate_here = token(dq, mixed[1:], gate_sum, steps=1)
    dkv = line_sum(after(dkv, gate_here))
    up_sum = line_sum(up_pair)
    partial = unproject_queries(spot, dq, all_q, deps=gate_here)
    out_near = plane_sum(core_sum((out_parts[0], after(out_parts[1], gate_here))), chip)
    query_parts = in_blocks_grad(spot, normed_one, dq, None, None, tp_count, deps=partial)
    grad_out = unfolded(line_scatter(out_near))
    query_near = plane_sum(core_sum(query_parts), chip)
    grad_query = line_scatter(query_near)
    mixed = finish_mixed(spot, residual, mixed, deps=query_parts)
    come = trade(after(jnp.stack([down_sum, gate_sum, up_sum], 1), out_near, query_near), 0, chip)
    grad_down = jnp.concatenate([jnp.concatenate([c[0, :, :block], c[0, :, block:]], 0) for c in come], 0)
    grad_gate, grad_up = (jnp.concatenate([c[n] for c in come], 1) for n in (1, 2))

    dkv = finish_pairs(spot, dkv, cos_rows, sin_rows, deps=[out_near, query_near])
    grad_normed_one, gain_one_terms = unproject_pairs(spot, partial, dkv, all_kv, scaled_one)
    gain_one_terms = gain_one_terms[0]
    gain_terms = jnp.stack([gain_one_terms.reshape(8, block), gain_two_terms.reshape(8, block)], 1)
    gain_terms = jnp.pad(gain_terms, ((0, 0), (0, 14), (0, kv_cols - block)))
    kv_parts = in_blocks_grad(spot, normed_one, dq, dkv, gain_terms, tp_count)
    kv_sum = line_scatter(plane_sum(core_sum(kv_parts), chip))
    grad_tokens = grad_residual + norm_backward(grad_normed_one * gain_one, x * norm_one, norm_one)
    grad_tokens = grad_tokens.astype(bf16)
    def gain_share(line):
        line = narrow(line, 0)
        share = line.shape[0] // tp_count
        return lax.dynamic_slice_in_dim(line, place * share, share, 0).astype(f32)

    half = kv_cols // 2
    return (
        outward(mixed).reshape(seqs, span, width),
        outward(grad_tokens).reshape(seqs, span, width),
        gain_share(kv_sum[block, :block]),
        narrow(grad_query, 0).astype(f32),
        narrow(kv_sum[:block, :half], 0).astype(f32),
        narrow(kv_sum[:block, half:], 0).astype(f32),
        narrow(grad_out, 1).astype(f32),
        gain_share(kv_sum[block + 1, :block]),
        narrow(grad_gate, 0).astype(f32),
        narrow(grad_up, 0).astype(f32),
        narrow(grad_down, 1).astype(f32),
    )


def solution(mesh):
    placed = (
        P("dp", "tensor", None),
        P("dp", None),
        P("dp"),
        P("dp", "tensor"),
        P("dp", "tensor"),
        P("dp", "tensor"),
        P("tensor", "dp"),
        P("dp"),
        P("dp", "tensor"),
        P("dp", "tensor"),
        P("tensor", "dp"),
        P("dp", "tensor", None),
    )
    return jax.shard_map(
        shards,
        mesh=mesh,
        in_specs=placed,
        out_specs=(
            P("dp", "tensor", None),
            P("dp", "tensor", None),
            P(("dp", "tensor")),
            P("dp", "tensor"),
            P("dp", "tensor"),
            P("dp", "tensor"),
            P("tensor", "dp"),
            P(("dp", "tensor")),
            P("dp", "tensor"),
            P("dp", "tensor"),
            P("tensor", "dp"),
        ),
        check_vma=False,
    )
```

```python
import functools

import jax
import jax.numpy as jnp
from jax import lax
from jax.experimental import pallas as pl
from jax.experimental.pallas import tpu as pltpu
from jax.sharding import PartitionSpec as P

HD = 64
EPS = 1e-05
THETA = 500000.0
LOG2E = 1.4426950408889634
LANES = 128
PLANE = 4
f32 = jnp.float32
bf16 = jnp.bfloat16


def call(body, flops, moved, vmem=50, **kw):
    return pl.pallas_call(
        body,
        compiler_params=pltpu.CompilerParams(vmem_limit_bytes=vmem * 2**20),
        cost_estimate=pl.CostEstimate(flops=flops, bytes_accessed=moved, transcendentals=0),
        **kw,
    )


def nn(a, b):
    return jnp.dot(a, b, preferred_element_type=f32)


def nt(a, b):
    return lax.dot_general(a, b, (((1,), (1,)), ((), ())), preferred_element_type=f32)


def tn(a, b):
    return lax.dot_general(a, b, (((0,), (0,)), ((), ())), preferred_element_type=f32)


def swap_halves(x):
    lane = lax.broadcasted_iota(jnp.int32, x.shape, 1)
    return jnp.where(lane % HD < HD // 2, pltpu.roll(x, LANES - HD // 2, 1), pltpu.roll(x, HD // 2, 1))


def gather_keys(k_refs, v_refs, blocks):
    k = jnp.concatenate([k_refs[j][0, 0] for j in range(blocks)], 0)
    v = jnp.concatenate([v_refs[j][0, 0] for j in range(blocks)], 0)
    return k, v


def padded_rows(part, e):
    zero = jnp.zeros_like(part)
    return jnp.concatenate([part, zero] if e == 0 else [zero, part], 0)


def attend_blocks(blocks, group, q_ref, k_refs, v_refs, bias_ref, o_ref, lse_ref, qt_ref, ot_ref):
    span = q_ref.shape[0]
    n = blocks * span
    k, v = gather_keys(k_refs, v_refs, blocks)
    vt = v.T
    qt_ref[...] = q_ref[...].T
    factor = HD**-0.5 * LOG2E

    def step(i, carry):
        for e in range(2):
            head = e * group + i
            rows = pl.ds(pl.multiple_of(head * HD, HD), HD)
            scores = nn(k, padded_rows(qt_ref[rows, :], e))
            logits = scores * factor + bias_ref[0, :n, :]
            top = jnp.max(logits, 0, keepdims=True)
            weights = jnp.exp2(logits - top)
            total = jnp.sum(weights, 0, keepdims=True)
            out = nn(vt[e * HD : (e + 1) * HD], weights.astype(bf16))
            ot_ref[rows, :] = out * (1.0 / total)
            lse_ref[0, 0, pl.ds(head, 1), :] = top + jnp.log2(total)
        return carry

    lax.fori_loop(0, group, step, 0, unroll=4)
    o_ref[...] = ot_ref[...].T.astype(bf16)


def attend_kernel(count, group, place, *refs):
    q_ref, k_refs, v_refs = refs[0], refs[1 : 1 + count], refs[1 + count : 1 + 2 * count]
    rest = refs[1 + 2 * count :]
    for blocks in range(1, count + 1):

        @pl.when(place[0] == blocks - 1)
        def _(blocks=blocks):
            attend_blocks(blocks, group, q_ref, k_refs, v_refs, *rest)


def key_specs(count, span):
    return [
        pl.BlockSpec(
            (1, 1, span, LANES), lambda b, p, s, part=part, j=j: (jnp.maximum(s[0] - j, 0), part, b, p)
        )
        for part in range(2)
        for j in range(count)
    ]


def attend(place, queries, pairs, bias, span, group):
    rows, width = queries.shape
    count = pairs.shape[0]
    seqs = rows // span
    kv_width = pairs.shape[3]
    tiles = kv_width // LANES
    wide = width // tiles
    in_specs = [pl.BlockSpec((span, wide), lambda b, p, s: (b, p))] + key_specs(count, span)
    in_specs.append(pl.BlockSpec((1, count * span, span), lambda b, p, s: (b, 0, 0)))
    heads = wide // HD
    spec = pltpu.PrefetchScalarGridSpec(
        num_scalar_prefetch=1,
        grid=(seqs, tiles),
        in_specs=in_specs,
        out_specs=[
            pl.BlockSpec((span, wide), lambda b, p, s: (b, p)),
            pl.BlockSpec((1, 1, heads, span), lambda b, p, s: (b, p, 0, 0)),
        ],
        scratch_shapes=[pltpu.VMEM((wide, span), bf16), pltpu.VMEM((wide, span), f32)],
    )
    return call(
        functools.partial(attend_kernel, count, group),
        flops=rows * width * span * count * 8,
        moved=rows * width * 4,
        grid_spec=spec,
        out_shape=[
            jax.ShapeDtypeStruct((rows, width), bf16),
            jax.ShapeDtypeStruct((seqs, tiles, heads, span), f32),
        ],
    )(place, queries, *([pairs] * (2 * count)), bias)


def unattend_blocks(
    blocks, count, group, q_ref, g_ref, k_refs, v_refs, bias_ref, lse_ref, cos_ref, sin_ref,
    dq_ref, dkv_ref, qt_ref, gt_ref, dqt_ref, dk_ref, dv_ref,
):
    span = q_ref.shape[0]
    n = blocks * span
    k, v = gather_keys(k_refs, v_refs, blocks)
    kt = k.T
    qt_ref[...] = q_ref[...].T
    gt_ref[...] = g_ref[...].T
    dk_ref[...] = jnp.zeros_like(dk_ref)
    dv_ref[...] = jnp.zeros_like(dv_ref)
    factor = HD**-0.5 * LOG2E
    lane = lax.broadcasted_iota(jnp.int32, (span, LANES), 1)

    def moved(tile, b, e):
        if b != e:
            tile = pltpu.roll(tile, HD, 1)
        return jnp.where((lane < HD) if e == 0 else (lane >= HD), tile, 0.0).astype(bf16)

    def step(i, carry):
        for e in range(2):
            tile_at = pl.ds(pl.multiple_of((e * (group // 2) + i) * LANES, LANES), LANES)
            q_tile = q_ref[:, tile_at].astype(f32)
            g_tile = g_ref[:, tile_at].astype(f32)
            all_ds, all_p = [], []
            for b in range(2):
                head = e * group + 2 * i + b
                rows = pl.ds(pl.multiple_of(head * HD, HD), HD)
                scores = nn(k, padded_rows(qt_ref[rows, :], e))
                lse = lse_ref[0, 0, pl.ds(head, 1), :]
                probs = jnp.exp2(scores * factor + bias_ref[0, :n, :] - lse)
                dp = nn(v, padded_rows(gt_ref[rows, :], e))
                delta = jnp.sum(probs * dp, 0, keepdims=True)
                ds = (probs * (dp - delta)).astype(bf16)
                dqt_ref[rows, :] = nn(kt[e * HD : (e + 1) * HD], ds)
                all_ds.append(ds)
                all_p.append(probs.astype(bf16))
            q_rows = jnp.concatenate([moved(q_tile, b, e) for b in range(2)], 0)
            g_rows = jnp.concatenate([moved(g_tile, b, e) for b in range(2)], 0)
            dk_ref[:n, :] += nn(jnp.concatenate(all_ds, 1), q_rows)
            dv_ref[:n, :] += nn(jnp.concatenate(all_p, 1), g_rows)
        return carry

    lax.fori_loop(0, group // 2, step, 0, unroll=2)
    scale = HD**-0.5
    dq = dqt_ref[...].T * scale
    for t in range(dq.shape[1] // LANES):
        part = dq[:, t * LANES : (t + 1) * LANES]
        dq_ref[:, t * LANES : (t + 1) * LANES] = (
            part * cos_ref[...] - swap_halves(part) * sin_ref[...]
        ).astype(bf16)
    for n in range(count):
        j = blocks - 1 - n if n < blocks else n
        dkv_ref[n, 0] = (dk_ref[j * span : (j + 1) * span, :] * scale).astype(bf16)
        dkv_ref[n, 1] = dv_ref[j * span : (j + 1) * span, :].astype(bf16)


def unattend_kernel(count, group, skip, place, *refs):
    refs = refs[skip:]
    q_ref, g_ref, k_refs, v_refs = refs[0], refs[1], refs[2 : 2 + count], refs[2 + count : 2 + 2 * count]
    rest = refs[2 + 2 * count :]
    for blocks in range(1, count + 1):

        @pl.when(place[0] == blocks - 1)
        def _(blocks=blocks):
            unattend_blocks(blocks, count, group, q_ref, g_ref, k_refs, v_refs, *rest)


def unattend(place, queries, grads, pairs, bias, lse, cos, sin, span, group, deps=()):
    rows, width = queries.shape
    count = pairs.shape[0]
    seqs = rows // span
    kv_width = pairs.shape[3]
    tiles = kv_width // LANES
    wide = width // tiles
    heads = wide // HD
    tall = pl.BlockSpec((span, wide), lambda b, p, s: (b, p))
    table = pl.BlockSpec((span, LANES), lambda b, p, s: (0, 0))
    deps = jax.tree.leaves(deps)
    in_specs = [pl.BlockSpec(memory_space=pl.ANY)] * len(deps) + [tall, tall] + key_specs(count, span)
    in_specs += [
        pl.BlockSpec((1, count * span, span), lambda b, p, s: (b, 0, 0)),
        pl.BlockSpec((1, 1, heads, span), lambda b, p, s: (b, p, 0, 0)),
        table,
        table,
    ]
    spec = pltpu.PrefetchScalarGridSpec(
        num_scalar_prefetch=1,
        grid=(seqs, tiles),
        in_specs=in_specs,
        out_specs=[tall, pl.BlockSpec((count, 2, span, LANES), lambda b, p, s: (0, 0, b, p))],
        scratch_shapes=[
            pltpu.VMEM((wide, span), bf16),
            pltpu.VMEM((wide, span), bf16),
            pltpu.VMEM((wide, span), f32),
            pltpu.VMEM((count * span, LANES), f32),
            pltpu.VMEM((count * span, LANES), f32),
        ],
    )
    return call(
        functools.partial(unattend_kernel, count, group, len(deps)),
        flops=rows * width * span * count * 20,
        moved=rows * width * 8,
        grid_spec=spec,
        out_shape=[
            jax.ShapeDtypeStruct((rows, width), bf16),
            jax.ShapeDtypeStruct((count, 2, rows, kv_width), bf16),
        ],
    )(place, *deps, queries, grads, *([pairs] * (2 * count)), bias, lse, cos, sin)


def turn(y, cos, sin, out_ref, start=0):
    for t in range(y.shape[1] // LANES):
        part = y[:, t * LANES : (t + 1) * LANES]
        out_ref[:, t * LANES : (t + 1) * LANES] = (part * cos + swap_halves(part) * sin).astype(bf16)


def block_home(spot, half, r):
    core = spot[1] if half == 0 else 1 - spot[1]
    return 2 * (spot[2] ^ r) + core


def lanes_at(ref, at, size):
    return ref[:, pl.ds(pl.multiple_of(at * size, size), size)]


def by_block(ref, spot, size):
    return jnp.concatenate(
        [lanes_at(ref, block_home(spot, half, r), size) for half in range(2) for r in range(PLANE)], 1
    )


def by_slot(ref, spot, shards, size):
    return jnp.concatenate([lanes_at(ref, slot_home(spot, s, shards), size) for s in range(shards)], 1)


def slot_home(spot, s, shards):
    return lax.rem(spot[0] + shards - s, shards)


def grid_call(body, grid, in_specs, out_specs, out_shape, flops, moved, scratch=(), deps=()):
    deps = jax.tree.leaves(deps)

    def late(spot, *refs):
        body(spot, *refs[len(deps) :])

    run = call(
        late,
        flops=flops,
        moved=moved,
        grid_spec=pltpu.PrefetchScalarGridSpec(
            num_scalar_prefetch=1,
            grid=grid,
            in_specs=[pl.BlockSpec(memory_space=pl.ANY)] * len(deps) + list(in_specs),
            out_specs=out_specs,
            scratch_shapes=list(scratch),
        ),
        out_shape=out_shape,
    )
    return lambda spot, *arrays: run(spot, *deps, *arrays)


def project_pairs(spot, normed, weights, cos, sin, depth, deps=()):
    rows, width = normed.shape
    parts, shards, _, cols = weights.shape
    half = cols // 2

    def body(spot, x_ref, w_ref, cos_ref, sin_ref, o_ref):
        w = w_ref[:, 0, :depth, :].reshape(parts * depth, cols)
        y = nn(x_ref[...], w)
        k = y[:, :half]
        o_ref[0] = (k * cos_ref[...] + swap_halves(k) * sin_ref[...]).astype(bf16)
        o_ref[1] = y[:, half:].astype(bf16)

    whole = lambda s, _: (0, 0)
    return grid_call(
        body,
        (shards,),
        [
            pl.BlockSpec((rows, width), whole),
            pl.BlockSpec((parts, 1, weights.shape[2], cols), lambda s, _: (0, s, 0, 0)),
            pl.BlockSpec((rows, LANES), whole),
            pl.BlockSpec((rows, LANES), whole),
        ],
        pl.BlockSpec((2, rows, half), lambda s, spot: (0, 0, slot_home(spot, s, shards))),
        jax.ShapeDtypeStruct((2, rows, half * shards), bf16),
        2 * rows * width * shards * cols,
        weights.size * 2 + normed.size * 2,
        deps=deps,
    )(spot, normed, weights, cos, sin)


def project_queries(spot, normed, weights, cos, sin):
    rows, width = normed.shape
    shards, depth, cols = weights[0].shape
    count = len(weights)

    def body(spot, *refs):
        x_ref, w_refs, cos_ref, sin_ref, o_ref, xs_ref = refs[0], refs[1 : 1 + count], *refs[1 + count :]

        @pl.when(pl.program_id(0) == 0)
        def _():
            xs_ref[...] = by_block(x_ref, spot, depth)

        y = nn(xs_ref[...], jnp.concatenate([w[0] for w in w_refs], 0))
        turn(y, cos_ref[...], sin_ref[...], o_ref)

    whole = lambda s, _: (0, 0)
    return grid_call(
        body,
        (shards,),
        [pl.BlockSpec((rows, width), whole)]
        + [pl.BlockSpec((1, depth, cols), lambda s, _: (s, 0, 0))] * count
        + [pl.BlockSpec((rows, LANES), whole)] * 2,
        pl.BlockSpec((rows, cols), lambda s, spot: (0, slot_home(spot, s, shards))),
        jax.ShapeDtypeStruct((rows, cols * shards), bf16),
        2 * rows * width * shards * cols,
        width * shards * cols * 2 + normed.size * 4,
        [pltpu.VMEM((rows, width), bf16)],
    )(spot, normed, *weights, cos, sin)


def folded(w):
    half = w.shape[0] // 2
    return jnp.concatenate([w[:half], w[half:]], 1)


def unfolded(w):
    half = w.shape[1] // 2
    return jnp.concatenate([w[:, :half], w[:, half:]], 0)


def project_out(spot, heads_out, weights, tokens, deps=()):
    rows, width = heads_out.shape
    shards, depth, cols = weights[0].shape
    depth, cols = 2 * depth, cols // 2
    count = len(weights)
    tall = min(256, rows)

    def body(spot, *refs):
        x_ref, w_refs, t_ref, o_ref = refs[0], refs[1 : 1 + count], *refs[1 + count :]
        x = by_slot(x_ref, spot, shards, depth)
        for n, w_ref in enumerate(w_refs):
            at = block_home(spot, n // PLANE, n % PLANE)
            y = nn(x, jnp.concatenate([unfolded(w_ref[s]) for s in range(shards)], 0))
            o_ref[:, pl.ds(pl.multiple_of(at * cols, cols), cols)] = lanes_at(t_ref, at, cols).astype(f32) + y

    tile = pl.BlockSpec((tall, width), lambda m, _: (m, 0))
    return grid_call(
        body,
        (rows // tall,),
        [tile] + [pl.BlockSpec(w.shape, lambda m, _: (0, 0, 0)) for w in weights] + [tile],
        tile,
        jax.ShapeDtypeStruct((rows, cols * count), f32),
        2 * rows * width * count * cols,
        width * cols * count * 2 + rows * width * 8,
        deps=deps,
    )(spot, heads_out, *weights, tokens)


def unproject_out(spot, grads, weights, deps=()):
    rows, width = grads.shape
    shards, depth, cols = weights[0].shape
    depth, cols = 2 * depth, cols // 2
    count = len(weights)

    def body(spot, *refs):
        x_ref, w_refs, o_ref, xs_ref = refs[0], refs[1 : 1 + count], *refs[1 + count :]

        @pl.when(pl.program_id(0) == 0)
        def _():
            xs_ref[...] = by_block(x_ref, spot, cols)

        w = jnp.concatenate([unfolded(w_ref[0]) for w_ref in w_refs], 1)
        o_ref[...] = nt(xs_ref[...], w).astype(bf16)

    return grid_call(
        body,
        (shards,),
        [pl.BlockSpec((rows, width), lambda s, _: (0, 0))]
        + [pl.BlockSpec((1, depth // 2, 2 * cols), lambda s, _: (s, 0, 0))] * count,
        pl.BlockSpec((rows, depth), lambda s, spot: (0, slot_home(spot, s, shards))),
        jax.ShapeDtypeStruct((rows, depth * shards), bf16),
        2 * rows * width * shards * depth,
        width * shards * depth * 2 + rows * width * 6,
        [pltpu.VMEM((rows, width), bf16)],
        deps=deps,
    )(spot, grads, *weights)


def still(shape, index):
    return pl.BlockSpec(shape, index, pipeline_mode=pl.Buffered(1))


def unproject_queries(spot, dq, w_q, deps=()):
    rows, width = dq.shape
    shards, depth, cols = w_q[0].shape
    count = len(w_q)
    tall = min(256, rows)

    def body(spot, q_ref, *refs):
        left = by_slot(q_ref, spot, shards, cols)
        for n, w_ref in enumerate(refs[:-1]):
            at = block_home(spot, n // PLANE, n % PLANE)
            y = nt(left, jnp.concatenate([w_ref[s] for s in range(shards)], 1))
            refs[-1][:, pl.ds(pl.multiple_of(at * depth, depth), depth)] = y

    tile = pl.BlockSpec((tall, width), lambda m, _: (m, 0))
    return grid_call(
        body,
        (rows // tall,),
        [tile] + [still(w.shape, lambda m, _: (0, 0, 0)) for w in w_q],
        pl.BlockSpec((tall, count * depth), lambda m, _: (m, 0)),
        jax.ShapeDtypeStruct((rows, count * depth), f32),
        2 * rows * count * depth * shards * cols,
        count * depth * shards * cols * 2 + rows * width * 6,
        deps=deps,
    )(spot, dq, *w_q)


def unproject_pairs(spot, partial, dkv, w_kv, scaled, deps=()):
    rows, width = partial.shape
    parts, shards, _, cols = w_kv.shape
    depth, thin = width // parts, cols // 2
    tall = min(256, rows)

    def body(spot, p_ref, kv_ref, w_ref, s_ref, o_ref, sum_ref):
        @pl.when(pl.program_id(0) == 0)
        def _():
            sum_ref[...] = jnp.zeros_like(sum_ref)

        left = jnp.concatenate(
            [
                kv_ref[n, :, pl.ds(pl.multiple_of(slot_home(spot, s, shards) * thin, thin), thin)]
                for s in range(shards)
                for n in range(2)
            ],
            1,
        )
        for i in range(parts):
            here = slice(i * depth, (i + 1) * depth)
            total = nt(left, jnp.concatenate([w_ref[i, s, :depth, :] for s in range(shards)], 1))
            total += p_ref[:, here]
            o_ref[:, here] = total
            sum_ref[0:1, here] += jnp.sum(s_ref[:, here].astype(f32) * total, 0, keepdims=True)

    tile = pl.BlockSpec((tall, width), lambda m, _: (m, 0))
    return grid_call(
        body,
        (rows // tall,),
        [
            tile,
            pl.BlockSpec((2, tall, dkv.shape[2]), lambda m, _: (0, m, 0)),
            still(w_kv.shape, lambda m, _: (0, 0, 0, 0)),
            tile,
        ],
        [tile, pl.BlockSpec((8, width), lambda m, _: (0, 0))],
        [jax.ShapeDtypeStruct((rows, width), f32), jax.ShapeDtypeStruct((8, width), f32)],
        2 * rows * width * shards * cols,
        w_kv.size * 2 + rows * width * 12,
        deps=deps,
    )(spot, partial, dkv, w_kv, scaled)


def of_core(ref, core, depth):
    return ref[:, pl.ds(pl.multiple_of(core * depth, depth), depth)]


def in_blocks_grad(spot, normed, dq, dkv, gains, shards, deps=()):
    rows, width = normed.shape
    depth = width // PLANE // 2
    y = dq if dkv is None else dkv
    cols = (dq.shape[1] if dkv is None else 2 * dkv.shape[2]) // shards
    extra = 0 if gains is None else gains.shape[1]

    def body(spot, x_ref, y_ref, *refs):
        for n, core in ((0, spot[1]), (1, 1 - spot[1])):
            x, o_ref = of_core(x_ref, core, depth), refs[-2 + n]
            totals = [tn(x, y_ref[...])] if dkv is None else [tn(x, y_ref[0]), tn(x, y_ref[1])]
            thin = cols // len(totals)
            for s in range(shards):
                for m, total in enumerate(totals):
                    o_ref[0, s, :depth, m * thin : (m + 1) * thin] = total[:, s * thin : (s + 1) * thin].astype(bf16)
                if extra:
                    o_ref[0, s, depth:, :] = refs[0][core].astype(bf16)

    whole = pl.BlockSpec(y.shape, (lambda q, _: (0, 0)) if dkv is None else (lambda q, _: (0, 0, 0)))
    more = [] if gains is None else [pl.BlockSpec((2, extra, gains.shape[2]), lambda q, _: (q, 0, 0))]
    shape = jax.ShapeDtypeStruct((PLANE, shards, depth + extra, cols), bf16)
    return grid_call(
        body,
        (PLANE,),
        [pl.BlockSpec((rows, 2 * depth), lambda q, _: (0, q)), whole] + more,
        [pl.BlockSpec((1, shards, depth + extra, cols), lambda q, _: (q, 0, 0, 0))] * 2,
        [shape] * 2,
        2 * rows * width * shards * cols,
        rows * width * 4 + width * shards * cols * 2,
    deps=deps,
        )(spot, normed, y, *([] if gains is None else [gains]))


def out_blocks_grad(spot, heads_out, grads, shards):
    rows, width = grads.shape
    cols, depth = width // PLANE // 2, heads_out.shape[1] // shards

    def body(spot, x_ref, y_ref, *o_refs):
        for n, core in ((0, spot[1]), (1, 1 - spot[1])):
            total = tn(x_ref[...], of_core(y_ref, core, cols)).astype(bf16)
            for s in range(shards):
                o_refs[n][0, s] = folded(total[s * depth : (s + 1) * depth])

    shape = jax.ShapeDtypeStruct((PLANE, shards, depth // 2, 2 * cols), bf16)
    return grid_call(
        body,
        (PLANE,),
        [
            pl.BlockSpec((rows, heads_out.shape[1]), lambda q, _: (0, 0)),
            pl.BlockSpec((rows, 2 * cols), lambda q, _: (0, q)),
        ],
        [pl.BlockSpec((1, shards, depth // 2, 2 * cols), lambda q, _: (q, 0, 0, 0))] * 2,
        [shape] * 2,
        2 * rows * width * heads_out.shape[1],
        rows * width * 4 + width * heads_out.shape[1] * 2,
    )(spot, heads_out, grads)


def finish_pairs(spot, own, cos, sin, deps=()):
    _, rows, width = own.shape

    def body(spot, a_ref, cos_ref, sin_ref, o_ref):
        k = a_ref[0].astype(f32)
        o_ref[0] = (k * cos_ref[...] - swap_halves(k) * sin_ref[...]).astype(bf16)
        o_ref[1] = a_ref[1]

    tile = pl.BlockSpec((2, rows, LANES), lambda s, _: (0, 0, s))
    table = pl.BlockSpec((rows, LANES), lambda s, _: (0, 0))
    return grid_call(
        body,
        (width // LANES,),
        [tile, table, table],
        tile,
        jax.ShapeDtypeStruct(own.shape, bf16),
        own.size * 6,
        own.size * 4,
        deps=deps,
    )(spot, own, cos, sin)


def lanes_of(x_refs, core, depth):
    return jnp.concatenate(
        [
            jnp.concatenate([lanes_at(x, 2 * q + core, depth) for q in range(PLANE)], 1)
            for x in x_refs
        ],
        0,
    )


def gate_up(spot, xs, own, other, deps=()):
    span, width = xs[0].shape
    rows = span * len(xs)
    shards, half, cols = own[0].shape
    depth = half // PLANE
    count = len(xs)

    def body(spot, *refs):
        x_refs, (og_ref, ou_ref, tg_ref, tu_ref, go_ref, uo_ref, i_ref) = refs[:count], refs[count:]
        core = spot[1]
        for at in range(0, count, PLANE):
            part = x_refs[at : at + PLANE]
            left, right = lanes_of(part, core, depth), lanes_of(part, 1 - core, depth)
            gate = nn(left, og_ref[0]) + nn(right, tg_ref[0])
            up = nn(left, ou_ref[0]) + nn(right, tu_ref[0])
            here = slice(at * span, (at + PLANE) * span)
            go_ref[here, :] = gate.astype(bf16)
            uo_ref[here, :] = up.astype(bf16)
            i_ref[here, :] = (gate / (1.0 + jnp.exp(-gate)) * up).astype(bf16)

    weight = pl.BlockSpec((1, half, cols), lambda s, _: (s, 0, 0))
    tile = pl.BlockSpec((rows, cols), lambda s, _: (0, s))
    shape = jax.ShapeDtypeStruct((rows, shards * cols), bf16)
    return grid_call(
        body,
        (shards,),
        [still((span, width), lambda s, _: (0, 0))] * count + [weight] * 4,
        [tile] * 3,
        [shape] * 3,
        4 * rows * width * shards * cols,
        own[0].size * 8 + rows * width * 10,
        deps=deps,
    )(spot, *xs, *own, *other)


def split_rows(total, o_refs, at, depth):
    span = total.shape[0] // len(o_refs)
    for r, o_ref in enumerate(o_refs):
        o_ref[:, pl.ds(pl.multiple_of(at * depth, depth), depth)] = total[r * span : (r + 1) * span].astype(bf16)


def down(spot, inner, own, other, seqs, deps=()):
    rows, width = inner.shape
    shards, _, deep, cols = own.shape
    depth = cols // 2
    tall = rows // seqs
    span = tall // PLANE

    def body(spot, x_ref, own_ref, other_ref, *o_refs):
        core = spot[1]
        for w_ref, at in ((own_ref, core), (other_ref, 1 - core)):
            w = jnp.concatenate([unfolded(w_ref[s, 0]) for s in range(shards)], 0)
            lanes = pl.ds(pl.multiple_of(at * depth, depth), depth)
            for b in range(seqs):
                total = nn(x_ref[b * tall : (b + 1) * tall, :], w).astype(bf16)
                for r, o_ref in enumerate(o_refs):
                    o_ref[b * span : (b + 1) * span, lanes] = total[r * span : (r + 1) * span]

    weight = pl.BlockSpec((shards, 1, deep, cols), lambda q, _: (0, q, 0, 0))
    return grid_call(
        body,
        (PLANE,),
        [still((rows, width), lambda q, _: (0, 0)), weight, weight],
        [pl.BlockSpec((seqs * span, 2 * depth), lambda q, _: (0, q))] * PLANE,
        [jax.ShapeDtypeStruct((seqs * span, 2 * PLANE * depth), bf16)] * PLANE,
        4 * rows * width * PLANE * depth,
        own.size * 4 + rows * width * 4,
        deps=deps,
    )(spot, inner, own, other)


def backward_chunk(spot, chunk, span, gs, own_down, other_down, gate, up, own, other, deps=()):
    width = gs[0].shape[1]
    rows = span * len(gs)
    shards, _, deep, cols = own_down.shape
    depth, cols = cols // 2, 2 * deep
    count = len(gs)
    half = own[0].shape[1]

    def body(spot, *refs):
        x_refs, refs = refs[:count], refs[count:]
        own_ref, other_ref, g_ref, u_ref, og_ref, ou_ref, tg_ref, tu_ref, dg_ref, du_ref = refs[:10]
        o_refs, (gs_ref, us_ref) = refs[10:-2], refs[-2:]
        core, step = spot[1], pl.program_id(0)

        @pl.when(step < shards)
        def _():
            grad = None
            for w_ref, at in ((own_ref, core), (other_ref, 1 - core)):
                w = jnp.concatenate([unfolded(w_ref[0, q]) for q in range(PLANE)], 1)
                part = nt(lanes_of(x_refs, at, depth), w)
                grad = part if grad is None else grad + part
            gate, up = g_ref[...].astype(f32), u_ref[...].astype(f32)
            s = 1.0 / (1.0 + jnp.exp(-gate))
            dg = (grad * up * s * (1.0 + gate * (1.0 - s))).astype(bf16)
            du = (grad * gate * s).astype(bf16)
            dg_ref[...] = dg
            du_ref[...] = du
            gs_ref[step] = dg
            us_ref[step] = du

        @pl.when(step >= shards)
        def _():
            for gate_ref, up_ref, at in ((og_ref, ou_ref, core), (tg_ref, tu_ref, 1 - core)):
                total = None
                for d_ref, w_ref in ((gs_ref, gate_ref), (us_ref, up_ref)):
                    left = jnp.concatenate([d_ref[s] for s in range(shards)], 1)
                    part = nt(left, jnp.concatenate([w_ref[s] for s in range(shards)], 1))
                    total = part if total is None else total + part
                split_rows(total, o_refs, at, depth)

    def early(t):
        return jnp.minimum(t, shards - 1)

    def late(t):
        return jnp.maximum(t - shards, 0)

    tile = pl.BlockSpec((rows, cols), lambda t, _: (0, early(t)))
    given = pl.BlockSpec((rows, cols), lambda t, _: (chunk, early(t)))
    first = pl.BlockSpec((1, PLANE, deep, 2 * depth), lambda t, _: (early(t), 0, 0, 0))
    second = pl.BlockSpec((shards, depth, cols), lambda t, _: (0, late(t), 0))
    shape = jax.ShapeDtypeStruct((rows, shards * cols), bf16)
    outs = grid_call(
        body,
        (shards + PLANE,),
        [still((span, width), lambda t, _: (chunk, 0))] * count + [first] * 2 + [given] * 2 + [second] * 4,
        [tile] * 2 + [pl.BlockSpec((span, 2 * depth), lambda t, _: (0, late(t)))] * PLANE,
        [shape] * 2 + [jax.ShapeDtypeStruct((span, 2 * half), bf16)] * PLANE,
        6 * rows * width * shards * cols,
        own_down.size * 12 + rows * width * 16,
        [pltpu.VMEM((shards, rows, cols), bf16)] * 2,
        deps=deps,
    )(spot, *gs, own_down, other_down, gate, up, *own, *other)
    return outs[0], outs[1], outs[2:]


def norm_backward(grad_scaled, unrounded, norm_scale):
    return norm_scale * (grad_scaled - unrounded * jnp.mean(unrounded * grad_scaled, -1, keepdims=True))


def residual_grads(spot, parts, residual, cotangent, gain, deps=()):
    rows, width = residual.shape
    tall = 128
    count, each = len(parts), len(parts[0])
    per = rows // tall // count

    def body(spot, *refs):
        p_refs = refs[: count * each]
        r_ref, c_ref, g_ref, o_ref, low_ref, sum_ref = refs[count * each :]
        m = pl.program_id(0)

        @pl.when(m == 0)
        def _():
            sum_ref[...] = jnp.zeros_like(sum_ref)

        residual = r_ref[...]
        scale = lax.rsqrt(jnp.mean(residual * residual, -1, keepdims=True) + EPS)
        unrounded = residual * scale
        for b in range(count):

            @pl.when(m // per == b)
            def _(b=b):
                grad = total_of([ref[...] for ref in p_refs[b * each : (b + 1) * each]])
                terms = unrounded.astype(bf16).astype(f32) * grad
                sum_ref[0:1, :] += jnp.sum(terms, 0, keepdims=True)
                out = c_ref[...].astype(f32) + norm_backward(grad * g_ref[...], unrounded, scale)
                o_ref[...] = out
                low_ref[...] = out.astype(bf16)

    def place_of(b):
        return lambda m, _: (jnp.clip(m - b * per, 0, per - 1), 0)

    tile = pl.BlockSpec((tall, width), lambda m, _: (m, 0))
    fixed = lambda m, _: (0, 0)
    return grid_call(
        body,
        (rows // tall,),
        [pl.BlockSpec((tall, width), place_of(b)) for b in range(count) for _ in range(each)]
        + [tile, tile, pl.BlockSpec((1, width), fixed)],
        [tile, tile, pl.BlockSpec((8, width), fixed)],
        [
            jax.ShapeDtypeStruct((rows, width), f32),
            jax.ShapeDtypeStruct((rows, width), bf16),
            jax.ShapeDtypeStruct((8, width), f32),
        ],
        rows * width * 20,
        rows * width * 20,
        deps=deps,
    )(spot, *sum(parts, []), residual, cotangent, gain)


def turned(x_refs, xt_ref):
    at = 0
    for x_ref in x_refs:
        xt_ref[:, at : at + x_ref.shape[0]] = x_ref[...].T
        at += x_ref.shape[0]


def summed(xt_ref, ys):
    total, at = None, 0
    for y in ys:
        part = nn(xt_ref[:, at : at + y.shape[0]], y)
        total, at = (part if total is None else total + part), at + y.shape[0]
    return total


def column_weight_grads(spot, xs, ys, shards, deps=()):
    span, width = xs[0].shape
    rows = span * len(xs)
    cols = ys[0][0].shape[1] // shards
    depth = width // PLANE // 2
    count, lists, pieces = len(xs), len(ys), len(ys[0])
    pair = 2

    def body(spot, *refs):
        x_refs, y_refs, o_refs, xt_ref = refs[:count], refs[count : -1 - 2 * lists], refs[-1 - 2 * lists : -1], refs[-1]
        m, s = pl.program_id(1), pl.program_id(2)

        @pl.when((m == 0) & (s == 0))
        def _():
            turned(x_refs, xt_ref)

        for n in range(lists):

            @pl.when(m == n)
            def _(n=n):
                mine = y_refs[n * pieces : (n + 1) * pieces]
                total = summed(xt_ref, [r[...] for r in mine]).astype(bf16)
                first = spot[1] == 0
                for q in range(pair):
                    a = total[2 * q * depth : (2 * q + 1) * depth]
                    b = total[(2 * q + 1) * depth : (2 * q + 2) * depth]
                    o_refs[2 * n][0, q] = jnp.where(first, a, b)
                    o_refs[2 * n + 1][0, q] = jnp.where(first, b, a)

    def column(n, m, s):
        return jnp.where(m == n, s, jnp.where(m < n, 0, shards - 1))

    shape = jax.ShapeDtypeStruct((shards, PLANE, depth, cols), bf16)
    y_specs, o_specs = [], []
    for n in range(lists):
        y_specs += [
            pl.BlockSpec((y.shape[0], cols), lambda q, m, s, _, n=n: (0, column(n, m, s))) for y in ys[n]
        ]
        o_specs += [
            pl.BlockSpec((1, pair, depth, cols), lambda q, m, s, _, n=n: (column(n, m, s), q, 0, 0))
        ] * 2
    outs = grid_call(
        body,
        (PLANE // pair, lists, shards),
        [pl.BlockSpec((span, 2 * pair * depth), lambda q, m, s, _: (0, q))] * count + y_specs,
        o_specs,
        [shape] * (2 * lists),
        2 * lists * rows * width * shards * cols,
        lists * rows * width * 6 + lists * width * shards * cols * 2,
        [pltpu.VMEM((2 * pair * depth, rows), bf16)],
        deps=deps,
    )(spot, *xs, *sum(ys, []))
    return [outs[2 * n : 2 * n + 2] for n in range(lists)]


def row_weight_grad(spot, xs, ys, span, shards, deps=()):
    width = ys[0].shape[1]
    rows = sum(y.shape[0] for y in ys)
    seqs = ys[0].shape[0] // span
    tall = xs[0].shape[1] // shards
    depth = width // PLANE // 2
    count = len(xs)
    pair = 2 if shards % 2 == 0 else 1

    def body(spot, *refs):
        x_refs, y_refs, o_refs, xt_ref = refs[:count], refs[count:-3], refs[-3:-1], refs[-1]

        @pl.when(pl.program_id(1) == 0)
        def _():
            turned(x_refs, xt_ref)

        y = jnp.concatenate([r[...] for r in y_refs], 0)
        total = nn(xt_ref[...], y).astype(bf16)
        first = spot[1] == 0
        for s in range(pair):
            part = total[s * tall : (s + 1) * tall]
            a, b = folded(part[:, :depth]), folded(part[:, depth:])
            o_refs[0][s, 0] = jnp.where(first, a, b)
            o_refs[1][s, 0] = jnp.where(first, b, a)

    shape = jax.ShapeDtypeStruct((shards, PLANE, tall // 2, 2 * depth), bf16)
    return grid_call(
        body,
        (shards // pair, PLANE),
        [pl.BlockSpec((x.shape[0], pair * tall), lambda s, q, _: (0, s)) for x in xs]
        + [pl.BlockSpec((span, 2 * depth), lambda s, q, _, b=b: (b, q)) for b in range(seqs) for _ in ys],
        [pl.BlockSpec((pair, 1, tall // 2, 2 * depth), lambda s, q, _: (s, q, 0, 0))] * 2,
        [shape] * 2,
        2 * rows * width * shards * tall,
        rows * width * 6 + width * shards * tall * 2,
        [pltpu.VMEM((pair * tall, rows), bf16)],
    deps=deps,
        )(spot, *xs, *(list(ys) * seqs))


def finish_mixed(spot, residual, blocks, deps=()):
    rows, width = residual.shape
    tall = min(128, rows)

    def body(spot, r_ref, *refs):
        total = r_ref[...]
        for ref in refs[:-1]:
            total += ref[...].astype(f32)
        refs[-1][...] = total.astype(bf16)

    tile = pl.BlockSpec((tall, width), lambda m, _: (m, 0))
    return grid_call(
        body,
        (rows // tall,),
        [tile] * (1 + len(blocks)),
        tile,
        jax.ShapeDtypeStruct((rows, width), bf16),
        rows * width * 5,
        rows * width * 14,
        deps=deps,
    )(spot, residual, *blocks)


def hop(a, bits):
    n = lax.axis_size("dp")
    return lax.ppermute(a, "dp", [(i, i ^ bits) for i in range(n)])


def added(a, b):
    return (a.astype(f32) + b.astype(f32)).astype(a.dtype)


def plane_gather(a):
    return [a] + [hop(a, 2 * r) for r in range(1, PLANE)]


def plane_trade(blocks):
    return [blocks[0]] + [hop(blocks[r], 2 * r) for r in range(1, PLANE)]


def total_of(blocks):
    total = blocks[0].astype(f32)
    for b in blocks[1:]:
        total += b.astype(f32)
    return total


def plane_scatter(blocks):
    return total_of(plane_trade(blocks))


def shift(a, step):
    n = lax.axis_size("tensor")
    return lax.ppermute(a, "tensor", [(i, (i + step) % n) for i in range(n)])


def line_gather(a):
    return [a] + [shift(a, s) for s in range(1, lax.axis_size("tensor"))]


def line_scatter(blocks):
    n, place = lax.axis_size("tensor"), lax.axis_index("tensor")
    total = lax.dynamic_index_in_dim(blocks, place, 0, keepdims=False).astype(f32)
    for step in range(1, n):
        mine = lax.dynamic_index_in_dim(blocks, lax.rem(place + step, n), 0, keepdims=False)
        total += shift(mine, step).astype(f32)
    return total


def after(a, *others):
    others = jax.tree.leaves(others)
    place = pl.BlockSpec(memory_space=pl.ANY)
    return pl.pallas_call(
        lambda *refs: None,
        in_specs=[place] * (1 + len(others)),
        out_specs=place,
        out_shape=jax.ShapeDtypeStruct(a.shape, a.dtype),
        input_output_aliases={0: 0},
        cost_estimate=pl.CostEstimate(flops=1, bytes_accessed=1, transcendentals=0),
    )(a, *others)


def token(*arrays, steps=2):
    arrays = jax.tree.leaves(arrays)
    place = pl.BlockSpec(memory_space=pl.ANY)

    def body(*refs):
        refs[-1][...] = jnp.zeros_like(refs[-1])

    for _ in range(steps):
        arrays = [
            pl.pallas_call(
                body,
                in_specs=[place] * len(arrays),
                out_specs=pl.BlockSpec(memory_space=pltpu.VMEM),
                out_shape=jax.ShapeDtypeStruct((8, LANES), f32),
            )(*arrays)
        ]
    return arrays[0]


def by_chip(parts, chip):
    a, b, c, d = parts
    odd = (chip & 1) == 1
    a, b, c, d = (
        jnp.where(odd, b, a),
        jnp.where(odd, a, b),
        jnp.where(odd, d, c),
        jnp.where(odd, c, d),
    )
    high = (chip & 2) == 2
    return (
        jnp.where(high, c, a),
        jnp.where(high, d, b),
        jnp.where(high, a, c),
        jnp.where(high, b, d),
    )


def trade(pieces, axis, chip, hold=lambda a: a):
    come = []
    for r in range(PLANE):
        piece = lax.dynamic_index_in_dim(pieces, chip ^ r, axis, keepdims=False)
        come.append(hold(piece) if r == 0 else hop(piece, 2 * r))
    return by_chip(come, chip)


def core_sum(pair, *others):
    return added(after(pair[0], others) if others else pair[0], hop(pair[1], 1))


def plane_sum(blocks, chip):
    mine = [lax.dynamic_index_in_dim(blocks, chip ^ r, 0, keepdims=False) for r in range(PLANE)]
    return plane_scatter(mine).astype(bf16)


def rotary_tables(positions):
    half_size = HD // 2
    frequency = THETA ** (-2.0 * jnp.arange(half_size, dtype=f32) / HD)
    angles = positions.astype(f32)[:, None] * frequency[None, :]
    cos, sin = jnp.cos(angles), jnp.sin(angles)
    return (
        jnp.concatenate([cos, cos] * (LANES // HD), -1),
        jnp.concatenate([-sin, sin] * (LANES // HD), -1),
    )


def shards(
    tokens, segments, attn_norm, w_query, w_key, w_value, w_out, mlp_norm, w_gate, w_up, w_down, cotangent
):
    dp_count, tp_count = lax.axis_size("dp"), lax.axis_size("tensor")
    groups = dp_count // 8
    place = lax.axis_index("tensor")
    index = lax.axis_index("dp")
    core, chip = index & 1, (index >> 1) & 3
    seqs, span, width = tokens.shape
    rows = seqs * span
    block = width // 8

    group_sets = [[g * 8 + l for g in range(groups)] for l in range(8)]

    def widen(a, axis):
        if groups == 1:
            return a
        return lax.all_gather(a, "dp", axis=axis, tiled=True, axis_index_groups=group_sets)

    def narrow(a, axis):
        if groups == 1:
            return a
        return lax.psum_scatter(
            a.astype(bf16), "dp", scatter_dimension=axis, tiled=True, axis_index_groups=group_sets
        )

    def inward(a):
        if groups == 1:
            return a
        lead = a.shape[:-1]
        return jnp.swapaxes(a.reshape(lead + (groups, 8, -1)), -3, -2).reshape(lead + (-1,))

    def outward(a):
        if groups == 1:
            return a
        lead = a.shape[:-1]
        return jnp.swapaxes(a.reshape(lead + (8, groups, -1)), -3, -2).reshape(lead + (-1,))

    eight = [[g * 8 + l for l in range(8)] for g in range(groups)]

    def along(a):
        return lax.all_gather(a, "tensor", axis=0, tiled=False)

    def in_plane(a):
        if groups == 1:
            return lax.all_gather(a, "dp", axis=0, tiled=False)
        return lax.all_gather(a, "dp", axis=0, tiled=False, axis_index_groups=eight)

    tokens = inward(tokens).reshape(rows, width)
    cotangent = inward(cotangent).reshape(rows, width)
    attn_norm, mlp_norm = widen(attn_norm, 0), widen(mlp_norm, 0)
    w_query, w_key, w_value = widen(w_query, 0), widen(w_key, 0), widen(w_value, 0)
    w_gate, w_up = widen(w_gate, 0), widen(w_up, 0)
    w_out, w_down = widen(w_out, 1), widen(w_down, 1)

    kv_cols = 2 * w_key.shape[1]
    kv_group = w_query.shape[1] // w_key.shape[1]
    gains = jnp.concatenate(
        [
            jnp.pad(attn_norm, (0, kv_cols - block))[None],
            jnp.pad(mlp_norm, (0, kv_cols - block))[None],
            jnp.zeros((14, kv_cols), bf16),
        ],
        0,
    )
    near_kv = line_gather(jnp.concatenate([jnp.concatenate([w_key, w_value], 1), gains], 0))
    lines = w_down.reshape(PLANE, 2, -1, block)
    pieces = jnp.stack(
        [
            jnp.swapaxes(w_gate.reshape(block, PLANE, -1), 0, 1),
            jnp.swapaxes(w_up.reshape(block, PLANE, -1), 0, 1),
            jnp.concatenate([lines[:, 0], lines[:, 1]], 2),
        ],
        1,
    )
    all_kv = in_plane(jnp.stack(near_kv, 0))
    gain_one = all_kv[:, 0, block, :block].reshape(width).astype(f32)
    gain_two = all_kv[:, 0, block + 1, :block].reshape(width).astype(f32)
    lined = line_gather(after(jnp.stack([w_query, folded(w_out)], 0), near_kv[1:]))
    lined_q, lined_out = (jnp.stack([a[n] for a in lined], 0) for n in range(2))
    chunks = [slice(b * span, (b + 1) * span) for b in range(seqs)]

    spot = jnp.stack([place, core, chip]).astype(jnp.int32)
    cos, sin = rotary_tables(place * span + jnp.arange(span, dtype=jnp.int32))
    cos_rows, sin_rows = jnp.tile(cos, (seqs, 1)), jnp.tile(sin, (seqs, 1))
    x = tokens.astype(f32)
    norm_one = lax.rsqrt(jnp.mean(x * x, -1, keepdims=True) + EPS)
    scaled_one = (x * norm_one).astype(bf16)
    normed_one = (scaled_one.astype(f32) * gain_one).astype(bf16)
    pair = project_pairs(spot, normed_one, all_kv, cos_rows, sin_rows, block, deps=lined[1:])
    pairs = along(pair)
    def both_cores(blocks, *others):
        if others:
            blocks = [after(b, others) for b in blocks]
        return blocks + [hop(b, 1) for b in blocks]

    all_q = plane_gather(after(lined_q, pair))
    sent = after(pieces, all_q[1:])
    all_q = both_cores(all_q)
    queries = project_queries(spot, normed_one, all_q, cos_rows, sin_rows)
    near = jnp.stack(trade(sent, 0, chip, lambda own: after(own, queries)), 1)
    tall = near.shape[1] * near.shape[2]
    own_gate, own_up = (along(after(near[n].reshape(tall, -1), pair)) for n in range(2))
    all_out = plane_gather(after(lined_out, all_q[1:], near))

    seg_blocks = segments.reshape(seqs, tp_count, span)
    own_seg = lax.dynamic_index_in_dim(seg_blocks, place, 1, keepdims=False)
    here = jnp.arange(span, dtype=jnp.int32)
    bias = []
    for j in range(tp_count):
        key_seg = lax.dynamic_index_in_dim(seg_blocks, jnp.maximum(place - j, 0), 1, keepdims=False)
        allowed = key_seg[:, :, None] == own_seg[:, None, :]
        if j == 0:
            allowed &= here[None, :, None] <= here[None, None, :]
        bias.append(jnp.where(allowed, 0.0, -1e30).astype(f32))
    bias = jnp.concatenate(bias, 1)
    heads_out, lse = attend(spot, queries, pairs, bias, span, kv_group)
    all_out = both_cores(all_out, heads_out)
    residual = project_out(spot, heads_out, all_out, tokens)

    norm_two = lax.rsqrt(jnp.mean(residual * residual, -1, keepdims=True) + EPS)
    scaled_two = (residual * norm_two).astype(bf16)
    normed_two = (scaled_two.astype(f32) * gain_two).astype(bf16)
    full_two = []
    for c in chunks:
        full_two.append(plane_gather(after(normed_two[c], full_two[-1][1:]) if full_two else normed_two[c]))
    cot_full = plane_gather(after(cotangent, full_two[-1][1:]))
    own_gate, own_up = after(own_gate, full_two[0][1:]), after(own_up, full_two[-1][1:])
    own_in = (own_gate, own_up)
    other_in = (hop(own_gate, 1), hop(own_up, 1))
    own_down = along(after(near[2], residual))
    tokens_two = sum(full_two, [])
    gate, up, inner = gate_up(spot, tokens_two, own_in, other_in)
    other_down = hop(own_down, 1)

    def line_sum(a):
        return lax.psum_scatter(a, "tensor", scatter_dimension=0, tiled=False)

    down_parts = row_weight_grad(spot, [inner], cot_full, span, tp_count)
    d_gate, d_up, from_plane, deps = [], [], [], down_parts
    for n in range(seqs):
        weights = (own_down, other_down, gate, up, own_in, other_in)
        dg, du, to_plane = backward_chunk(spot, n, span, cot_full, *weights, deps=deps)
        d_gate.append(dg)
        d_up.append(du)
        deps = to_plane
        from_plane.append(plane_trade(list(to_plane)))
    down_pair = core_sum(down_parts, d_gate[0])
    down_sum = line_sum(down_pair)
    deps = [down_pair, to_plane, [f[1:] for f in from_plane[:-1]]]
    gate_parts, up_parts = column_weight_grads(spot, tokens_two, [d_gate, d_up], tp_count, deps=deps)
    grad_residual, grad_low, gain_two_terms = residual_grads(
        spot, from_plane, residual, cotangent, gain_two[None], deps=[up_parts[0], down_sum]
    )
    gain_two_terms = gain_two_terms[0]
    gate_parts, up_parts = ((p[0], after(p[1], grad_low)) for p in (gate_parts, up_parts))
    shares = down(spot, inner, own_down, other_down, seqs, deps=grad_low)
    gate_pair, up_pair = core_sum(gate_parts, shares[0]), core_sum(up_parts, shares[0])
    gate_sum = line_sum(gate_pair)
    mixed = plane_trade(list(shares))

    out_parts = out_blocks_grad(spot, heads_out, grad_low, tp_count)
    grad_heads = unproject_out(spot, grad_low, all_out, deps=[up_parts[0], out_parts])
    deps = [out_parts, up_pair, gate_pair]
    dq, dkv = unattend(spot, queries, grad_heads, pairs, bias, lse, cos, sin, span, kv_group, deps=deps)
    gate_here = token(dq, mixed[1:], gate_sum, steps=1)
    dkv = line_sum(after(dkv, gate_here))
    up_sum = line_sum(up_pair)
    partial = unproject_queries(spot, dq, all_q, deps=gate_here)
    out_near = plane_sum(core_sum((out_parts[0], after(out_parts[1], gate_here))), chip)
    query_parts = in_blocks_grad(spot, normed_one, dq, None, None, tp_count, deps=partial)
    grad_out = unfolded(line_scatter(out_near))
    query_near = plane_sum(core_sum(query_parts), chip)
    grad_query = line_scatter(query_near)
    mixed = finish_mixed(spot, residual, mixed, deps=query_parts)
    dkv = finish_pairs(spot, dkv, cos_rows, sin_rows, deps=[out_near, query_near])
    grad_normed_one, gain_one_terms = unproject_pairs(spot, partial, dkv, all_kv, scaled_one)
    gain_one_terms = gain_one_terms[0]
    gain_terms = jnp.stack([gain_one_terms.reshape(8, block), gain_two_terms.reshape(8, block)], 1)
    gain_terms = jnp.pad(gain_terms, ((0, 0), (0, 14), (0, kv_cols - block)))
    kv_parts = in_blocks_grad(spot, normed_one, dq, dkv, gain_terms, tp_count)
    held = lambda a: after(a, kv_parts)
    come = trade(after(jnp.stack([down_sum, gate_sum, up_sum], 1), out_near, query_near), 0, chip, held)
    grad_down = jnp.concatenate([jnp.concatenate([c[0, :, :block], c[0, :, block:]], 0) for c in come], 0)
    grad_gate, grad_up = (jnp.concatenate([c[n] for c in come], 1) for n in (1, 2))

    kv_sum = line_scatter(plane_sum(core_sum(kv_parts), chip))
    grad_tokens = grad_residual + norm_backward(grad_normed_one * gain_one, x * norm_one, norm_one)
    grad_tokens = grad_tokens.astype(bf16)
    def gain_share(line):
        line = narrow(line, 0)
        share = line.shape[0] // tp_count
        return lax.dynamic_slice_in_dim(line, place * share, share, 0).astype(f32)

    half = kv_cols // 2
    return (
        outward(mixed).reshape(seqs, span, width),
        outward(grad_tokens).reshape(seqs, span, width),
        gain_share(kv_sum[block, :block]),
        narrow(grad_query, 0).astype(f32),
        narrow(kv_sum[:block, :half], 0).astype(f32),
        narrow(kv_sum[:block, half:], 0).astype(f32),
        narrow(grad_out, 1).astype(f32),
        gain_share(kv_sum[block + 1, :block]),
        narrow(grad_gate, 0).astype(f32),
        narrow(grad_up, 0).astype(f32),
        narrow(grad_down, 1).astype(f32),
    )


def solution(mesh):
    placed = (
        P("dp", "tensor", None),
        P("dp", None),
        P("dp"),
        P("dp", "tensor"),
        P("dp", "tensor"),
        P("dp", "tensor"),
        P("tensor", "dp"),
        P("dp"),
        P("dp", "tensor"),
        P("dp", "tensor"),
        P("tensor", "dp"),
        P("dp", "tensor", None),
    )
    return jax.shard_map(
        shards,
        mesh=mesh,
        in_specs=placed,
        out_specs=(
            P("dp", "tensor", None),
            P("dp", "tensor", None),
            P(("dp", "tensor")),
            P("dp", "tensor"),
            P("dp", "tensor"),
            P("dp", "tensor"),
            P("tensor", "dp"),
            P(("dp", "tensor")),
            P("dp", "tensor"),
            P("dp", "tensor"),
            P("tensor", "dp"),
        ),
        check_vma=False,
    )
```
